256 devices in a mesh: blk: 32 (over x, z), tile: 8 (over y, core).
Axes of the slice: x: 4, y: 4, z: 8, core: 2. Of those that a mesh axis runs over, the one named last changes fastest.
Arguments:
- stream_in: bfloat16 [32, 64, 16, 2240], P('tile', 'blk'), may hold values from -6 to 6
- queries: bfloat16 [32, 64, 16, 2240], P('tile', 'blk'), may hold values from -12 to 12
- key_rows: bfloat16 [32, 64, 16, 2240], P('tile', 'blk'), may hold values from -12 to 12
- value_rows: bfloat16 [32, 64, 16, 2240], P('tile', 'blk'), may hold values from -12 to 12
- w_output: bfloat16 [2240, 2240], P('tile'), may hold values from -0.125 to 0.125
- w_inner: bfloat16 [2240, 2, 4096], P(None, None, 'tile'), may hold values from -0.125 to 0.125
- w_down: bfloat16 [4096, 2240], P('tile'), may hold values from -0.09375 to 0.09375
- spatial_taps: float32 [3, 3, 2, 4096], P(None, None, None, 'tile'), may hold values from -2 to 2
- temporal_taps: float32 [3, 2, 4096], P(None, None, 'tile'), may hold values from -3.5 to 3.5
Outputs:
- layer_out: bfloat16 [32, 64, 16, 2240], P('tile', 'blk')
The draws below stay inside these ranges and needn't reach their ends.
All inputs are finite; a program needn't handle non-finite values.
Results may differ from the reference program's by a relative error of at most 0.009.
Values may be sent and summed in bfloat16 or wider, within the bound.
No kernel may reach another device: no remote copies, remote signals or barrier semaphores. Data moves between devices by JAX's collectives and lax.ppermute only.
A program may use at most 128 MiB of HBM per device.

```python
import jax
import jax.numpy as jnp
from jax import lax

HEADS = 20
HEAD_DIM = 112
D = 2240
FF_WIN = 4096
ROWS = 32
COLS = 16
BLOCK_F = 4
TAPS = 3
FRAMES = 64


def cluster_tables(key):
    mask_key = jax.random.fold_in(key, 101)
    magnitude_key = jax.random.fold_in(key, 102)
    value_key = jax.random.fold_in(key, 103)
    active = jax.random.bernoulli(mask_key, 0.12, (HEADS, HEAD_DIM, HEAD_DIM))
    own_channel = jnp.eye(HEAD_DIM, dtype=jnp.float32)[None] > 0.5
    active = jnp.logical_or(active, own_channel)
    magnitude = jnp.exp(jax.random.uniform(magnitude_key, (HEADS, HEAD_DIM, HEAD_DIM), jnp.float32, 0.405, 1.386))
    proto_key = jnp.where(active, magnitude, 0.0)
    proto_value = 2.0 * jax.random.normal(value_key, (HEADS, HEAD_DIM, HEAD_DIM), jnp.float32)
    return (proto_key, proto_value)


def token_noise(noise_key):
    shape_heads = (ROWS, FRAMES, COLS, HEADS, HEAD_DIM)
    return jax.random.normal(noise_key, shape_heads, jnp.float32)


def pick_rows(table, clusters):
    head_index = jnp.arange(HEADS, dtype=jnp.int32)
    return table[head_index, clusters]


def positive_rows(key, salt):
    proto_key, proto_value = cluster_tables(key)
    clusters = jax.random.randint(jax.random.fold_in(key, salt), (ROWS, FRAMES, COLS, HEADS), 0, HEAD_DIM)
    gain = jnp.exp(jax.random.uniform(jax.random.fold_in(key, salt + 1), (ROWS, FRAMES, COLS, HEADS, 1), jnp.float32, -1.5, 1.5))
    noise = token_noise(jax.random.fold_in(key, salt + 2))
    rows = gain * (pick_rows(proto_key, clusters) + 0.3 * noise)
    return (rows, clusters, proto_value)


def draw_queries(key, part):
    rows, clusters, proto_value = positive_rows(key, 211)
    return jnp.clip(rows, -12.0, 12.0).reshape(ROWS, FRAMES, COLS, D).astype(jnp.bfloat16)


def draw_key_rows(key, part):
    rows, clusters, proto_value = positive_rows(key, 311)
    return jnp.clip(rows, -12.0, 12.0).reshape(ROWS, FRAMES, COLS, D).astype(jnp.bfloat16)


def draw_value_rows(key, part):
    rows, clusters, proto_value = positive_rows(key, 311)
    noise = token_noise(jax.random.fold_in(key, 411))
    offset = 2.0 * jax.random.normal(jax.random.fold_in(key, 412), (1, FRAMES, 1, HEADS, HEAD_DIM), jnp.float32)
    values = noise + pick_rows(proto_value, clusters) + offset
    return jnp.clip(values, -12.0, 12.0).reshape(ROWS, FRAMES, COLS, D).astype(jnp.bfloat16)


def level_of(rng, dims, shards, low, largest):
    def one(position, parts):
        steps = jax.random.uniform(jax.random.fold_in(jax.random.fold_in(rng, 6), position), (parts,), jnp.float32, low / len(shards), largest / len(shards))
        return jnp.repeat(jnp.exp(steps), dims[position] // parts).reshape((-1,) + (1,) * (len(dims) - position - 1))

    factor_of = one(*shards[0])
    for cut in shards[1:]:
        factor_of = factor_of * one(*cut)
    return factor_of


def gaussian(rng, shape, width, bound, cuts=(), held_as=jnp.bfloat16):
    values = jax.random.normal(rng, shape, jnp.float32) * width
    if len(cuts) > 0:
        values = level_of(rng, shape, cuts, -0.22, 0.18) * values
    return jnp.clip(values, min=-bound, max=bound).astype(held_as)


def setup_inputs(seed: int = 0) -> dict:
    key_of = jax.random.split(jax.random.key(seed), 10)
    return {
        "stream_in": gaussian(key_of[0], (ROWS, FRAMES, COLS, D), 1.0, 6.0, ((0, 8), (1, 32))),
        "queries": draw_queries(jax.random.fold_in(key_of[9], 71), 0),
        "key_rows": draw_key_rows(jax.random.fold_in(key_of[9], 71), 0),
        "value_rows": draw_value_rows(jax.random.fold_in(key_of[9], 71), 0),
        "w_output": gaussian(key_of[4], (D, D), D ** -0.5, 0.125, ((0, 8),)),
        "w_inner": gaussian(key_of[5], (D, 2, FF_WIN), D ** -0.5, 0.125, ((2, 8),)),
        "w_down": gaussian(key_of[6], (FF_WIN, D), FF_WIN ** -0.5, 0.09375, ((0, 8),)),
        "spatial_taps": gaussian(key_of[7], (3, 3, 2, FF_WIN), 9 ** -0.5, 2.0, ((3, 8),), jnp.float32),
        "temporal_taps": gaussian(key_of[8], (TAPS, 2, FF_WIN), TAPS ** -0.5, 3.5, ((2, 8),), jnp.float32),
    }


EPS = 1e-6


def spatial_conv(inner_act, spatial_taps):
    row_count = inner_act.shape[0]
    col_count = inner_act.shape[2]
    padded = jnp.pad(inner_act, ((1, 1), (0, 0), (1, 1), (0, 0), (0, 0)))
    running = jnp.zeros(inner_act.shape, jnp.float32)
    for tap_row in range(3):
        for tap_col in range(3):
            window = padded[tap_row:tap_row + row_count, :, tap_col:tap_col + col_count]
            running = running + window.astype(jnp.float32) * spatial_taps[tap_row, tap_col]
    return running


def reference(stream_in, queries, key_rows, value_rows, w_output, w_inner, w_down, spatial_taps, temporal_taps):
    highest = lax.Precision.HIGHEST
    shape_heads = (ROWS, FRAMES, COLS, HEADS, HEAD_DIM)
    query_pos = jax.nn.relu(queries.astype(jnp.float32)).reshape(shape_heads)
    key_pos = jax.nn.relu(key_rows.astype(jnp.float32)).reshape(shape_heads)
    values = value_rows.astype(jnp.float32).reshape(shape_heads)
    frame_kv = jnp.einsum('rfchd,rfche->fhde', key_pos, values, precision=highest)
    frame_z = jnp.sum(key_pos, axis=(0, 2))
    block_count = FRAMES // BLOCK_F
    block_kv = frame_kv.reshape(block_count, BLOCK_F, HEADS, HEAD_DIM, HEAD_DIM).sum(1)
    block_z = frame_z.reshape(block_count, BLOCK_F, HEADS, HEAD_DIM).sum(1)
    state = jnp.repeat(jnp.cumsum(block_kv, 0), BLOCK_F, axis=0)
    zsum = jnp.repeat(jnp.cumsum(block_z, 0), BLOCK_F, axis=0)
    numerator = jnp.einsum('rfchd,fhde->rfche', query_pos, state, precision=highest)
    denominator = jnp.einsum('rfchd,fhd->rfch', query_pos, zsum, precision=highest) + EPS
    attended = (numerator / denominator[..., None]).reshape(ROWS * FRAMES * COLS, D).astype(jnp.bfloat16)
    attn_out = jnp.dot(attended, w_output, preferred_element_type=jnp.float32)
    hidden = (stream_in.astype(jnp.float32).reshape(-1, D) + attn_out).astype(jnp.bfloat16)
    inner_act = jax.nn.silu(jnp.dot(hidden, w_inner.reshape(D, 2 * FF_WIN), preferred_element_type=jnp.float32))
    inner_act = inner_act.astype(jnp.bfloat16).reshape(ROWS, FRAMES, COLS, 2, FF_WIN)
    spatial = spatial_conv(inner_act, spatial_taps).astype(jnp.bfloat16)
    extended = jnp.pad(spatial, ((0, 0), (TAPS - 1, 0), (0, 0), (0, 0), (0, 0)))
    temporal_mix = jnp.zeros(spatial.shape, jnp.float32)
    for lag in range(TAPS):
        window = extended[:, TAPS - 1 - lag:TAPS - 1 - lag + FRAMES]
        temporal_mix = temporal_mix + window.astype(jnp.float32) * temporal_taps[lag]
    gated_out = (temporal_mix[..., 0, :] * jax.nn.silu(temporal_mix[..., 1, :])).astype(jnp.bfloat16)
    ffn_out = jnp.dot(gated_out.reshape(-1, FF_WIN), w_down, preferred_element_type=jnp.float32)
    layer_out = (hidden.astype(jnp.float32) + ffn_out).astype(jnp.bfloat16)
    return layer_out.reshape(ROWS, FRAMES, COLS, D)
```

```python
import functools

import jax
import jax.numpy as jnp
from jax import lax
from jax.experimental import pallas as pl
from jax.experimental.pallas import tpu as pltpu
from jax.sharding import PartitionSpec as P

HEADS = 20
HEAD_DIM = 112
D = 2240
TAPS = 3
EPS = 1e-6
LANES = 128
SLABS = 18
SUB = 14
PIECES = 256
BF = jnp.bfloat16
F32 = jnp.float32
MIB = 1 << 20


def slab_of(c):
    first = (LANES * c) // HEAD_DIM
    bound = HEAD_DIM * (first + 1) - LANES * c
    start = (HEAD_DIM * first) // LANES * LANES
    pair = 2 if first + 1 < HEADS else 1
    stop = min(-(-(HEAD_DIM * (first + pair)) // LANES) * LANES, D)
    return first, pair, bound, start, stop, HEAD_DIM * first - start


def kv_kernel(k_ref, v_ref, out_ref, last_ref):
    tokens = k_ref.shape[0]
    key_pos = jnp.maximum(k_ref[...], 0)
    last_ref[...] = jnp.ones((tokens, LANES), BF)
    last_ref[:, : D - LANES * (SLABS - 1)] = v_ref[:, LANES * (SLABS - 1) :]
    lane = lax.broadcasted_iota(jnp.int32, (HEAD_DIM, LANES), 1)
    over_tokens = (((0,), (0,)), ((), ()))
    for c in range(SLABS):
        first, pair, bound, start, stop, offset = slab_of(c)
        values = last_ref[...] if c == SLABS - 1 else v_ref[:, LANES * c : LANES * (c + 1)]
        product = lax.dot_general(
            key_pos[:, start:stop], values, over_tokens, preferred_element_type=F32
        )
        tile = product[offset : offset + HEAD_DIM]
        if pair == 2:
            tile = jnp.where(lane < bound, tile, product[offset + HEAD_DIM : offset + 2 * HEAD_DIM])
        if c == SLABS - 1:
            sums = lax.dot_general(
                key_pos, jnp.ones((tokens, LANES), BF), over_tokens, preferred_element_type=F32
            )
            tile = jnp.where(lane < bound, tile, 0.0)
            for h in range(HEADS):
                tile = jnp.where(
                    lane == bound + h, sums[HEAD_DIM * h : HEAD_DIM * (h + 1)], tile
                )
        out_ref[SUB * c : SUB * (c + 1)] = tile.reshape(SUB, 8, LANES).astype(BF)
    rest = PIECES - SUB * SLABS
    out_ref[SUB * SLABS :] = jnp.zeros((rest, 8, LANES), BF)


def prefix_kernel(in_ref, out_ref):
    per_block = 16

    def block(b, total):
        here = in_ref[pl.ds(b * per_block, per_block)].astype(F32)
        total = total + jnp.sum(here, axis=0)
        out_ref[pl.ds(b * per_block, per_block)] = jnp.broadcast_to(
            total.astype(BF)[None], (per_block, 8, LANES)
        )
        return total

    lax.fori_loop(0, PIECES // per_block, block, jnp.zeros((8, LANES), F32))


def hidden_kernel(q_ref, state_ref, stream_ref, w_hbm, hid0_ref, hid1_ref, w_ref, att_ref, sem):
    copy = pltpu.make_async_copy(w_hbm, w_ref, sem)
    copy.start()
    tokens = q_ref.shape[0]
    query_pos = jnp.maximum(q_ref[...], 0)
    lane = lax.broadcasted_iota(jnp.int32, (HEAD_DIM, LANES), 1)
    tile_of = lambda c: state_ref[SUB * c : SUB * (c + 1)].astype(F32).reshape(HEAD_DIM, LANES)
    sums = tile_of(SLABS - 1)
    z_lane = D - LANES * (SLABS - 1)
    for c in range(SLABS):
        first, pair, bound, start, stop, offset = slab_of(c)
        tile = tile_of(c)
        weights = []
        for which in range(2):
            rows = []
            if offset > 0:
                rows.append(jnp.zeros((offset, LANES), F32))
            for k in range(pair):
                if which == 0:
                    part = tile
                else:
                    h = z_lane + first + k
                    part = jnp.broadcast_to(sums[:, h : h + 1], (HEAD_DIM, LANES))
                inside = (lane < bound) if k == 0 else (lane >= bound)
                rows.append(jnp.where(inside, part, 0.0))
            left = stop - start - offset - pair * HEAD_DIM
            if left > 0:
                rows.append(jnp.zeros((left, LANES), F32))
            weights.append(jnp.concatenate(rows, axis=0))
        weight = jnp.concatenate(weights, axis=1).astype(BF)
        both = jnp.dot(query_pos[:, start:stop], weight, preferred_element_type=F32)
        attended = (both[:, :LANES] / (both[:, LANES:] + EPS)).astype(BF)
        width = min(LANES, D - LANES * c)
        att_ref[:, LANES * c : LANES * c + width] = attended[:, :width]
    copy.wait()
    step = 256
    for n in range(0, D, step):
        cols = slice(n, min(n + step, D))
        out = jnp.dot(att_ref[...], w_ref[:, cols], preferred_element_type=F32)
        out = (out + stream_ref[:, cols].astype(F32)).astype(BF)
        for r in range(tokens // 32):
            hid0_ref[16 * r : 16 * r + 16, cols] = out[32 * r : 32 * r + 16]
            hid1_ref[16 * r : 16 * r + 16, cols] = out[32 * r + 16 : 32 * r + 32]


def spatial_kernel(hid_ref, w_ref, taps_ref, out_ref, act_ref):
    tokens, cols = hid_ref.shape[0], 16
    width = w_ref.shape[1]
    product = jnp.dot(hid_ref[...], w_ref[...], preferred_element_type=F32)
    act = (product * jax.nn.sigmoid(product)).astype(BF).astype(F32)
    act_ref[:cols] = jnp.zeros((cols, width), F32)
    act_ref[cols + tokens :] = jnp.zeros((cols, width), F32)
    act_ref[cols : cols + tokens] = act
    taps = taps_ref[...]
    chunk = 32
    col = lax.broadcasted_iota(jnp.int32, (chunk, width), 0) % cols
    for r in range(0, tokens, chunk):
        rows = [act_ref[r + cols * a : r + cols * a + chunk] for a in range(3)]
        left, mid, right = (
            rows[0] * taps[b : b + 1] + rows[1] * taps[3 + b : 4 + b] + rows[2] * taps[6 + b : 7 + b]
            for b in range(3)
        )
        left = jnp.where(col == 0, 0.0, pltpu.roll(left, 1, 0))
        right = jnp.where(col == cols - 1, 0.0, pltpu.roll(right, chunk - 1, 0))
        out_ref[r : r + chunk] = (left + mid + right).astype(BF)


def point_kernel(place_ref, now_ref, one_ref, two_ref, taps_ref, w_ref, mine_ref, other_ref):
    half = w_ref.shape[0]
    taps = taps_ref[...]
    mix = now_ref[...].astype(F32) * taps[0:1]
    mix = mix + one_ref[...].astype(F32) * taps[1:2]
    mix = mix + two_ref[...].astype(F32) * taps[2:3]
    gate = mix[:, half:]
    gated = (mix[:, :half] * (gate * jax.nn.sigmoid(gate))).astype(BF)
    out = jnp.dot(gated, w_ref[...], preferred_element_type=F32).astype(BF)
    y, core = place_ref[0], place_ref[1]
    i = pl.program_id(0)
    rows = out.shape[0] // 4
    for k in range(4):
        target = 4 * i + k
        slot = (target // 2 - y + 4) % 4

        @pl.when(core == k % 2)
        def _():
            mine_ref[slot] = out[rows * k : rows * (k + 1)]

        @pl.when(core != k % 2)
        def _():
            other_ref[slot] = out[rows * k : rows * (k + 1)]


def params(mib):
    return pltpu.CompilerParams(vmem_limit_bytes=mib * MIB)


VMEM = pl.BlockSpec(memory_space=pltpu.VMEM)


def on_device(
    stream_in, queries, key_rows, value_rows, w_output, w_inner, w_down, spatial_taps, temporal_taps
):
    row_count, frames, col_count, width = queries.shape
    tokens = row_count * frames * col_count
    flat = lambda a: a.reshape(tokens, width)
    chan = w_inner.shape[2]
    peers = lax.axis_size("tile")
    place = lax.axis_index("tile")
    where_am_i = jnp.stack([place // 2, place % 2]).astype(jnp.int32)

    w_out_whole = lax.all_gather(w_output, "tile", axis=0, tiled=True)
    w_flat = w_inner.reshape(width, 2 * chan)
    taps_s = spatial_taps.reshape(9, 2 * chan)
    taps_t = temporal_taps.reshape(TAPS, 2 * chan)

    pieces = jax.ShapeDtypeStruct((PIECES, 8, LANES), BF)
    parts = pl.pallas_call(
        kv_kernel,
        out_shape=pieces,
        in_specs=[VMEM] * 2,
        out_specs=VMEM,
        scratch_shapes=[pltpu.VMEM((tokens, LANES), BF)],
        compiler_params=params(40),
    )(flat(key_rows), flat(value_rows))
    everyone = ("blk", "tile")
    parts = lax.all_to_all(parts, everyone, 0, 0, tiled=True)
    sums = pl.pallas_call(
        prefix_kernel, out_shape=pieces, in_specs=[VMEM], out_specs=VMEM, compiler_params=params(40)
    )(parts)
    state = lax.all_to_all(sums, everyone, 0, 0, tiled=True)

    frame_rows = row_count * col_count
    hidden = pl.pallas_call(
        hidden_kernel,
        out_shape=[jax.ShapeDtypeStruct((frame_rows, width), BF)] * 2,
        in_specs=[VMEM, VMEM, VMEM, pl.BlockSpec(memory_space=pl.ANY)],
        out_specs=[VMEM, VMEM],
        scratch_shapes=[
            pltpu.VMEM((width, width), BF),
            pltpu.VMEM((tokens, width), BF),
            pltpu.SemaphoreType.DMA,
        ],
        compiler_params=params(48),
    )(flat(queries), state, flat(stream_in), w_out_whole)

    whole_rows = peers * frame_rows
    block = 256
    spatial_call = pl.pallas_call(
        spatial_kernel,
        out_shape=jax.ShapeDtypeStruct((whole_rows, 2 * chan), BF),
        grid=(2 * chan // block,),
        in_specs=[
            pl.BlockSpec((whole_rows, width), lambda i: (0, 0)),
            pl.BlockSpec((width, block), lambda i: (0, i)),
            pl.BlockSpec((9, block), lambda i: (0, i)),
        ],
        out_specs=pl.BlockSpec((whole_rows, block), lambda i: (0, i)),
        scratch_shapes=[pltpu.VMEM((whole_rows + 2 * col_count, block), F32)],
        compiler_params=params(40),
    )
    row_block = 256
    point_call = pl.pallas_call(
        point_kernel,
        out_shape=[jax.ShapeDtypeStruct((4, frame_rows, width), BF)] * 2,
        grid=(whole_rows // row_block,),
        in_specs=[pl.BlockSpec(memory_space=pltpu.SMEM)]
        + [pl.BlockSpec((row_block, 2 * chan), lambda i: (i, 0))] * 3
        + [
            pl.BlockSpec((TAPS, 2 * chan), lambda i: (0, 0)),
            pl.BlockSpec((chan, width), lambda i: (0, 0)),
        ],
        out_specs=[pl.BlockSpec((4, frame_rows, width), lambda i: (0, 0, 0))] * 2,
        compiler_params=params(40),
    )

    blocks = lax.axis_size("blk")
    next_frames = [(i, i + 1) for i in range(blocks - 1)]
    other_core = [(i, i ^ 1) for i in range(peers)]
    spatial, halo = [None, None], [None, None]
    for f in (1, 0):
        whole = lax.all_gather(hidden[f], "tile", axis=0, tiled=True)
        spatial[f] = spatial_call(whole, w_flat, taps_s)
        halo[f] = lax.ppermute(spatial[f], "blk", next_frames)

    def reduced(f):
        now, one, two = (spatial[1], spatial[0], halo[1]) if f else (spatial[0], halo[1], halo[0])
        mine, other = point_call(where_am_i, now, one, two, taps_t, w_down)
        from_core = lax.ppermute(other, "tile", other_core)
        total = mine.astype(F32) + from_core.astype(F32)
        result = hidden[f].astype(F32) + total[0]
        for k in range(1, 4):
            pairs = [(i, (i + 2 * k) % peers) for i in range(peers)]
            result = result + lax.ppermute(total[k].astype(BF), "tile", pairs).astype(F32)
        return result.astype(BF).reshape(row_count, 1, col_count, width)

    late = reduced(1)
    early = reduced(0)
    return jnp.concatenate([early, late], axis=1)


def solution(mesh):
    in_specs = (
        P("tile", "blk", None, None),
        P("tile", "blk", None, None),
        P("tile", "blk", None, None),
        P("tile", "blk", None, None),
        P("tile", None),
        P(None, None, "tile"),
        P("tile", None),
        P(None, None, None, "tile"),
        P(None, None, "tile"),
    )
    out_specs = P("tile", "blk", None, None)
    return jax.shard_map(
        on_device, mesh=mesh, in_specs=in_specs, out_specs=out_specs, check_vma=False
    )
```

```python
import functools

import jax
import jax.numpy as jnp
from jax import lax
from jax.experimental import pallas as pl
from jax.experimental.pallas import tpu as pltpu
from jax.sharding import PartitionSpec as P

HEADS = 20
HEAD_DIM = 112
D = 2240
TAPS = 3
EPS = 1e-6
LANES = 128
SLABS = 18
SUB = 14
PIECES = 256
BF = jnp.bfloat16
F32 = jnp.float32
MIB = 1 << 20


def slab_of(c):
    first = (LANES * c) // HEAD_DIM
    bound = HEAD_DIM * (first + 1) - LANES * c
    start = (HEAD_DIM * first) // LANES * LANES
    pair = 2 if first + 1 < HEADS else 1
    stop = min(-(-(HEAD_DIM * (first + pair)) // LANES) * LANES, D)
    return first, pair, bound, start, stop, HEAD_DIM * first - start


def kv_kernel(k_ref, v_ref, out_ref, last_ref):
    tokens = k_ref.shape[0]
    key_pos = jnp.maximum(k_ref[...], 0)
    last_ref[...] = jnp.ones((tokens, LANES), BF)
    last_ref[:, : D - LANES * (SLABS - 1)] = v_ref[:, LANES * (SLABS - 1) :]
    lane = lax.broadcasted_iota(jnp.int32, (HEAD_DIM, LANES), 1)
    over_tokens = (((0,), (0,)), ((), ()))
    for c in range(SLABS):
        first, pair, bound, start, stop, offset = slab_of(c)
        values = last_ref[...] if c == SLABS - 1 else v_ref[:, LANES * c : LANES * (c + 1)]
        product = lax.dot_general(
            key_pos[:, start:stop], values, over_tokens, preferred_element_type=F32
        )
        tile = product[offset : offset + HEAD_DIM]
        if pair == 2:
            tile = jnp.where(lane < bound, tile, product[offset + HEAD_DIM : offset + 2 * HEAD_DIM])
        if c == SLABS - 1:
            sums = lax.dot_general(
                key_pos, jnp.ones((tokens, LANES), BF), over_tokens, preferred_element_type=F32
            )
            tile = jnp.where(lane < bound, tile, 0.0)
            for h in range(HEADS):
                tile = jnp.where(
                    lane == bound + h, sums[HEAD_DIM * h : HEAD_DIM * (h + 1)], tile
                )
        out_ref[SUB * c : SUB * (c + 1)] = tile.reshape(SUB, 8, LANES).astype(BF)
    rest = PIECES - SUB * SLABS
    out_ref[SUB * SLABS :] = jnp.zeros((rest, 8, LANES), BF)


def prefix_kernel(in_ref, out_ref):
    per_block = 16

    def block(b, total):
        here = in_ref[pl.ds(b * per_block, per_block)].astype(F32)
        total = total + jnp.sum(here, axis=0)
        out_ref[pl.ds(b * per_block, per_block)] = jnp.broadcast_to(
            total.astype(BF)[None], (per_block, 8, LANES)
        )
        return total

    lax.fori_loop(0, PIECES // per_block, block, jnp.zeros((8, LANES), F32))


def attend_kernel(q_ref, state_ref, att_ref):
    query_pos = jnp.maximum(q_ref[...], 0)
    lane = lax.broadcasted_iota(jnp.int32, (HEAD_DIM, LANES), 1)
    tile_of = lambda c: state_ref[SUB * c : SUB * (c + 1)].astype(F32).reshape(HEAD_DIM, LANES)
    sums = tile_of(SLABS - 1)
    z_lane = D - LANES * (SLABS - 1)
    for c in range(SLABS):
        first, pair, bound, start, stop, offset = slab_of(c)
        tile = tile_of(c)
        weights = []
        for which in range(2):
            rows = []
            if offset > 0:
                rows.append(jnp.zeros((offset, LANES), F32))
            for k in range(pair):
                if which == 0:
                    part = tile
                else:
                    h = z_lane + first + k
                    part = jnp.broadcast_to(sums[:, h : h + 1], (HEAD_DIM, LANES))
                inside = (lane < bound) if k == 0 else (lane >= bound)
                rows.append(jnp.where(inside, part, 0.0))
            left = stop - start - offset - pair * HEAD_DIM
            if left > 0:
                rows.append(jnp.zeros((left, LANES), F32))
            weights.append(jnp.concatenate(rows, axis=0))
        weight = jnp.concatenate(weights, axis=1).astype(BF)
        both = jnp.dot(query_pos[:, start:stop], weight, preferred_element_type=F32)
        attended = (both[:, :LANES] / (both[:, LANES:] + EPS)).astype(BF)
        width = min(LANES, D - LANES * c)
        att_ref[:, LANES * c : LANES * c + width] = attended[:, :width]


def hidden_kernel(att_ref, stream_ref, w_hbm, both_ref, early_ref, w_ref, sems):
    tokens = att_ref.shape[0]
    step = 384
    spans = [(n, min(n + step, D)) for n in range(0, D, step)]
    copies = []
    for i, (n, stop) in enumerate(spans):
        span = pl.ds(n, stop - n)
        copies.append(pltpu.make_async_copy(w_hbm.at[:, span], w_ref.at[:, span], sems.at[i]))
    for copy in copies:
        copy.start()
    for copy, (n, stop) in zip(copies, spans):
        cols = slice(n, stop)
        copy.wait()
        out = jnp.dot(att_ref[...], w_ref[:, cols], preferred_element_type=F32)
        out = (out + stream_ref[:, cols].astype(F32)).astype(BF)
        for r in range(tokens // 32):
            rows = slice(16 * r, 16 * r + 16)
            both_ref[0, rows, cols] = out[32 * r : 32 * r + 16]
            early_ref[rows, cols] = out[32 * r : 32 * r + 16]
            both_ref[1, rows, cols] = out[32 * r + 16 : 32 * r + 32]


def spatial_kernel(hid_ref, w_ref, taps_ref, out_ref, act_ref):
    groups, rows, model = hid_ref.shape
    tokens, cols = groups * rows, 16
    width = w_ref.shape[1]
    hid = hid_ref[...].reshape(tokens, model)
    product = jnp.dot(hid, w_ref[...], preferred_element_type=F32)
    act = (product * jax.nn.sigmoid(product)).astype(BF).astype(F32)
    act_ref[:cols] = jnp.zeros((cols, width), F32)
    act_ref[cols + tokens :] = jnp.zeros((cols, width), F32)
    act_ref[cols : cols + tokens] = act
    taps = taps_ref[...]
    chunk = 32
    col = lax.broadcasted_iota(jnp.int32, (chunk, width), 0) % cols
    for r in range(0, tokens, chunk):
        near = [act_ref[r + cols * a : r + cols * a + chunk] for a in range(3)]
        left, mid, right = (
            near[0] * taps[b : b + 1] + near[1] * taps[3 + b : 4 + b] + near[2] * taps[6 + b : 7 + b]
            for b in range(3)
        )
        left = jnp.where(col == 0, 0.0, pltpu.roll(left, 1, 0))
        right = jnp.where(col == cols - 1, 0.0, pltpu.roll(right, chunk - 1, 0))
        out_ref[r : r + chunk] = (left + mid + right).astype(BF)


def point_kernel(place_ref, now_ref, one_ref, two_ref, taps_ref, w_ref, mine_ref, other_ref):
    half = w_ref.shape[0]
    taps = taps_ref[...]
    mix = now_ref[...].astype(F32) * taps[0:1]
    mix = mix + one_ref[...].astype(F32) * taps[1:2]
    mix = mix + two_ref[...].astype(F32) * taps[2:3]
    gate = mix[:, half:]
    gated = (mix[:, :half] * (gate * jax.nn.sigmoid(gate))).astype(BF)
    out = jnp.dot(gated, w_ref[...], preferred_element_type=F32).astype(BF)
    y, core = place_ref[0], place_ref[1]
    i = pl.program_id(0)
    rows = out.shape[0] // 4
    for k in range(4):
        target = 4 * i + k
        slot = (target // 2 - y + 4) % 4

        @pl.when(core == k % 2)
        def _():
            mine_ref[slot] = out[rows * k : rows * (k + 1)]

        @pl.when(core != k % 2)
        def _():
            other_ref[slot] = out[rows * k : rows * (k + 1)]


def sum_kernel(count, mine_ref, other_ref, hidden_ref, *refs):
    kept_ref, *sends = refs[count:]
    total = lambda k: mine_ref[k].astype(F32) + other_ref[k].astype(F32)
    kept_ref[...] = hidden_ref[...].astype(F32) + total(0)
    for k, send in enumerate(sends):
        send[...] = total(k + 1).astype(BF)


def final_kernel(early_ref, late_ref, *refs):
    pieces, out_ref = refs[:6], refs[6]
    for f, kept in enumerate((early_ref, late_ref)):
        total = kept[...]
        for piece in pieces[3 * f : 3 * f + 3]:
            total = total + piece[...].astype(F32)
        out = total.astype(BF)
        for r in range(out_ref.shape[0]):
            out_ref[r, f] = out[16 * r : 16 * r + 16]


def params(mib):
    return pltpu.CompilerParams(vmem_limit_bytes=mib * MIB)


VMEM = pl.BlockSpec(memory_space=pltpu.VMEM)


def on_device(
    stream_in, queries, key_rows, value_rows, w_output, w_inner, w_down, spatial_taps, temporal_taps
):
    row_count, frames, col_count, width = queries.shape
    tokens = row_count * frames * col_count
    flat = lambda a: a.reshape(tokens, width)
    chan = w_inner.shape[2]
    peers = lax.axis_size("tile")
    place = lax.axis_index("tile")
    where_am_i = jnp.stack([place // 2, place % 2]).astype(jnp.int32)

    w_out_whole = lax.all_gather(w_output, "tile", axis=0, tiled=True)
    w_flat = w_inner.reshape(width, 2 * chan)
    taps_s = spatial_taps.reshape(9, 2 * chan)
    taps_t = temporal_taps.reshape(TAPS, 2 * chan)

    pieces = jax.ShapeDtypeStruct((PIECES, 8, LANES), BF)
    parts = pl.pallas_call(
        kv_kernel,
        out_shape=pieces,
        in_specs=[VMEM] * 2,
        out_specs=VMEM,
        scratch_shapes=[pltpu.VMEM((tokens, LANES), BF)],
        compiler_params=params(40),
    )(flat(key_rows), flat(value_rows))
    everyone = ("blk", "tile")
    parts = lax.all_to_all(parts, everyone, 0, 0, tiled=True)
    sums = pl.pallas_call(
        prefix_kernel, out_shape=pieces, in_specs=[VMEM], out_specs=VMEM, compiler_params=params(40)
    )(parts)
    state = lax.all_to_all(sums, everyone, 0, 0, tiled=True)

    anywhere = pl.BlockSpec(memory_space=pl.ANY)
    frame_rows = row_count * col_count
    attended = pl.pallas_call(
        attend_kernel,
        out_shape=jax.ShapeDtypeStruct((tokens, width), BF),
        in_specs=[VMEM, VMEM],
        out_specs=VMEM,
        compiler_params=params(40),
    )(flat(queries), state)
    one_frame = jax.ShapeDtypeStruct((frame_rows, width), BF)
    hidden, early = pl.pallas_call(
        hidden_kernel,
        out_shape=[jax.ShapeDtypeStruct((2, frame_rows, width), BF), one_frame],
        in_specs=[VMEM, VMEM, anywhere],
        out_specs=[VMEM, VMEM],
        scratch_shapes=[pltpu.VMEM((width, width), BF), pltpu.SemaphoreType.DMA((6,))],
        compiler_params=params(52),
    )(attended, flat(stream_in), w_out_whole)

    whole_rows = peers * frame_rows
    block = 256

    def spatial_call(whole, f):
        return pl.pallas_call(
            spatial_kernel,
            out_shape=jax.ShapeDtypeStruct((whole_rows, 2 * chan), BF),
            grid=(2 * chan // block,),
            in_specs=[
                pl.BlockSpec((peers, None, frame_rows, width), lambda i: (0, f, 0, 0)),
                pl.BlockSpec((width, block), lambda i: (0, i)),
                pl.BlockSpec((9, block), lambda i: (0, i)),
            ],
            out_specs=pl.BlockSpec((whole_rows, block), lambda i: (0, i)),
            scratch_shapes=[pltpu.VMEM((whole_rows + 2 * col_count, block), F32)],
            compiler_params=params(52),
        )(whole, w_flat, taps_s)

    row_block = 256
    point_call = pl.pallas_call(
        point_kernel,
        out_shape=[jax.ShapeDtypeStruct((4, frame_rows, width), BF)] * 2,
        grid=(whole_rows // row_block,),
        in_specs=[pl.BlockSpec(memory_space=pltpu.SMEM)]
        + [pl.BlockSpec((row_block, 2 * chan), lambda i: (i, 0))] * 3
        + [
            pl.BlockSpec((TAPS, 2 * chan), lambda i: (0, 0)),
            pl.BlockSpec((chan, width), lambda i: (0, 0)),
        ],
        out_specs=[pl.BlockSpec((4, frame_rows, width), lambda i: (0, 0, 0))] * 2,
        compiler_params=params(40),
    )

    blocks = lax.axis_size("blk")
    next_frames = [(i, i + 1) for i in range(blocks - 1)]
    other_core = [(i, i ^ 1) for i in range(peers)]
    ahead = [[(i, (i + 2 * k) % peers) for i in range(peers)] for k in range(4)]

    before_early = lax.ppermute(early, "blk", next_frames)
    whole = lax.all_gather(hidden, "tile", axis=0)
    before_whole = lax.all_gather(before_early[None], "tile", axis=0)
    late_sp = spatial_call(whole, 1)
    before_late_sp = lax.ppermute(late_sp, "blk", next_frames)
    early_sp = spatial_call(whole, 0)
    before_early_sp = spatial_call(before_whole, 0)

    def reduced(f, now, one, two, needed):
        mine, other = point_call(where_am_i, now, one, two, taps_t, w_down)
        from_core = lax.ppermute(other, "tile", other_core)
        kept, *sends = pl.pallas_call(
            functools.partial(sum_kernel, len(needed)),
            out_shape=[jax.ShapeDtypeStruct((frame_rows, width), F32)] + [one_frame] * 3,
            grid=(1,),
            in_specs=[pl.BlockSpec((4, frame_rows, width), lambda i: (0, 0, 0))] * 2
            + [pl.BlockSpec((None, frame_rows, width), lambda i: (f, 0, 0))]
            + [anywhere] * len(needed),
            out_specs=[pl.BlockSpec((frame_rows, width), lambda i: (0, 0))] * 4,
            compiler_params=params(20),
        )(mine, from_core, hidden, *needed)
        return kept, [lax.ppermute(part, "tile", ahead[k + 1]) for k, part in enumerate(sends)]

    late_kept, late_back = reduced(1, late_sp, early_sp, before_late_sp, [])
    early_kept, early_back = reduced(0, early_sp, before_late_sp, before_early_sp, late_back[:1])
    return pl.pallas_call(
        final_kernel,
        out_shape=jax.ShapeDtypeStruct(stream_in.shape, BF),
        in_specs=[VMEM] * 8,
        out_specs=VMEM,
        compiler_params=params(20),
    )(early_kept, late_kept, *early_back, *late_back)


def solution(mesh):
    in_specs = (
        P("tile", "blk", None, None),
        P("tile", "blk", None, None),
        P("tile", "blk", None, None),
        P("tile", "blk", None, None),
        P("tile", None),
        P(None, None, "tile"),
        P("tile", None),
        P(None, None, None, "tile"),
        P(None, None, "tile"),
    )
    out_specs = P("tile", "blk", None, None)
    return jax.shard_map(
        on_device, mesh=mesh, in_specs=in_specs, out_specs=out_specs, check_vma=False
    )
```

```python
import functools

import jax
import jax.numpy as jnp
from jax import lax
from jax.experimental import pallas as pl
from jax.experimental.pallas import tpu as pltpu
from jax.sharding import PartitionSpec as P

HEADS = 20
HEAD_DIM = 112
D = 2240
TAPS = 3
EPS = 1e-6
LANES = 128
SLABS = 18
SUB = 14
PIECES = 256
BF = jnp.bfloat16
F32 = jnp.float32
MIB = 1 << 20


def slab_of(c):
    first = (LANES * c) // HEAD_DIM
    bound = HEAD_DIM * (first + 1) - LANES * c
    start = (HEAD_DIM * first) // LANES * LANES
    pair = 2 if first + 1 < HEADS else 1
    stop = min(-(-(HEAD_DIM * (first + pair)) // LANES) * LANES, D)
    return first, pair, bound, start, stop, HEAD_DIM * first - start


def kv_kernel(k_ref, v_ref, out_ref, last_ref):
    tokens = k_ref.shape[0]
    key_pos = jnp.maximum(k_ref[...], 0)
    last_ref[...] = jnp.ones((tokens, LANES), BF)
    last_ref[:, : D - LANES * (SLABS - 1)] = v_ref[:, LANES * (SLABS - 1) :]
    lane = lax.broadcasted_iota(jnp.int32, (HEAD_DIM, LANES), 1)
    over_tokens = (((0,), (0,)), ((), ()))
    for c in range(SLABS):
        first, pair, bound, start, stop, offset = slab_of(c)
        values = last_ref[...] if c == SLABS - 1 else v_ref[:, LANES * c : LANES * (c + 1)]
        product = lax.dot_general(
            key_pos[:, start:stop], values, over_tokens, preferred_element_type=F32
        )
        tile = product[offset : offset + HEAD_DIM]
        if pair == 2:
            tile = jnp.where(lane < bound, tile, product[offset + HEAD_DIM : offset + 2 * HEAD_DIM])
        if c == SLABS - 1:
            sums = lax.dot_general(
                key_pos, jnp.ones((tokens, LANES), BF), over_tokens, preferred_element_type=F32
            )
            tile = jnp.where(lane < bound, tile, 0.0)
            for h in range(HEADS):
                tile = jnp.where(
                    lane == bound + h, sums[HEAD_DIM * h : HEAD_DIM * (h + 1)], tile
                )
        out_ref[SUB * c : SUB * (c + 1)] = tile.reshape(SUB, 8, LANES).astype(BF)
    rest = PIECES - SUB * SLABS
    out_ref[SUB * SLABS :] = jnp.zeros((rest, 8, LANES), BF)


def prefix_kernel(in_ref, out_ref):
    per_block = 16

    def block(b, total):
        here = in_ref[pl.ds(b * per_block, per_block)].astype(F32)
        total = total + jnp.sum(here, axis=0)
        out_ref[pl.ds(b * per_block, per_block)] = jnp.broadcast_to(
            total.astype(BF)[None], (per_block, 8, LANES)
        )
        return total

    lax.fori_loop(0, PIECES // per_block, block, jnp.zeros((8, LANES), F32))


def attend_kernel(q_ref, state_ref, att_ref):
    query_pos = jnp.maximum(q_ref[...], 0)
    lane = lax.broadcasted_iota(jnp.int32, (HEAD_DIM, LANES), 1)
    tile_of = lambda c: state_ref[SUB * c : SUB * (c + 1)].astype(F32).reshape(HEAD_DIM, LANES)
    sums = tile_of(SLABS - 1)
    z_lane = D - LANES * (SLABS - 1)
    for c in range(SLABS):
        first, pair, bound, start, stop, offset = slab_of(c)
        tile = tile_of(c)
        weights = []
        for which in range(2):
            rows = []
            if offset > 0:
                rows.append(jnp.zeros((offset, LANES), F32))
            for k in range(pair):
                if which == 0:
                    part = tile
                else:
                    h = z_lane + first + k
                    part = jnp.broadcast_to(sums[:, h : h + 1], (HEAD_DIM, LANES))
                inside = (lane < bound) if k == 0 else (lane >= bound)
                rows.append(jnp.where(inside, part, 0.0))
            left = stop - start - offset - pair * HEAD_DIM
            if left > 0:
                rows.append(jnp.zeros((left, LANES), F32))
            weights.append(jnp.concatenate(rows, axis=0))
        weight = jnp.concatenate(weights, axis=1).astype(BF)
        both = jnp.dot(query_pos[:, start:stop], weight, preferred_element_type=F32)
        attended = (both[:, :LANES] / (both[:, LANES:] + EPS)).astype(BF)
        width = min(LANES, D - LANES * c)
        att_ref[:, LANES * c : LANES * c + width] = attended[:, :width]


def hidden_kernel(att_ref, stream_ref, w_hbm, early_ref, late_ref, w_ref, sems):
    tokens = att_ref.shape[0]
    step = 384
    spans = [(n, min(n + step, D)) for n in range(0, D, step)]
    copies = []
    for i, (n, stop) in enumerate(spans):
        span = pl.ds(n, stop - n)
        copies.append(pltpu.make_async_copy(w_hbm.at[:, span], w_ref.at[:, span], sems.at[i]))
    for copy in copies:
        copy.start()
    for copy, (n, stop) in zip(copies, spans):
        cols = slice(n, stop)
        copy.wait()
        out = jnp.dot(att_ref[...], w_ref[:, cols], preferred_element_type=F32)
        out = (out + stream_ref[:, cols].astype(F32)).astype(BF)
        for r in range(tokens // 32):
            rows = slice(16 * r, 16 * r + 16)
            early_ref[rows, cols] = out[32 * r : 32 * r + 16]
            late_ref[rows, cols] = out[32 * r + 16 : 32 * r + 32]


def depthwise(hid, w_ref, taps_ref, out_ref, act_ref):
    tokens, cols = hid.shape[0], 16
    width = w_ref.shape[1]
    product = jnp.dot(hid, w_ref[...], preferred_element_type=F32)
    act = (product * jax.nn.sigmoid(product)).astype(BF).astype(F32)
    act_ref[:cols] = jnp.zeros((cols, width), F32)
    act_ref[cols + tokens :] = jnp.zeros((cols, width), F32)
    act_ref[cols : cols + tokens] = act
    taps = taps_ref[...]
    chunk = 32
    col = lax.broadcasted_iota(jnp.int32, (chunk, width), 0) % cols
    for r in range(0, tokens, chunk):
        near = [act_ref[r + cols * a : r + cols * a + chunk] for a in range(3)]
        left, mid, right = (
            near[0] * taps[b : b + 1] + near[1] * taps[3 + b : 4 + b] + near[2] * taps[6 + b : 7 + b]
            for b in range(3)
        )
        left = jnp.where(col == 0, 0.0, pltpu.roll(left, 1, 0))
        right = jnp.where(col == cols - 1, 0.0, pltpu.roll(right, chunk - 1, 0))
        out_ref[r : r + chunk] = (left + mid + right).astype(BF)


def spatial_kernel(hid_ref, w_ref, taps_ref, needed_ref, out_ref, act_ref):
    groups, rows, model = hid_ref.shape
    depthwise(hid_ref[...].reshape(groups * rows, model), w_ref, taps_ref, out_ref, act_ref)


def pieces_kernel(place_ref, *refs):
    peers = 8
    pieces, (w_ref, taps_ref, out_ref, act_ref, hid_ref) = refs[:peers], refs[peers:]
    rows = pieces[0].shape[0]

    @pl.when(pl.program_id(0) == 0)
    def _():
        for p, piece in enumerate(pieces):
            source = 2 * ((place_ref[0] + 4 - p // 2) % 4) + (place_ref[1] + p % 2) % 2
            hid_ref[pl.ds(pl.multiple_of(source * rows, rows), rows)] = piece[...]

    depthwise(hid_ref[...], w_ref, taps_ref, out_ref, act_ref)


def point_kernel(
    place_ref, now_ref, one_ref, two_ref, taps_ref, w_ref, needed_ref, mine_ref, other_ref
):
    half = w_ref.shape[0]
    taps = taps_ref[...]
    mix = now_ref[...].astype(F32) * taps[0:1]
    mix = mix + one_ref[...].astype(F32) * taps[1:2]
    mix = mix + two_ref[...].astype(F32) * taps[2:3]
    gate = mix[:, half:]
    gated = (mix[:, :half] * (gate * jax.nn.sigmoid(gate))).astype(BF)
    out = jnp.dot(gated, w_ref[...], preferred_element_type=F32).astype(BF)
    y, core = place_ref[0], place_ref[1]
    i = pl.program_id(0)
    rows = out.shape[0] // 4
    for k in range(4):
        target = 4 * i + k
        slot = (target // 2 - y + 4) % 4

        @pl.when(core == k % 2)
        def _():
            mine_ref[slot] = out[rows * k : rows * (k + 1)]

        @pl.when(core != k % 2)
        def _():
            other_ref[slot] = out[rows * k : rows * (k + 1)]


def sum_kernel(mine_ref, other_ref, hidden_ref, kept_ref, *sends):
    total = lambda k: mine_ref[k].astype(F32) + other_ref[k].astype(F32)
    kept_ref[...] = hidden_ref[...].astype(F32) + total(0)
    for k, send in enumerate(sends):
        send[...] = total(k + 1).astype(BF)


def stack_kernel(one_ref, two_ref, needed_ref, out_ref):
    out_ref[0] = one_ref[...]
    out_ref[1] = two_ref[...]


def final_kernel(early_ref, late_ref, *refs):
    pieces, out_ref = refs[:6], refs[6]
    for f, kept in enumerate((early_ref, late_ref)):
        total = kept[...]
        for piece in pieces[3 * f : 3 * f + 3]:
            total = total + piece[...].astype(F32)
        out = total.astype(BF)
        for r in range(out_ref.shape[0]):
            out_ref[r, f] = out[16 * r : 16 * r + 16]


def params(mib):
    return pltpu.CompilerParams(vmem_limit_bytes=mib * MIB)


VMEM = pl.BlockSpec(memory_space=pltpu.VMEM)


def on_device(
    stream_in, queries, key_rows, value_rows, w_output, w_inner, w_down, spatial_taps, temporal_taps
):
    row_count, frames, col_count, width = queries.shape
    tokens = row_count * frames * col_count
    flat = lambda a: a.reshape(tokens, width)
    chan = w_inner.shape[2]
    peers = lax.axis_size("tile")
    place = lax.axis_index("tile")
    where_am_i = jnp.stack([place // 2, place % 2]).astype(jnp.int32)

    w_out_whole = lax.all_gather(w_output, "tile", axis=0, tiled=True)
    w_flat = w_inner.reshape(width, 2 * chan)
    taps_s = spatial_taps.reshape(9, 2 * chan)
    taps_t = temporal_taps.reshape(TAPS, 2 * chan)

    pieces = jax.ShapeDtypeStruct((PIECES, 8, LANES), BF)
    parts = pl.pallas_call(
        kv_kernel,
        out_shape=pieces,
        in_specs=[VMEM] * 2,
        out_specs=VMEM,
        scratch_shapes=[pltpu.VMEM((tokens, LANES), BF)],
        compiler_params=params(40),
    )(flat(key_rows), flat(value_rows))
    everyone = ("blk", "tile")
    parts = lax.all_to_all(parts, everyone, 0, 0, tiled=True)
    sums = pl.pallas_call(
        prefix_kernel, out_shape=pieces, in_specs=[VMEM], out_specs=VMEM, compiler_params=params(40)
    )(parts)
    state = lax.all_to_all(sums, everyone, 0, 0, tiled=True)

    anywhere = pl.BlockSpec(memory_space=pl.ANY)
    frame_rows = row_count * col_count
    attended = pl.pallas_call(
        attend_kernel,
        out_shape=jax.ShapeDtypeStruct((tokens, width), BF),
        in_specs=[VMEM, VMEM],
        out_specs=VMEM,
        compiler_params=params(40),
    )(flat(queries), state)
    one_frame = jax.ShapeDtypeStruct((frame_rows, width), BF)
    early, late = pl.pallas_call(
        hidden_kernel,
        out_shape=[one_frame] * 2,
        in_specs=[VMEM, VMEM, anywhere],
        out_specs=[VMEM, VMEM],
        scratch_shapes=[pltpu.VMEM((width, width), BF), pltpu.SemaphoreType.DMA((6,))],
        compiler_params=params(52),
    )(attended, flat(stream_in), w_out_whole)

    whole_rows = peers * frame_rows
    block = 256

    spatial_out = dict(
        out_shape=jax.ShapeDtypeStruct((whole_rows, 2 * chan), BF),
        grid=(2 * chan // block,),
        out_specs=pl.BlockSpec((whole_rows, block), lambda i: (0, i)),
        compiler_params=params(52),
    )
    weight_specs = [
        pl.BlockSpec((width, block), lambda i: (0, i)),
        pl.BlockSpec((9, block), lambda i: (0, i)),
    ]
    act_scratch = pltpu.VMEM((whole_rows + 2 * col_count, block), F32)

    def spatial_call(whole, f, needed):
        return pl.pallas_call(
            spatial_kernel,
            in_specs=[pl.BlockSpec((peers, None, frame_rows, width), lambda i: (0, f, 0, 0))]
            + weight_specs
            + [anywhere],
            scratch_shapes=[act_scratch],
            **spatial_out,
        )(whole, w_flat, taps_s, needed)

    def pieces_call(pieces):
        return pl.pallas_call(
            pieces_kernel,
            in_specs=[pl.BlockSpec(memory_space=pltpu.SMEM)]
            + [pl.BlockSpec((frame_rows, width), lambda i: (0, 0))] * peers
            + weight_specs,
            scratch_shapes=[act_scratch, pltpu.VMEM((whole_rows, width), BF)],
            **spatial_out,
        )(where_am_i, *pieces, w_flat, taps_s)

    row_block = 256
    point_call = pl.pallas_call(
        point_kernel,
        out_shape=[jax.ShapeDtypeStruct((4, frame_rows, width), BF)] * 2,
        grid=(whole_rows // row_block,),
        in_specs=[pl.BlockSpec(memory_space=pltpu.SMEM)]
        + [pl.BlockSpec((row_block, 2 * chan), lambda i: (i, 0))] * 3
        + [
            pl.BlockSpec((TAPS, 2 * chan), lambda i: (0, 0)),
            pl.BlockSpec((chan, width), lambda i: (0, 0)),
            anywhere,
        ],
        out_specs=[pl.BlockSpec((4, frame_rows, width), lambda i: (0, 0, 0))] * 2,
        compiler_params=params(40),
    )

    blocks = lax.axis_size("blk")
    next_frames = [(i, i + 1) for i in range(blocks - 1)]
    other_core = [(i, i ^ 1) for i in range(peers)]
    ahead = [[(i, (i + 2 * k) % peers) for i in range(peers)] for k in range(4)]

    late_along = [late] + [lax.ppermute(late, "tile", ahead[k]) for k in (1, 2, 3)]
    before_early = lax.ppermute(early, "blk", next_frames)
    pieces = []
    for part in late_along:
        pieces += [part, lax.ppermute(part, "tile", other_core)]
    stacked = pl.pallas_call(
        stack_kernel,
        out_shape=jax.ShapeDtypeStruct((2, frame_rows, width), BF),
        in_specs=[VMEM, VMEM, anywhere],
        out_specs=VMEM,
        compiler_params=params(20),
    )(early, before_early, late_along[1])
    whole = lax.all_gather(stacked, "tile", axis=0)
    late_sp = pieces_call(pieces)
    before_late_sp = lax.ppermute(late_sp, "blk", next_frames)
    early_sp = spatial_call(whole, 0, late_sp)
    before_early_sp = spatial_call(whole, 1, early_sp)

    def core_shares(now, one, two, needed):
        mine, other = point_call(where_am_i, now, one, two, taps_t, w_down, needed)
        return mine, lax.ppermute(other, "tile", other_core)

    def sums(mine, from_core, rows):
        kept, *sends = pl.pallas_call(
            sum_kernel,
            out_shape=[jax.ShapeDtypeStruct((frame_rows, width), F32)] + [one_frame] * 3,
            in_specs=[VMEM] * 3,
            out_specs=[VMEM] * 4,
            compiler_params=params(20),
        )(mine, from_core, rows)
        return kept, [lax.ppermute(part, "tile", ahead[k + 1]) for k, part in enumerate(sends)]

    late_shares = core_shares(late_sp, early_sp, before_late_sp, before_early_sp)
    early_shares = core_shares(early_sp, before_late_sp, before_early_sp, late_shares[0])
    late_kept, late_back = sums(*late_shares, late)
    early_kept, early_back = sums(*early_shares, early)
    return pl.pallas_call(
        final_kernel,
        out_shape=jax.ShapeDtypeStruct(stream_in.shape, BF),
        in_specs=[VMEM] * 8,
        out_specs=VMEM,
        compiler_params=params(20),
    )(early_kept, late_kept, *early_back, *late_back)


def solution(mesh):
    in_specs = (
        P("tile", "blk", None, None),
        P("tile", "blk", None, None),
        P("tile", "blk", None, None),
        P("tile", "blk", None, None),
        P("tile", None),
        P(None, None, "tile"),
        P("tile", None),
        P(None, None, None, "tile"),
        P(None, None, "tile"),
    )
    out_specs = P("tile", "blk", None, None)
    return jax.shard_map(
        on_device, mesh=mesh, in_specs=in_specs, out_specs=out_specs, check_vma=False
    )
```

```python
import functools

import jax
import jax.numpy as jnp
from jax import lax
from jax.experimental import pallas as pl
from jax.experimental.pallas import tpu as pltpu
from jax.sharding import PartitionSpec as P

HEADS = 20
HEAD_DIM = 112
D = 2240
TAPS = 3
EPS = 1e-6
LANES = 128
SLABS = 18
SUB = 14
PIECES = 256
BF = jnp.bfloat16
F32 = jnp.float32
MIB = 1 << 20


def slab_of(c):
    first = (LANES * c) // HEAD_DIM
    bound = HEAD_DIM * (first + 1) - LANES * c
    start = (HEAD_DIM * first) // LANES * LANES
    pair = 2 if first + 1 < HEADS else 1
    stop = min(-(-(HEAD_DIM * (first + pair)) // LANES) * LANES, D)
    return first, pair, bound, start, stop, HEAD_DIM * first - start


def kv_kernel(k_ref, v_ref, out_ref, last_ref):
    tokens = k_ref.shape[0]
    key_pos = jnp.maximum(k_ref[...], 0)
    last_ref[...] = jnp.ones((tokens, LANES), BF)
    last_ref[:, : D - LANES * (SLABS - 1)] = v_ref[:, LANES * (SLABS - 1) :]
    lane = lax.broadcasted_iota(jnp.int32, (HEAD_DIM, LANES), 1)
    over_tokens = (((0,), (0,)), ((), ()))
    for c in range(SLABS):
        first, pair, bound, start, stop, offset = slab_of(c)
        values = last_ref[...] if c == SLABS - 1 else v_ref[:, LANES * c : LANES * (c + 1)]
        product = lax.dot_general(
            key_pos[:, start:stop], values, over_tokens, preferred_element_type=F32
        )
        tile = product[offset : offset + HEAD_DIM]
        if pair == 2:
            tile = jnp.where(lane < bound, tile, product[offset + HEAD_DIM : offset + 2 * HEAD_DIM])
        if c == SLABS - 1:
            sums = lax.dot_general(
                key_pos, jnp.ones((tokens, LANES), BF), over_tokens, preferred_element_type=F32
            )
            tile = jnp.where(lane < bound, tile, 0.0)
            for h in range(HEADS):
                tile = jnp.where(
                    lane == bound + h, sums[HEAD_DIM * h : HEAD_DIM * (h + 1)], tile
                )
        out_ref[SUB * c : SUB * (c + 1)] = tile.reshape(SUB, 8, LANES).astype(BF)
    rest = PIECES - SUB * SLABS
    out_ref[SUB * SLABS :] = jnp.zeros((rest, 8, LANES), BF)


def prefix_kernel(in_ref, out_ref):
    per_block = 16

    def block(b, total):
        here = in_ref[pl.ds(b * per_block, per_block)].astype(F32)
        total = total + jnp.sum(here, axis=0)
        out_ref[pl.ds(b * per_block, per_block)] = jnp.broadcast_to(
            total.astype(BF)[None], (per_block, 8, LANES)
        )
        return total

    lax.fori_loop(0, PIECES // per_block, block, jnp.zeros((8, LANES), F32))


def attend_kernel(q_ref, state_ref, att_ref):
    query_pos = jnp.maximum(q_ref[...], 0)
    lane = lax.broadcasted_iota(jnp.int32, (HEAD_DIM, LANES), 1)
    tile_of = lambda c: state_ref[SUB * c : SUB * (c + 1)].astype(F32).reshape(HEAD_DIM, LANES)
    sums = tile_of(SLABS - 1)
    z_lane = D - LANES * (SLABS - 1)
    for c in range(SLABS):
        first, pair, bound, start, stop, offset = slab_of(c)
        tile = tile_of(c)
        weights = []
        for which in range(2):
            rows = []
            if offset > 0:
                rows.append(jnp.zeros((offset, LANES), F32))
            for k in range(pair):
                if which == 0:
                    part = tile
                else:
                    h = z_lane + first + k
                    part = jnp.broadcast_to(sums[:, h : h + 1], (HEAD_DIM, LANES))
                inside = (lane < bound) if k == 0 else (lane >= bound)
                rows.append(jnp.where(inside, part, 0.0))
            left = stop - start - offset - pair * HEAD_DIM
            if left > 0:
                rows.append(jnp.zeros((left, LANES), F32))
            weights.append(jnp.concatenate(rows, axis=0))
        weight = jnp.concatenate(weights, axis=1).astype(BF)
        both = jnp.dot(query_pos[:, start:stop], weight, preferred_element_type=F32)
        attended = (both[:, :LANES] / (both[:, LANES:] + EPS)).astype(BF)
        width = min(LANES, D - LANES * c)
        att_ref[:, LANES * c : LANES * c + width] = attended[:, :width]


def hidden_kernel(att_ref, stream_ref, w_hbm, needed_ref, early_ref, late_ref, w_ref, sems):
    tokens = att_ref.shape[0]
    step = 384
    spans = [(n, min(n + step, D)) for n in range(0, D, step)]
    copies = []
    for i, (n, stop) in enumerate(spans):
        span = pl.ds(n, stop - n)
        copies.append(pltpu.make_async_copy(w_hbm.at[:, span], w_ref.at[:, span], sems.at[i]))
    for copy in copies:
        copy.start()
    for copy, (n, stop) in zip(copies, spans):
        cols = slice(n, stop)
        copy.wait()
        out = jnp.dot(att_ref[...], w_ref[:, cols], preferred_element_type=F32)
        out = (out + stream_ref[:, cols].astype(F32)).astype(BF)
        for r in range(tokens // 32):
            rows = slice(16 * r, 16 * r + 16)
            early_ref[rows, cols] = out[32 * r : 32 * r + 16]
            late_ref[rows, cols] = out[32 * r + 16 : 32 * r + 32]


def depthwise(hid, w_ref, taps_ref, out_ref, act_ref):
    tokens, cols = hid.shape[0], 16
    width = w_ref.shape[1]
    product = jnp.dot(hid, w_ref[...], preferred_element_type=F32)
    act = (product * jax.nn.sigmoid(product)).astype(BF).astype(F32)
    act_ref[:cols] = jnp.zeros((cols, width), F32)
    act_ref[cols + tokens :] = jnp.zeros((cols, width), F32)
    act_ref[cols : cols + tokens] = act
    taps = taps_ref[...]
    chunk = 32
    col = lax.broadcasted_iota(jnp.int32, (chunk, width), 0) % cols
    for r in range(0, tokens, chunk):
        near = [act_ref[r + cols * a : r + cols * a + chunk] for a in range(3)]
        left, mid, right = (
            near[0] * taps[b : b + 1] + near[1] * taps[3 + b : 4 + b] + near[2] * taps[6 + b : 7 + b]
            for b in range(3)
        )
        left = jnp.where(col == 0, 0.0, pltpu.roll(left, 1, 0))
        right = jnp.where(col == cols - 1, 0.0, pltpu.roll(right, chunk - 1, 0))
        out_ref[r : r + chunk] = (left + mid + right).astype(BF)


def spatial_kernel(hid_ref, w_ref, taps_ref, needed_ref, out_ref, act_ref):
    groups, rows, model = hid_ref.shape
    depthwise(hid_ref[...].reshape(groups * rows, model), w_ref, taps_ref, out_ref, act_ref)


def pieces_kernel(place_ref, *refs):
    peers = 8
    pieces, (w_ref, taps_ref, out_ref, act_ref, hid_ref) = refs[:peers], refs[peers:]
    rows = pieces[0].shape[0]

    @pl.when(pl.program_id(0) == 0)
    def _():
        for p, piece in enumerate(pieces):
            source = 2 * ((place_ref[0] + 4 - p // 2) % 4) + (place_ref[1] + p % 2) % 2
            hid_ref[pl.ds(pl.multiple_of(source * rows, rows), rows)] = piece[...]

    depthwise(hid_ref[...], w_ref, taps_ref, out_ref, act_ref)


def point_kernel(
    place_ref, now_ref, one_ref, two_ref, taps_ref, w_ref, needed_ref, mine_ref, other_ref
):
    half = w_ref.shape[0]
    taps = taps_ref[...]
    mix = now_ref[...].astype(F32) * taps[0:1]
    mix = mix + one_ref[...].astype(F32) * taps[1:2]
    mix = mix + two_ref[...].astype(F32) * taps[2:3]
    gate = mix[:, half:]
    gated = (mix[:, :half] * (gate * jax.nn.sigmoid(gate))).astype(BF)
    out = jnp.dot(gated, w_ref[...], preferred_element_type=F32).astype(BF)
    y, core = place_ref[0], place_ref[1]
    i = pl.program_id(0)
    rows = out.shape[0] // 4
    for k in range(4):
        target = 4 * i + k
        slot = (target // 2 - y + 4) % 4

        @pl.when(core == k % 2)
        def _():
            mine_ref[slot] = out[rows * k : rows * (k + 1)]

        @pl.when(core != k % 2)
        def _():
            other_ref[slot] = out[rows * k : rows * (k + 1)]


def sum_kernel(mine_ref, other_ref, hidden_ref, kept_ref, *sends):
    total = lambda k: mine_ref[k].astype(F32) + other_ref[k].astype(F32)
    kept_ref[...] = hidden_ref[...].astype(F32) + total(0)
    for k, send in enumerate(sends):
        send[...] = total(k + 1).astype(BF)


def stack_kernel(one_ref, two_ref, *refs):
    out_ref = refs[-1]
    out_ref[0] = one_ref[...]
    out_ref[1] = two_ref[...]


def final_kernel(early_ref, late_ref, *refs):
    pieces, out_ref = refs[:6], refs[6]
    for f, kept in enumerate((early_ref, late_ref)):
        total = kept[...]
        for piece in pieces[3 * f : 3 * f + 3]:
            total = total + piece[...].astype(F32)
        out = total.astype(BF)
        for r in range(out_ref.shape[0]):
            out_ref[r, f] = out[16 * r : 16 * r + 16]


def params(mib):
    return pltpu.CompilerParams(vmem_limit_bytes=mib * MIB)


VMEM = pl.BlockSpec(memory_space=pltpu.VMEM)


def on_device(
    stream_in, queries, key_rows, value_rows, w_output, w_inner, w_down, spatial_taps, temporal_taps
):
    row_count, frames, col_count, width = queries.shape
    tokens = row_count * frames * col_count
    flat = lambda a: a.reshape(tokens, width)
    chan = w_inner.shape[2]
    peers = lax.axis_size("tile")
    place = lax.axis_index("tile")
    where_am_i = jnp.stack([place // 2, place % 2]).astype(jnp.int32)

    w_out_whole = lax.all_gather(w_output, "tile", axis=0, tiled=True)
    w_flat = w_inner.reshape(width, 2 * chan)
    taps_s = spatial_taps.reshape(9, 2 * chan)
    taps_t = temporal_taps.reshape(TAPS, 2 * chan)

    pieces = jax.ShapeDtypeStruct((PIECES, 8, LANES), BF)
    parts = pl.pallas_call(
        kv_kernel,
        out_shape=pieces,
        in_specs=[VMEM] * 2,
        out_specs=VMEM,
        scratch_shapes=[pltpu.VMEM((tokens, LANES), BF)],
        compiler_params=params(40),
    )(flat(key_rows), flat(value_rows))
    everyone = ("blk", "tile")
    parts = lax.all_to_all(parts, everyone, 0, 0, tiled=True)
    sums = pl.pallas_call(
        prefix_kernel, out_shape=pieces, in_specs=[VMEM], out_specs=VMEM, compiler_params=params(40)
    )(parts)
    state = lax.all_to_all(sums, everyone, 0, 0, tiled=True)

    anywhere = pl.BlockSpec(memory_space=pl.ANY)
    frame_rows = row_count * col_count
    attended = pl.pallas_call(
        attend_kernel,
        out_shape=jax.ShapeDtypeStruct((tokens, width), BF),
        in_specs=[VMEM, VMEM],
        out_specs=VMEM,
        compiler_params=params(40),
    )(flat(queries), state)
    one_frame = jax.ShapeDtypeStruct((frame_rows, width), BF)
    early, late = pl.pallas_call(
        hidden_kernel,
        out_shape=[one_frame] * 2,
        in_specs=[VMEM, VMEM, anywhere, anywhere],
        out_specs=[VMEM, VMEM],
        scratch_shapes=[pltpu.VMEM((width, width), BF), pltpu.SemaphoreType.DMA((6,))],
        compiler_params=params(52),
    )(attended, flat(stream_in), w_out_whole, w_flat)

    whole_rows = peers * frame_rows
    block = 256

    spatial_out = dict(
        out_shape=jax.ShapeDtypeStruct((whole_rows, 2 * chan), BF),
        grid=(2 * chan // block,),
        out_specs=pl.BlockSpec((whole_rows, block), lambda i: (0, i)),
        compiler_params=params(52),
    )
    weight_specs = [
        pl.BlockSpec((width, block), lambda i: (0, i)),
        pl.BlockSpec((9, block), lambda i: (0, i)),
    ]
    act_scratch = pltpu.VMEM((whole_rows + 2 * col_count, block), F32)

    def spatial_call(whole, f, needed):
        return pl.pallas_call(
            spatial_kernel,
            in_specs=[pl.BlockSpec((peers, None, frame_rows, width), lambda i: (0, f, 0, 0))]
            + weight_specs
            + [anywhere],
            scratch_shapes=[act_scratch],
            **spatial_out,
        )(whole, w_flat, taps_s, needed)

    def pieces_call(pieces):
        return pl.pallas_call(
            pieces_kernel,
            in_specs=[pl.BlockSpec(memory_space=pltpu.SMEM)]
            + [pl.BlockSpec((frame_rows, width), lambda i: (0, 0))] * peers
            + weight_specs,
            scratch_shapes=[act_scratch, pltpu.VMEM((whole_rows, width), BF)],
            **spatial_out,
        )(where_am_i, *pieces, w_flat, taps_s)

    row_block = 256
    point_call = pl.pallas_call(
        point_kernel,
        out_shape=[jax.ShapeDtypeStruct((4, frame_rows, width), BF)] * 2,
        grid=(whole_rows // row_block,),
        in_specs=[pl.BlockSpec(memory_space=pltpu.SMEM)]
        + [pl.BlockSpec((row_block, 2 * chan), lambda i: (i, 0))] * 3
        + [
            pl.BlockSpec((TAPS, 2 * chan), lambda i: (0, 0)),
            pl.BlockSpec((chan, width), lambda i: (0, 0)),
            anywhere,
        ],
        out_specs=[pl.BlockSpec((4, frame_rows, width), lambda i: (0, 0, 0))] * 2,
        compiler_params=params(40),
    )

    blocks = lax.axis_size("blk")
    next_frames = [(i, i + 1) for i in range(blocks - 1)]
    other_core = [(i, i ^ 1) for i in range(peers)]
    ahead = [[(i, (i + 2 * k) % peers) for i in range(peers)] for k in range(4)]

    late_along = [late] + [lax.ppermute(late, "tile", ahead[k]) for k in (1, 2, 3)]
    before_early = lax.ppermute(early, "blk", next_frames)
    pieces = []
    for part in late_along:
        pieces += [part, lax.ppermute(part, "tile", other_core)]
    stacked = pl.pallas_call(
        stack_kernel,
        out_shape=jax.ShapeDtypeStruct((2, frame_rows, width), BF),
        in_specs=[VMEM, VMEM] + [anywhere] * 3,
        out_specs=VMEM,
        compiler_params=params(20),
    )(early, before_early, *late_along[1:])
    whole = lax.all_gather(stacked, "tile", axis=0)
    late_sp = pieces_call(pieces)
    before_late_sp = lax.ppermute(late_sp, "blk", next_frames)
    early_sp = spatial_call(whole, 0, late_sp)

    def core_shares(now, one, two, needed):
        mine, other = point_call(where_am_i, now, one, two, taps_t, w_down, needed)
        return mine, lax.ppermute(other, "tile", other_core)

    def sums(mine, from_core, rows):
        kept, *sends = pl.pallas_call(
            sum_kernel,
            out_shape=[jax.ShapeDtypeStruct((frame_rows, width), F32)] + [one_frame] * 3,
            in_specs=[VMEM] * 3,
            out_specs=[VMEM] * 4,
            compiler_params=params(20),
        )(mine, from_core, rows)
        return kept, [lax.ppermute(part, "tile", ahead[k + 1]) for k, part in enumerate(sends)]

    late_shares = core_shares(late_sp, early_sp, before_late_sp, early_sp)
    before_early_sp = spatial_call(whole, 1, late_shares[0])
    late_kept, late_back = sums(*late_shares, late)
    early_shares = core_shares(early_sp, before_late_sp, before_early_sp, late_kept)
    early_kept, early_back = sums(*early_shares, early)
    return pl.pallas_call(
        final_kernel,
        out_shape=jax.ShapeDtypeStruct(stream_in.shape, BF),
        in_specs=[VMEM] * 8,
        out_specs=VMEM,
        compiler_params=params(20),
    )(early_kept, late_kept, *early_back, *late_back)


def solution(mesh):
    in_specs = (
        P("tile", "blk", None, None),
        P("tile", "blk", None, None),
        P("tile", "blk", None, None),
        P("tile", "blk", None, None),
        P("tile", None),
        P(None, None, "tile"),
        P("tile", None),
        P(None, None, None, "tile"),
        P(None, None, "tile"),
    )
    out_specs = P("tile", "blk", None, None)
    return jax.shard_map(
        on_device, mesh=mesh, in_specs=in_specs, out_specs=out_specs, check_vma=False
    )
```

```python
import functools

import jax
import jax.numpy as jnp
from jax import lax
from jax.experimental import pallas as pl
from jax.experimental.pallas import tpu as pltpu
from jax.sharding import PartitionSpec as P

HEADS = 20
HEAD_DIM = 112
D = 2240
TAPS = 3
EPS = 1e-6
LANES = 128
SLABS = 18
SUB = 14
PIECES = 256
BF = jnp.bfloat16
F32 = jnp.float32
MIB = 1 << 20


def slab_of(c):
    first = (LANES * c) // HEAD_DIM
    bound = HEAD_DIM * (first + 1) - LANES * c
    start = (HEAD_DIM * first) // LANES * LANES
    pair = 2 if first + 1 < HEADS else 1
    stop = min(-(-(HEAD_DIM * (first + pair)) // LANES) * LANES, D)
    return first, pair, bound, start, stop, HEAD_DIM * first - start


def kv_kernel(k_ref, v_ref, out_ref, last_ref):
    tokens = k_ref.shape[0]
    key_pos = jnp.maximum(k_ref[...], 0)
    last_ref[...] = jnp.ones((tokens, LANES), BF)
    last_ref[:, : D - LANES * (SLABS - 1)] = v_ref[:, LANES * (SLABS - 1) :]
    lane = lax.broadcasted_iota(jnp.int32, (HEAD_DIM, LANES), 1)
    over_tokens = (((0,), (0,)), ((), ()))
    for c in range(SLABS):
        first, pair, bound, start, stop, offset = slab_of(c)
        values = last_ref[...] if c == SLABS - 1 else v_ref[:, LANES * c : LANES * (c + 1)]
        product = lax.dot_general(
            key_pos[:, start:stop], values, over_tokens, preferred_element_type=F32
        )
        tile = product[offset : offset + HEAD_DIM]
        if pair == 2:
            tile = jnp.where(lane < bound, tile, product[offset + HEAD_DIM : offset + 2 * HEAD_DIM])
        if c == SLABS - 1:
            sums = lax.dot_general(
                key_pos, jnp.ones((tokens, LANES), BF), over_tokens, preferred_element_type=F32
            )
            tile = jnp.where(lane < bound, tile, 0.0)
            for h in range(HEADS):
                tile = jnp.where(
                    lane == bound + h, sums[HEAD_DIM * h : HEAD_DIM * (h + 1)], tile
                )
        out_ref[SUB * c : SUB * (c + 1)] = tile.reshape(SUB, 8, LANES).astype(BF)
    rest = PIECES - SUB * SLABS
    out_ref[SUB * SLABS :] = jnp.zeros((rest, 8, LANES), BF)


def prefix_kernel(in_ref, out_ref):
    per_block = 16

    def block(b, total):
        here = in_ref[pl.ds(b * per_block, per_block)].astype(F32)
        total = total + jnp.sum(here, axis=0)
        out_ref[pl.ds(b * per_block, per_block)] = jnp.broadcast_to(
            total.astype(BF)[None], (per_block, 8, LANES)
        )
        return total

    lax.fori_loop(0, PIECES // per_block, block, jnp.zeros((8, LANES), F32))


def attend_kernel(q_ref, state_ref, att_ref):
    query_pos = jnp.maximum(q_ref[...], 0)
    lane = lax.broadcasted_iota(jnp.int32, (HEAD_DIM, LANES), 1)
    tile_of = lambda c: state_ref[SUB * c : SUB * (c + 1)].astype(F32).reshape(HEAD_DIM, LANES)
    sums = tile_of(SLABS - 1)
    z_lane = D - LANES * (SLABS - 1)
    for c in range(SLABS):
        first, pair, bound, start, stop, offset = slab_of(c)
        tile = tile_of(c)
        weights = []
        for which in range(2):
            rows = []
            if offset > 0:
                rows.append(jnp.zeros((offset, LANES), F32))
            for k in range(pair):
                if which == 0:
                    part = tile
                else:
                    h = z_lane + first + k
                    part = jnp.broadcast_to(sums[:, h : h + 1], (HEAD_DIM, LANES))
                inside = (lane < bound) if k == 0 else (lane >= bound)
                rows.append(jnp.where(inside, part, 0.0))
            left = stop - start - offset - pair * HEAD_DIM
            if left > 0:
                rows.append(jnp.zeros((left, LANES), F32))
            weights.append(jnp.concatenate(rows, axis=0))
        weight = jnp.concatenate(weights, axis=1).astype(BF)
        both = jnp.dot(query_pos[:, start:stop], weight, preferred_element_type=F32)
        attended = (both[:, :LANES] / (both[:, LANES:] + EPS)).astype(BF)
        width = min(LANES, D - LANES * c)
        att_ref[:, LANES * c : LANES * c + width] = attended[:, :width]


def hidden_kernel(att_ref, stream_ref, w_hbm, needed_ref, early_ref, late_ref, w_ref, sems):
    tokens = att_ref.shape[0]
    step = 384
    spans = [(n, min(n + step, D)) for n in range(0, D, step)]
    copies = []
    for i, (n, stop) in enumerate(spans):
        span = pl.ds(n, stop - n)
        copies.append(pltpu.make_async_copy(w_hbm.at[:, span], w_ref.at[:, span], sems.at[i]))
    for copy in copies:
        copy.start()
    for copy, (n, stop) in zip(copies, spans):
        cols = slice(n, stop)
        copy.wait()
        out = jnp.dot(att_ref[...], w_ref[:, cols], preferred_element_type=F32)
        out = (out + stream_ref[:, cols].astype(F32)).astype(BF)
        for r in range(tokens // 32):
            rows = slice(16 * r, 16 * r + 16)
            early_ref[rows, cols] = out[32 * r : 32 * r + 16]
            late_ref[rows, cols] = out[32 * r + 16 : 32 * r + 32]


def depthwise(hid, w_ref, taps_ref, out_ref, act_ref):
    tokens, cols = hid.shape[0], 16
    width = w_ref.shape[1]
    product = jnp.dot(hid, w_ref[...], preferred_element_type=F32)
    act = (product * jax.nn.sigmoid(product)).astype(BF).astype(F32)
    act_ref[:cols] = jnp.zeros((cols, width), F32)
    act_ref[cols + tokens :] = jnp.zeros((cols, width), F32)
    act_ref[cols : cols + tokens] = act
    taps = taps_ref[...]
    chunk = 32
    col = lax.broadcasted_iota(jnp.int32, (chunk, width), 0) % cols
    for r in range(0, tokens, chunk):
        near = [act_ref[r + cols * a : r + cols * a + chunk] for a in range(3)]
        left, mid, right = (
            near[0] * taps[b : b + 1] + near[1] * taps[3 + b : 4 + b] + near[2] * taps[6 + b : 7 + b]
            for b in range(3)
        )
        left = jnp.where(col == 0, 0.0, pltpu.roll(left, 1, 0))
        right = jnp.where(col == cols - 1, 0.0, pltpu.roll(right, chunk - 1, 0))
        out_ref[r : r + chunk] = (left + mid + right).astype(BF)


def pieces_kernel(place_ref, *refs):
    peers = 8
    pieces, (w_ref, taps_ref, _, out_ref, act_ref, hid_ref) = refs[:peers], refs[peers:]
    rows = pieces[0].shape[0]

    @pl.when(pl.program_id(0) == 0)
    def _():
        for p, piece in enumerate(pieces):
            source = 2 * ((place_ref[0] + 4 - p // 2) % 4) + (place_ref[1] + p % 2) % 2
            hid_ref[pl.ds(pl.multiple_of(source * rows, rows), rows)] = piece[...]

    depthwise(hid_ref[...], w_ref, taps_ref, out_ref, act_ref)


def point_kernel(
    place_ref, now_ref, one_ref, two_ref, taps_ref, w_ref, needed_ref, mine_ref, other_ref
):
    half = w_ref.shape[0]
    taps = taps_ref[...]
    mix = now_ref[...].astype(F32) * taps[0:1]
    mix = mix + one_ref[...].astype(F32) * taps[1:2]
    mix = mix + two_ref[...].astype(F32) * taps[2:3]
    gate = mix[:, half:]
    gated = (mix[:, :half] * (gate * jax.nn.sigmoid(gate))).astype(BF)
    out = jnp.dot(gated, w_ref[...], preferred_element_type=F32).astype(BF)
    y, core = place_ref[0], place_ref[1]
    i = pl.program_id(0)
    rows = out.shape[0] // 4
    for k in range(4):
        target = 4 * i + k
        slot = (target // 2 - y + 4) % 4

        @pl.when(core == k % 2)
        def _():
            mine_ref[slot] = out[rows * k : rows * (k + 1)]

        @pl.when(core != k % 2)
        def _():
            other_ref[slot] = out[rows * k : rows * (k + 1)]


def sum_kernel(mine_ref, other_ref, hidden_ref, kept_ref, *sends):
    total = lambda k: mine_ref[k].astype(F32) + other_ref[k].astype(F32)
    kept_ref[...] = hidden_ref[...].astype(F32) + total(0)
    for k, send in enumerate(sends):
        send[...] = total(k + 1).astype(BF)


def stack_kernel(*refs):
    one_ref, two_ref, out_ref = refs[-3:]
    out_ref[0] = one_ref[...]
    out_ref[1] = two_ref[...]


def final_kernel(early_ref, late_ref, *refs):
    pieces, out_ref = refs[:6], refs[6]
    for f, kept in enumerate((early_ref, late_ref)):
        total = kept[...]
        for piece in pieces[3 * f : 3 * f + 3]:
            total = total + piece[...].astype(F32)
        out = total.astype(BF)
        for r in range(out_ref.shape[0]):
            out_ref[r, f] = out[16 * r : 16 * r + 16]


def params(mib):
    return pltpu.CompilerParams(vmem_limit_bytes=mib * MIB)


VMEM = pl.BlockSpec(memory_space=pltpu.VMEM)


def on_device(
    stream_in, queries, key_rows, value_rows, w_output, w_inner, w_down, spatial_taps, temporal_taps
):
    row_count, frames, col_count, width = queries.shape
    tokens = row_count * frames * col_count
    flat = lambda a: a.reshape(tokens, width)
    chan = w_inner.shape[2]
    peers = lax.axis_size("tile")
    place = lax.axis_index("tile")
    where_am_i = jnp.stack([place // 2, place % 2]).astype(jnp.int32)

    w_out_whole = lax.all_gather(w_output, "tile", axis=0, tiled=True)
    w_flat = w_inner.reshape(width, 2 * chan)
    taps_s = spatial_taps.reshape(9, 2 * chan)
    taps_t = temporal_taps.reshape(TAPS, 2 * chan)

    pieces = jax.ShapeDtypeStruct((PIECES, 8, LANES), BF)
    parts = pl.pallas_call(
        kv_kernel,
        out_shape=pieces,
        in_specs=[VMEM] * 2,
        out_specs=VMEM,
        scratch_shapes=[pltpu.VMEM((tokens, LANES), BF)],
        compiler_params=params(40),
    )(flat(key_rows), flat(value_rows))
    everyone = ("blk", "tile")
    parts = lax.all_to_all(parts, everyone, 0, 0, tiled=True)
    sums = pl.pallas_call(
        prefix_kernel, out_shape=pieces, in_specs=[VMEM], out_specs=VMEM, compiler_params=params(40)
    )(parts)
    state = lax.all_to_all(sums, everyone, 0, 0, tiled=True)

    anywhere = pl.BlockSpec(memory_space=pl.ANY)
    frame_rows = row_count * col_count
    attended = pl.pallas_call(
        attend_kernel,
        out_shape=jax.ShapeDtypeStruct((tokens, width), BF),
        in_specs=[VMEM, VMEM],
        out_specs=VMEM,
        compiler_params=params(40),
    )(flat(queries), state)
    one_frame = jax.ShapeDtypeStruct((frame_rows, width), BF)
    early, late = pl.pallas_call(
        hidden_kernel,
        out_shape=[one_frame] * 2,
        in_specs=[VMEM, VMEM, anywhere, anywhere],
        out_specs=[VMEM, VMEM],
        scratch_shapes=[pltpu.VMEM((width, width), BF), pltpu.SemaphoreType.DMA((6,))],
        compiler_params=params(52),
    )(attended, flat(stream_in), w_out_whole, w_flat)

    whole_rows = peers * frame_rows
    block = 256

    spatial_out = dict(
        out_shape=jax.ShapeDtypeStruct((whole_rows, 2 * chan), BF),
        grid=(2 * chan // block,),
        out_specs=pl.BlockSpec((whole_rows, block), lambda i: (0, i)),
        compiler_params=params(52),
    )
    weight_specs = [
        pl.BlockSpec((width, block), lambda i: (0, i)),
        pl.BlockSpec((9, block), lambda i: (0, i)),
    ]
    act_scratch = pltpu.VMEM((whole_rows + 2 * col_count, block), F32)

    def pieces_call(pieces, f, needed):
        return pl.pallas_call(
            pieces_kernel,
            in_specs=[pl.BlockSpec(memory_space=pltpu.SMEM)]
            + [pl.BlockSpec((None, frame_rows, width), lambda i: (f, 0, 0))] * peers
            + weight_specs
            + [anywhere],
            scratch_shapes=[act_scratch, pltpu.VMEM((whole_rows, width), BF)],
            **spatial_out,
        )(where_am_i, *pieces, w_flat, taps_s, needed)

    row_block = 256
    point_call = pl.pallas_call(
        point_kernel,
        out_shape=[jax.ShapeDtypeStruct((4, frame_rows, width), BF)] * 2,
        grid=(whole_rows // row_block,),
        in_specs=[pl.BlockSpec(memory_space=pltpu.SMEM)]
        + [pl.BlockSpec((row_block, 2 * chan), lambda i: (i, 0))] * 3
        + [
            pl.BlockSpec((TAPS, 2 * chan), lambda i: (0, 0)),
            pl.BlockSpec((chan, width), lambda i: (0, 0)),
            anywhere,
        ],
        out_specs=[pl.BlockSpec((4, frame_rows, width), lambda i: (0, 0, 0))] * 2,
        compiler_params=params(40),
    )

    blocks = lax.axis_size("blk")
    next_frames = [(i, i + 1) for i in range(blocks - 1)]
    other_core = [(i, i ^ 1) for i in range(peers)]
    ahead = [[(i, (i + 2 * k) % peers) for i in range(peers)] for k in range(4)]

    def along_of(rows):
        return [rows] + [lax.ppermute(rows, "tile", ahead[k]) for k in (1, 2, 3)]

    late_along = along_of(late[None])
    before_early = lax.ppermute(early, "blk", next_frames)
    others = pl.pallas_call(
        stack_kernel,
        out_shape=jax.ShapeDtypeStruct((2, frame_rows, width), BF),
        in_specs=[anywhere] * 3 + [VMEM] * 2,
        out_specs=VMEM,
        compiler_params=params(20),
    )(*late_along[1:], early, before_early)
    others_along = along_of(others)
    pieces = []
    for part in late_along:
        pieces += [part, lax.ppermute(part, "tile", other_core)]
    late_sp = pieces_call(pieces, 0, taps_t)
    before_late_sp = lax.ppermute(late_sp, "blk", next_frames)
    both = []
    for part in others_along:
        both += [part, lax.ppermute(part, "tile", other_core)]
    early_sp = pieces_call(both, 0, late_sp)
    before_early_sp = pieces_call(both, 1, early_sp)

    def core_shares(now, one, two, needed):
        mine, other = point_call(where_am_i, now, one, two, taps_t, w_down, needed)
        return mine, lax.ppermute(other, "tile", other_core)

    def sums(mine, from_core, rows):
        kept, *sends = pl.pallas_call(
            sum_kernel,
            out_shape=[jax.ShapeDtypeStruct((frame_rows, width), F32)] + [one_frame] * 3,
            in_specs=[VMEM] * 3,
            out_specs=[VMEM] * 4,
            compiler_params=params(20),
        )(mine, from_core, rows)
        return kept, [lax.ppermute(part, "tile", ahead[k + 1]) for k, part in enumerate(sends)]

    late_shares = core_shares(late_sp, early_sp, before_late_sp, before_early_sp)
    late_kept, late_back = sums(*late_shares, late)
    early_shares = core_shares(early_sp, before_late_sp, before_early_sp, late_shares[0])
    early_kept, early_back = sums(*early_shares, early)
    return pl.pallas_call(
        final_kernel,
        out_shape=jax.ShapeDtypeStruct(stream_in.shape, BF),
        in_specs=[VMEM] * 8,
        out_specs=VMEM,
        compiler_params=params(20),
    )(early_kept, late_kept, *early_back, *late_back)


def solution(mesh):
    in_specs = (
        P("tile", "blk", None, None),
        P("tile", "blk", None, None),
        P("tile", "blk", None, None),
        P("tile", "blk", None, None),
        P("tile", None),
        P(None, None, "tile"),
        P("tile", None),
        P(None, None, None, "tile"),
        P(None, None, "tile"),
    )
    out_specs = P("tile", "blk", None, None)
    return jax.shard_map(
        on_device, mesh=mesh, in_specs=in_specs, out_specs=out_specs, check_vma=False
    )
```

```python
import functools

import jax
import jax.numpy as jnp
from jax import lax
from jax.experimental import pallas as pl
from jax.experimental.pallas import tpu as pltpu
from jax.sharding import PartitionSpec as P

HEADS = 20
HEAD_DIM = 112
D = 2240
TAPS = 3
EPS = 1e-6
LANES = 128
SLABS = 18
SUB = 14
PIECES = 256
BF = jnp.bfloat16
F32 = jnp.float32
MIB = 1 << 20


def slab_of(c):
    first = (LANES * c) // HEAD_DIM
    bound = HEAD_DIM * (first + 1) - LANES * c
    start = (HEAD_DIM * first) // LANES * LANES
    pair = 2 if first + 1 < HEADS else 1
    stop = min(-(-(HEAD_DIM * (first + pair)) // LANES) * LANES, D)
    return first, pair, bound, start, stop, HEAD_DIM * first - start


def kv_kernel(k_ref, v_ref, out_ref, last_ref):
    tokens = k_ref.shape[0]
    key_pos = jnp.maximum(k_ref[...], 0)
    last_ref[...] = jnp.ones((tokens, LANES), BF)
    last_ref[:, : D - LANES * (SLABS - 1)] = v_ref[:, LANES * (SLABS - 1) :]
    lane = lax.broadcasted_iota(jnp.int32, (HEAD_DIM, LANES), 1)
    over_tokens = (((0,), (0,)), ((), ()))
    for c in range(SLABS):
        first, pair, bound, start, stop, offset = slab_of(c)
        values = last_ref[...] if c == SLABS - 1 else v_ref[:, LANES * c : LANES * (c + 1)]
        product = lax.dot_general(
            key_pos[:, start:stop], values, over_tokens, preferred_element_type=F32
        )
        tile = product[offset : offset + HEAD_DIM]
        if pair == 2:
            tile = jnp.where(lane < bound, tile, product[offset + HEAD_DIM : offset + 2 * HEAD_DIM])
        if c == SLABS - 1:
            sums = lax.dot_general(
                key_pos, jnp.ones((tokens, LANES), BF), over_tokens, preferred_element_type=F32
            )
            tile = jnp.where(lane < bound, tile, 0.0)
            for h in range(HEADS):
                tile = jnp.where(
                    lane == bound + h, sums[HEAD_DIM * h : HEAD_DIM * (h + 1)], tile
                )
        out_ref[SUB * c : SUB * (c + 1)] = tile.reshape(SUB, 8, LANES).astype(BF)
    rest = PIECES - SUB * SLABS
    out_ref[SUB * SLABS :] = jnp.zeros((rest, 8, LANES), BF)


def prefix_kernel(in_ref, out_ref):
    per_block = 16

    def block(b, total):
        here = in_ref[pl.ds(b * per_block, per_block)].astype(F32)
        total = total + jnp.sum(here, axis=0)
        out_ref[pl.ds(b * per_block, per_block)] = jnp.broadcast_to(
            total.astype(BF)[None], (per_block, 8, LANES)
        )
        return total

    lax.fori_loop(0, PIECES // per_block, block, jnp.zeros((8, LANES), F32))


def attend_kernel(q_ref, state_ref, att_ref):
    query_pos = jnp.maximum(q_ref[...], 0)
    lane = lax.broadcasted_iota(jnp.int32, (HEAD_DIM, LANES), 1)
    tile_of = lambda c: state_ref[SUB * c : SUB * (c + 1)].astype(F32).reshape(HEAD_DIM, LANES)
    sums = tile_of(SLABS - 1)
    z_lane = D - LANES * (SLABS - 1)
    for c in range(SLABS):
        first, pair, bound, start, stop, offset = slab_of(c)
        tile = tile_of(c)
        weights = []
        for which in range(2):
            rows = []
            if offset > 0:
                rows.append(jnp.zeros((offset, LANES), F32))
            for k in range(pair):
                if which == 0:
                    part = tile
                else:
                    h = z_lane + first + k
                    part = jnp.broadcast_to(sums[:, h : h + 1], (HEAD_DIM, LANES))
                inside = (lane < bound) if k == 0 else (lane >= bound)
                rows.append(jnp.where(inside, part, 0.0))
            left = stop - start - offset - pair * HEAD_DIM
            if left > 0:
                rows.append(jnp.zeros((left, LANES), F32))
            weights.append(jnp.concatenate(rows, axis=0))
        weight = jnp.concatenate(weights, axis=1).astype(BF)
        both = jnp.dot(query_pos[:, start:stop], weight, preferred_element_type=F32)
        attended = (both[:, :LANES] / (both[:, LANES:] + EPS)).astype(BF)
        width = min(LANES, D - LANES * c)
        att_ref[:, LANES * c : LANES * c + width] = attended[:, :width]


def hidden_kernel(att_ref, stream_ref, w_hbm, needed_ref, early_ref, late_ref, w_ref, sems):
    tokens = att_ref.shape[0]
    step = 384
    spans = [(n, min(n + step, D)) for n in range(0, D, step)]
    copies = []
    for i, (n, stop) in enumerate(spans):
        span = pl.ds(n, stop - n)
        copies.append(pltpu.make_async_copy(w_hbm.at[:, span], w_ref.at[:, span], sems.at[i]))
    for copy in copies:
        copy.start()
    for copy, (n, stop) in zip(copies, spans):
        cols = slice(n, stop)
        copy.wait()
        out = jnp.dot(att_ref[...], w_ref[:, cols], preferred_element_type=F32)
        out = (out + stream_ref[:, cols].astype(F32)).astype(BF)
        for r in range(tokens // 32):
            rows = slice(16 * r, 16 * r + 16)
            early_ref[rows, cols] = out[32 * r : 32 * r + 16]
            late_ref[rows, cols] = out[32 * r + 16 : 32 * r + 32]


def depthwise(hid, w_ref, taps_ref, out_ref, act_ref):
    tokens, cols = hid.shape[0], 16
    width = w_ref.shape[1]
    product = jnp.dot(hid, w_ref[...], preferred_element_type=F32)
    act = (product * jax.nn.sigmoid(product)).astype(BF).astype(F32)
    act_ref[:cols] = jnp.zeros((cols, width), F32)
    act_ref[cols + tokens :] = jnp.zeros((cols, width), F32)
    act_ref[cols : cols + tokens] = act
    taps = taps_ref[...]
    chunk = 32
    col = lax.broadcasted_iota(jnp.int32, (chunk, width), 0) % cols
    for r in range(0, tokens, chunk):
        near = [act_ref[r + cols * a : r + cols * a + chunk] for a in range(3)]
        left, mid, right = (
            near[0] * taps[b : b + 1] + near[1] * taps[3 + b : 4 + b] + near[2] * taps[6 + b : 7 + b]
            for b in range(3)
        )
        left = jnp.where(col == 0, 0.0, pltpu.roll(left, 1, 0))
        right = jnp.where(col == cols - 1, 0.0, pltpu.roll(right, chunk - 1, 0))
        out_ref[r : r + chunk] = (left + mid + right).astype(BF)


def pieces_kernel(place_ref, *refs):
    peers = 8
    pieces, (w_ref, taps_ref, _, out_ref, act_ref, hid_ref) = refs[:peers], refs[peers:]
    rows = pieces[0].shape[0]

    @pl.when(pl.program_id(0) == 0)
    def _():
        for p, piece in enumerate(pieces):
            source = 2 * ((place_ref[0] + 4 - p // 2) % 4) + (place_ref[1] + p % 2) % 2
            hid_ref[pl.ds(pl.multiple_of(source * rows, rows), rows)] = piece[...]

    depthwise(hid_ref[...], w_ref, taps_ref, out_ref, act_ref)


def both_kernel(place_ref, *refs):
    peers, frames = 8, 2
    pieces = refs[:peers]
    w_ref, taps_ref, _, one_ref, two_ref, act_ref, hid_ref = refs[peers:]
    rows = pieces[0].shape[1]

    @pl.when(pl.program_id(0) == 0)
    def _():
        for p, piece in enumerate(pieces):
            source = 2 * ((place_ref[0] + 4 - p // 2) % 4) + (place_ref[1] + p % 2) % 2
            target = pl.ds(pl.multiple_of(source * rows, rows), rows)
            for f in range(frames):
                hid_ref[f, target] = piece[f]

    for f, out_ref in enumerate((one_ref, two_ref)):
        depthwise(hid_ref[f], w_ref, taps_ref, out_ref, act_ref.at[f])


def point_kernel(
    place_ref,
    now_ref,
    one_ref,
    two_ref,
    taps_ref,
    w_hbm,
    needed_ref,
    mine_ref,
    other_ref,
    w_ref,
    sem,
):
    half = w_ref.shape[0]
    copy = pltpu.make_async_copy(w_hbm, w_ref, sem)

    @pl.when(pl.program_id(0) == 0)
    def _():
        copy.start()

    taps = taps_ref[...]
    mix = now_ref[...].astype(F32) * taps[0:1]
    mix = mix + one_ref[...].astype(F32) * taps[1:2]
    mix = mix + two_ref[...].astype(F32) * taps[2:3]
    gate = mix[:, half:]
    gated = (mix[:, :half] * (gate * jax.nn.sigmoid(gate))).astype(BF)

    @pl.when(pl.program_id(0) == 0)
    def _():
        copy.wait()

    out = jnp.dot(gated, w_ref[...], preferred_element_type=F32).astype(BF)
    y, core = place_ref[0], place_ref[1]
    i = pl.program_id(0)
    rows = out.shape[0] // 4
    for k in range(4):
        target = 4 * i + k
        slot = (target // 2 - y + 4) % 4

        @pl.when(core == k % 2)
        def _():
            mine_ref[slot] = out[rows * k : rows * (k + 1)]

        @pl.when(core != k % 2)
        def _():
            other_ref[slot] = out[rows * k : rows * (k + 1)]


def sum_kernel(mine_ref, other_ref, hidden_ref, kept_ref, *sends):
    total = lambda k: mine_ref[k].astype(F32) + other_ref[k].astype(F32)
    kept_ref[...] = hidden_ref[...].astype(F32) + total(0)
    for k, send in enumerate(sends):
        send[...] = total(k + 1).astype(BF)


def stack_kernel(*refs):
    one_ref, two_ref, out_ref = refs[-3:]
    out_ref[0] = one_ref[...]
    out_ref[1] = two_ref[...]


def final_kernel(early_ref, late_ref, *refs):
    pieces, out_ref = refs[:6], refs[6]
    for f, kept in enumerate((early_ref, late_ref)):
        total = kept[...]
        for piece in pieces[3 * f : 3 * f + 3]:
            total = total + piece[...].astype(F32)
        out = total.astype(BF)
        for r in range(out_ref.shape[0]):
            out_ref[r, f] = out[16 * r : 16 * r + 16]


def params(mib):
    return pltpu.CompilerParams(vmem_limit_bytes=mib * MIB)


VMEM = pl.BlockSpec(memory_space=pltpu.VMEM)


def on_device(
    stream_in, queries, key_rows, value_rows, w_output, w_inner, w_down, spatial_taps, temporal_taps
):
    row_count, frames, col_count, width = queries.shape
    tokens = row_count * frames * col_count
    flat = lambda a: a.reshape(tokens, width)
    chan = w_inner.shape[2]
    peers = lax.axis_size("tile")
    place = lax.axis_index("tile")
    where_am_i = jnp.stack([place // 2, place % 2]).astype(jnp.int32)

    w_out_whole = lax.all_gather(w_output, "tile", axis=0, tiled=True)
    w_flat = w_inner.reshape(width, 2 * chan)
    taps_s = spatial_taps.reshape(9, 2 * chan)
    taps_t = temporal_taps.reshape(TAPS, 2 * chan)

    pieces = jax.ShapeDtypeStruct((PIECES, 8, LANES), BF)
    parts = pl.pallas_call(
        kv_kernel,
        out_shape=pieces,
        in_specs=[VMEM] * 2,
        out_specs=VMEM,
        scratch_shapes=[pltpu.VMEM((tokens, LANES), BF)],
        compiler_params=params(40),
    )(flat(key_rows), flat(value_rows))
    everyone = ("blk", "tile")
    parts = lax.all_to_all(parts, everyone, 0, 0, tiled=True)
    sums = pl.pallas_call(
        prefix_kernel, out_shape=pieces, in_specs=[VMEM], out_specs=VMEM, compiler_params=params(40)
    )(parts)
    state = lax.all_to_all(sums, everyone, 0, 0, tiled=True)

    anywhere = pl.BlockSpec(memory_space=pl.ANY)
    frame_rows = row_count * col_count
    attended = pl.pallas_call(
        attend_kernel,
        out_shape=jax.ShapeDtypeStruct((tokens, width), BF),
        in_specs=[VMEM, VMEM],
        out_specs=VMEM,
        compiler_params=params(40),
    )(flat(queries), state)
    one_frame = jax.ShapeDtypeStruct((frame_rows, width), BF)
    early, late = pl.pallas_call(
        hidden_kernel,
        out_shape=[one_frame] * 2,
        in_specs=[VMEM, VMEM, anywhere, anywhere],
        out_specs=[VMEM, VMEM],
        scratch_shapes=[pltpu.VMEM((width, width), BF), pltpu.SemaphoreType.DMA((6,))],
        compiler_params=params(52),
    )(attended, flat(stream_in), w_out_whole, w_flat)

    whole_rows = peers * frame_rows
    block = 256

    spatial_out = jax.ShapeDtypeStruct((whole_rows, 2 * chan), BF)
    weight_specs = [
        pl.BlockSpec((width, block), lambda i: (0, i)),
        pl.BlockSpec((9, block), lambda i: (0, i)),
    ]

    def pieces_call(kernel, frames, pieces, needed):
        outs = 1 if frames is None else frames
        lead = () if frames is None else (frames,)
        return pl.pallas_call(
            kernel,
            out_shape=[spatial_out] * outs,
            grid=(2 * chan // block,),
            in_specs=[pl.BlockSpec(memory_space=pltpu.SMEM)]
            + [pl.BlockSpec(part.shape, lambda i, n=part.ndim: (0,) * n) for part in pieces]
            + weight_specs
            + [anywhere],
            out_specs=[pl.BlockSpec((whole_rows, block), lambda i: (0, i))] * outs,
            scratch_shapes=[
                pltpu.VMEM(lead + (whole_rows + 2 * col_count, block), F32),
                pltpu.VMEM(lead + (whole_rows, width), BF),
            ],
            compiler_params=params(52),
        )(where_am_i, *pieces, w_flat, taps_s, needed)

    row_block = 256
    point_call = pl.pallas_call(
        point_kernel,
        out_shape=[jax.ShapeDtypeStruct((4, frame_rows, width), BF)] * 2,
        grid=(whole_rows // row_block,),
        in_specs=[pl.BlockSpec(memory_space=pltpu.SMEM)]
        + [pl.BlockSpec((row_block, 2 * chan), lambda i: (i, 0))] * 3
        + [
            pl.BlockSpec((TAPS, 2 * chan), lambda i: (0, 0)),
            anywhere,
            anywhere,
        ],
        out_specs=[pl.BlockSpec((4, frame_rows, width), lambda i: (0, 0, 0))] * 2,
        scratch_shapes=[pltpu.VMEM((chan, width), BF), pltpu.SemaphoreType.DMA],
        compiler_params=params(40),
    )

    w_down_far = pltpu.with_memory_space_constraint(w_down, pltpu.HBM)
    blocks = lax.axis_size("blk")
    next_frames = [(i, i + 1) for i in range(blocks - 1)]
    other_core = [(i, i ^ 1) for i in range(peers)]
    ahead = [[(i, (i + 2 * k) % peers) for i in range(peers)] for k in range(4)]

    def along_of(rows):
        return [rows] + [lax.ppermute(rows, "tile", ahead[k]) for k in (1, 2, 3)]

    late_along = along_of(late)
    before_early = lax.ppermute(early, "blk", next_frames)
    others = pl.pallas_call(
        stack_kernel,
        out_shape=jax.ShapeDtypeStruct((2, frame_rows, width), BF),
        in_specs=[anywhere] * 3 + [VMEM] * 2,
        out_specs=VMEM,
        compiler_params=params(20),
    )(*late_along[1:], early, before_early)
    others_along = along_of(others)
    pieces = []
    for part in late_along:
        pieces += [part, lax.ppermute(part, "tile", other_core)]
    (late_sp,) = pieces_call(pieces_kernel, None, pieces, taps_t)
    before_late_sp = lax.ppermute(late_sp, "blk", next_frames)
    both = []
    for part in others_along:
        both += [part, lax.ppermute(part, "tile", other_core)]
    early_sp, before_early_sp = pieces_call(both_kernel, 2, both, late_sp)

    def core_shares(now, one, two, needed):
        mine, other = point_call(
            where_am_i, now, one, two, taps_t, w_down_far, needed
        )
        return mine, lax.ppermute(other, "tile", other_core)

    def sums(mine, from_core, rows):
        kept, *sends = pl.pallas_call(
            sum_kernel,
            out_shape=[jax.ShapeDtypeStruct((frame_rows, width), F32)] + [one_frame] * 3,
            in_specs=[VMEM] * 3,
            out_specs=[VMEM] * 4,
            compiler_params=params(20),
        )(mine, from_core, rows)
        return kept, [lax.ppermute(part, "tile", ahead[k + 1]) for k, part in enumerate(sends)]

    late_shares = core_shares(late_sp, early_sp, before_late_sp, before_early_sp)
    late_kept, late_back = sums(*late_shares, late)
    early_shares = core_shares(early_sp, before_late_sp, before_early_sp, late_shares[0])
    early_kept, early_back = sums(*early_shares, early)
    return pl.pallas_call(
        final_kernel,
        out_shape=jax.ShapeDtypeStruct(stream_in.shape, BF),
        in_specs=[VMEM] * 8,
        out_specs=VMEM,
        compiler_params=params(20),
    )(early_kept, late_kept, *early_back, *late_back)


def solution(mesh):
    in_specs = (
        P("tile", "blk", None, None),
        P("tile", "blk", None, None),
        P("tile", "blk", None, None),
        P("tile", "blk", None, None),
        P("tile", None),
        P(None, None, "tile"),
        P("tile", None),
        P(None, None, None, "tile"),
        P(None, None, "tile"),
    )
    out_specs = P("tile", "blk", None, None)
    return jax.shard_map(
        on_device, mesh=mesh, in_specs=in_specs, out_specs=out_specs, check_vma=False
    )
```

```python
import functools

import jax
import jax.numpy as jnp
from jax import lax
from jax.experimental import pallas as pl
from jax.experimental.pallas import tpu as pltpu
from jax.sharding import PartitionSpec as P

HEADS = 20
HEAD_DIM = 112
D = 2240
TAPS = 3
EPS = 1e-6
LANES = 128
SLABS = 18
SUB = 14
PIECES = 256
BF = jnp.bfloat16
F32 = jnp.float32
MIB = 1 << 20


def slab_of(c):
    first = (LANES * c) // HEAD_DIM
    bound = HEAD_DIM * (first + 1) - LANES * c
    start = (HEAD_DIM * first) // LANES * LANES
    pair = 2 if first + 1 < HEADS else 1
    stop = min(-(-(HEAD_DIM * (first + pair)) // LANES) * LANES, D)
    return first, pair, bound, start, stop, HEAD_DIM * first - start


def kv_kernel(k_ref, v_ref, out_ref, last_ref):
    tokens = k_ref.shape[0]
    key_pos = jnp.maximum(k_ref[...], 0)
    last_ref[...] = jnp.ones((tokens, LANES), BF)
    last_ref[:, : D - LANES * (SLABS - 1)] = v_ref[:, LANES * (SLABS - 1) :]
    lane = lax.broadcasted_iota(jnp.int32, (HEAD_DIM, LANES), 1)
    over_tokens = (((0,), (0,)), ((), ()))
    for c in range(SLABS):
        first, pair, bound, start, stop, offset = slab_of(c)
        values = last_ref[...] if c == SLABS - 1 else v_ref[:, LANES * c : LANES * (c + 1)]
        product = lax.dot_general(
            key_pos[:, start:stop], values, over_tokens, preferred_element_type=F32
        )
        tile = product[offset : offset + HEAD_DIM]
        if pair == 2:
            tile = jnp.where(lane < bound, tile, product[offset + HEAD_DIM : offset + 2 * HEAD_DIM])
        if c == SLABS - 1:
            sums = lax.dot_general(
                key_pos, jnp.ones((tokens, LANES), BF), over_tokens, preferred_element_type=F32
            )
            tile = jnp.where(lane < bound, tile, 0.0)
            for h in range(HEADS):
                tile = jnp.where(
                    lane == bound + h, sums[HEAD_DIM * h : HEAD_DIM * (h + 1)], tile
                )
        out_ref[SUB * c : SUB * (c + 1)] = tile.reshape(SUB, 8, LANES).astype(BF)
    rest = PIECES - SUB * SLABS
    out_ref[SUB * SLABS :] = jnp.zeros((rest, 8, LANES), BF)


def prefix_kernel(in_ref, out_ref):
    per_block = 16

    def block(b, total):
        here = in_ref[pl.ds(b * per_block, per_block)].astype(F32)
        total = total + jnp.sum(here, axis=0)
        out_ref[pl.ds(b * per_block, per_block)] = jnp.broadcast_to(
            total.astype(BF)[None], (per_block, 8, LANES)
        )
        return total

    lax.fori_loop(0, PIECES // per_block, block, jnp.zeros((8, LANES), F32))


def attend_kernel(q_ref, state_ref, att_ref):
    query_pos = jnp.maximum(q_ref[...], 0)
    lane = lax.broadcasted_iota(jnp.int32, (HEAD_DIM, LANES), 1)
    tile_of = lambda c: state_ref[SUB * c : SUB * (c + 1)].astype(F32).reshape(HEAD_DIM, LANES)
    sums = tile_of(SLABS - 1)
    z_lane = D - LANES * (SLABS - 1)
    for c in range(SLABS):
        first, pair, bound, start, stop, offset = slab_of(c)
        tile = tile_of(c)
        weights = []
        for which in range(2):
            rows = []
            if offset > 0:
                rows.append(jnp.zeros((offset, LANES), F32))
            for k in range(pair):
                if which == 0:
                    part = tile
                else:
                    h = z_lane + first + k
                    part = jnp.broadcast_to(sums[:, h : h + 1], (HEAD_DIM, LANES))
                inside = (lane < bound) if k == 0 else (lane >= bound)
                rows.append(jnp.where(inside, part, 0.0))
            left = stop - start - offset - pair * HEAD_DIM
            if left > 0:
                rows.append(jnp.zeros((left, LANES), F32))
            weights.append(jnp.concatenate(rows, axis=0))
        weight = jnp.concatenate(weights, axis=1).astype(BF)
        both = jnp.dot(query_pos[:, start:stop], weight, preferred_element_type=F32)
        attended = (both[:, :LANES] / (both[:, LANES:] + EPS)).astype(BF)
        width = min(LANES, D - LANES * c)
        att_ref[:, LANES * c : LANES * c + width] = attended[:, :width]


def hidden_kernel(att_ref, stream_ref, w_hbm, needed_ref, early_ref, late_ref, w_ref, sems):
    tokens = att_ref.shape[0]
    step = 384
    spans = [(n, min(n + step, D)) for n in range(0, D, step)]
    copies = []
    for i, (n, stop) in enumerate(spans):
        span = pl.ds(n, stop - n)
        copies.append(pltpu.make_async_copy(w_hbm.at[:, span], w_ref.at[:, span], sems.at[i]))
    for copy in copies:
        copy.start()
    for copy, (n, stop) in zip(copies, spans):
        cols = slice(n, stop)
        copy.wait()
        out = jnp.dot(att_ref[...], w_ref[:, cols], preferred_element_type=F32)
        out = (out + stream_ref[:, cols].astype(F32)).astype(BF)
        for r in range(tokens // 32):
            rows = slice(16 * r, 16 * r + 16)
            early_ref[rows, cols] = out[32 * r : 32 * r + 16]
            late_ref[rows, cols] = out[32 * r + 16 : 32 * r + 32]


def depthwise(hid, w_ref, taps_ref, out_ref, act_ref):
    tokens, cols = hid.shape[0], 16
    width = w_ref.shape[1]
    product = jnp.dot(hid, w_ref[...], preferred_element_type=F32)
    act = (product * jax.nn.sigmoid(product)).astype(BF).astype(F32)
    act_ref[:cols] = jnp.zeros((cols, width), F32)
    act_ref[cols + tokens :] = jnp.zeros((cols, width), F32)
    act_ref[cols : cols + tokens] = act
    taps = taps_ref[...]
    chunk = 32
    col = lax.broadcasted_iota(jnp.int32, (chunk, width), 0) % cols
    for r in range(0, tokens, chunk):
        near = [act_ref[r + cols * a : r + cols * a + chunk] for a in range(3)]
        left, mid, right = (
            near[0] * taps[b : b + 1] + near[1] * taps[3 + b : 4 + b] + near[2] * taps[6 + b : 7 + b]
            for b in range(3)
        )
        left = jnp.where(col == 0, 0.0, pltpu.roll(left, 1, 0))
        right = jnp.where(col == cols - 1, 0.0, pltpu.roll(right, chunk - 1, 0))
        out_ref[r : r + chunk] = (left + mid + right).astype(BF)


def pieces_kernel(place_ref, *refs):
    peers = 8
    pieces, (w_ref, taps_ref, _, out_ref, act_ref, hid_ref) = refs[:peers], refs[peers:]
    rows = pieces[0].shape[0]

    @pl.when(pl.program_id(0) == 0)
    def _():
        for p, piece in enumerate(pieces):
            source = 2 * ((place_ref[0] + 4 - p // 2) % 4) + (place_ref[1] + p % 2) % 2
            hid_ref[pl.ds(pl.multiple_of(source * rows, rows), rows)] = piece[...]

    depthwise(hid_ref[...], w_ref, taps_ref, out_ref, act_ref)


def both_kernel(place_ref, *refs):
    peers, frames = 8, 2
    pieces = refs[:peers]
    w_ref, taps_ref, _, one_ref, two_ref, act_ref, hid_ref = refs[peers:]
    rows = pieces[0].shape[1]

    @pl.when(pl.program_id(0) == 0)
    def _():
        for p, piece in enumerate(pieces):
            source = 2 * ((place_ref[0] + 4 - p // 2) % 4) + (place_ref[1] + p % 2) % 2
            target = pl.ds(pl.multiple_of(source * rows, rows), rows)
            for f in range(frames):
                hid_ref[f, target] = piece[f]

    for f, out_ref in enumerate((one_ref, two_ref)):
        depthwise(hid_ref[f], w_ref, taps_ref, out_ref, act_ref.at[f])


def point_kernel(
    place_ref, now_ref, one_ref, two_ref, taps_ref, w_ref, needed_ref, mine_ref, other_ref
):
    half = w_ref.shape[1]
    taps = taps_ref[...]
    mix = now_ref[...].astype(F32) * taps[0:1]
    mix = mix + one_ref[...].astype(F32) * taps[1:2]
    mix = mix + two_ref[...].astype(F32) * taps[2:3]
    gate = mix[:, half:]
    gated = (mix[:, :half] * (gate * jax.nn.sigmoid(gate))).astype(BF)
    over_channels = (((1,), (1,)), ((), ()))
    out = lax.dot_general(gated, w_ref[...], over_channels, preferred_element_type=F32).astype(BF)
    y, core = place_ref[0], place_ref[1]
    i = pl.program_id(0)
    rows = out.shape[0] // 4
    for k in range(4):
        target = 4 * i + k
        slot = (target // 2 - y + 4) % 4

        @pl.when(core == k % 2)
        def _():
            mine_ref[slot] = out[rows * k : rows * (k + 1)]

        @pl.when(core != k % 2)
        def _():
            other_ref[slot] = out[rows * k : rows * (k + 1)]


def sum_kernel(mine_ref, other_ref, hidden_ref, kept_ref, *sends):
    total = lambda k: mine_ref[k].astype(F32) + other_ref[k].astype(F32)
    kept_ref[...] = hidden_ref[...].astype(F32) + total(0)
    for k, send in enumerate(sends):
        send[...] = total(k + 1).astype(BF)


def stack_kernel(*refs):
    one_ref, two_ref, out_ref = refs[-3:]
    out_ref[0] = one_ref[...]
    out_ref[1] = two_ref[...]


def final_kernel(early_ref, late_ref, *refs):
    pieces, out_ref = refs[:6], refs[6]
    for f, kept in enumerate((early_ref, late_ref)):
        total = kept[...]
        for piece in pieces[3 * f : 3 * f + 3]:
            total = total + piece[...].astype(F32)
        out = total.astype(BF)
        for r in range(out_ref.shape[0]):
            out_ref[r, f] = out[16 * r : 16 * r + 16]


def params(mib):
    return pltpu.CompilerParams(vmem_limit_bytes=mib * MIB)


VMEM = pl.BlockSpec(memory_space=pltpu.VMEM)


def on_device(
    stream_in, queries, key_rows, value_rows, w_output, w_inner, w_down, spatial_taps, temporal_taps
):
    row_count, frames, col_count, width = queries.shape
    tokens = row_count * frames * col_count
    flat = lambda a: a.reshape(tokens, width)
    chan = w_inner.shape[2]
    peers = lax.axis_size("tile")
    place = lax.axis_index("tile")
    where_am_i = jnp.stack([place // 2, place % 2]).astype(jnp.int32)

    w_out_whole = lax.all_gather(w_output, "tile", axis=0, tiled=True)
    w_flat = w_inner.reshape(width, 2 * chan)
    taps_s = spatial_taps.reshape(9, 2 * chan)
    taps_t = temporal_taps.reshape(TAPS, 2 * chan)

    pieces = jax.ShapeDtypeStruct((PIECES, 8, LANES), BF)
    parts = pl.pallas_call(
        kv_kernel,
        out_shape=pieces,
        in_specs=[VMEM] * 2,
        out_specs=VMEM,
        scratch_shapes=[pltpu.VMEM((tokens, LANES), BF)],
        compiler_params=params(40),
    )(flat(key_rows), flat(value_rows))
    everyone = ("blk", "tile")
    parts = lax.all_to_all(parts, everyone, 0, 0, tiled=True)
    sums = pl.pallas_call(
        prefix_kernel, out_shape=pieces, in_specs=[VMEM], out_specs=VMEM, compiler_params=params(40)
    )(parts)
    state = lax.all_to_all(sums, everyone, 0, 0, tiled=True)

    anywhere = pl.BlockSpec(memory_space=pl.ANY)
    frame_rows = row_count * col_count
    attended = pl.pallas_call(
        attend_kernel,
        out_shape=jax.ShapeDtypeStruct((tokens, width), BF),
        in_specs=[VMEM, VMEM],
        out_specs=VMEM,
        compiler_params=params(40),
    )(flat(queries), state)
    one_frame = jax.ShapeDtypeStruct((frame_rows, width), BF)
    early, late = pl.pallas_call(
        hidden_kernel,
        out_shape=[one_frame] * 2,
        in_specs=[VMEM, VMEM, anywhere, anywhere],
        out_specs=[VMEM, VMEM],
        scratch_shapes=[pltpu.VMEM((width, width), BF), pltpu.SemaphoreType.DMA((6,))],
        compiler_params=params(52),
    )(attended, flat(stream_in), w_out_whole, w_flat)

    whole_rows = peers * frame_rows
    block = 256

    spatial_out = jax.ShapeDtypeStruct((whole_rows, 2 * chan), BF)
    weight_specs = [
        pl.BlockSpec((width, block), lambda i: (0, i)),
        pl.BlockSpec((9, block), lambda i: (0, i)),
    ]

    def pieces_call(kernel, frames, pieces, needed):
        outs = 1 if frames is None else frames
        lead = () if frames is None else (frames,)
        return pl.pallas_call(
            kernel,
            out_shape=[spatial_out] * outs,
            grid=(2 * chan // block,),
            in_specs=[pl.BlockSpec(memory_space=pltpu.SMEM)]
            + [pl.BlockSpec(part.shape, lambda i, n=part.ndim: (0,) * n) for part in pieces]
            + weight_specs
            + [anywhere],
            out_specs=[pl.BlockSpec((whole_rows, block), lambda i: (0, i))] * outs,
            scratch_shapes=[
                pltpu.VMEM(lead + (whole_rows + 2 * col_count, block), F32),
                pltpu.VMEM(lead + (whole_rows, width), BF),
            ],
            compiler_params=params(52),
        )(where_am_i, *pieces, w_flat, taps_s, needed)

    row_block = 256
    point_call = pl.pallas_call(
        point_kernel,
        out_shape=[jax.ShapeDtypeStruct((4, frame_rows, width), BF)] * 2,
        grid=(whole_rows // row_block,),
        in_specs=[pl.BlockSpec(memory_space=pltpu.SMEM)]
        + [pl.BlockSpec((row_block, 2 * chan), lambda i: (i, 0))] * 3
        + [
            pl.BlockSpec((TAPS, 2 * chan), lambda i: (0, 0)),
            pl.BlockSpec((width, chan), lambda i: (0, 0)),
            anywhere,
        ],
        out_specs=[pl.BlockSpec((4, frame_rows, width), lambda i: (0, 0, 0))] * 2,
        compiler_params=params(40),
    )

    w_point = w_down.T
    blocks = lax.axis_size("blk")
    next_frames = [(i, i + 1) for i in range(blocks - 1)]
    other_core = [(i, i ^ 1) for i in range(peers)]
    ahead = [[(i, (i + 2 * k) % peers) for i in range(peers)] for k in range(4)]

    def along_of(rows):
        return [rows] + [lax.ppermute(rows, "tile", ahead[k]) for k in (1, 2, 3)]

    late_along = along_of(late)
    before_early = lax.ppermute(early, "blk", next_frames)
    others = pl.pallas_call(
        stack_kernel,
        out_shape=jax.ShapeDtypeStruct((2, frame_rows, width), BF),
        in_specs=[anywhere] * 3 + [VMEM] * 2,
        out_specs=VMEM,
        compiler_params=params(20),
    )(*late_along[1:], early, before_early)
    others_along = along_of(others)
    pieces = []
    for part in late_along:
        pieces += [part, lax.ppermute(part, "tile", other_core)]
    (late_sp,) = pieces_call(pieces_kernel, None, pieces, taps_t)
    before_late_sp = lax.ppermute(late_sp, "blk", next_frames)
    both = []
    for part in others_along:
        both += [part, lax.ppermute(part, "tile", other_core)]
    early_sp, before_early_sp = pieces_call(both_kernel, 2, both, late_sp)

    def core_shares(now, one, two, needed):
        mine, other = point_call(where_am_i, now, one, two, taps_t, w_point, needed)
        return mine, lax.ppermute(other, "tile", other_core)

    def sums(mine, from_core, rows):
        kept, *sends = pl.pallas_call(
            sum_kernel,
            out_shape=[jax.ShapeDtypeStruct((frame_rows, width), F32)] + [one_frame] * 3,
            in_specs=[VMEM] * 3,
            out_specs=[VMEM] * 4,
            compiler_params=params(20),
        )(mine, from_core, rows)
        return kept, [lax.ppermute(part, "tile", ahead[k + 1]) for k, part in enumerate(sends)]

    late_shares = core_shares(late_sp, early_sp, before_late_sp, before_early_sp)
    late_kept, late_back = sums(*late_shares, late)
    early_shares = core_shares(early_sp, before_late_sp, before_early_sp, late_shares[0])
    early_kept, early_back = sums(*early_shares, early)
    return pl.pallas_call(
        final_kernel,
        out_shape=jax.ShapeDtypeStruct(stream_in.shape, BF),
        in_specs=[VMEM] * 8,
        out_specs=VMEM,
        compiler_params=params(20),
    )(early_kept, late_kept, *early_back, *late_back)


def solution(mesh):
    in_specs = (
        P("tile", "blk", None, None),
        P("tile", "blk", None, None),
        P("tile", "blk", None, None),
        P("tile", "blk", None, None),
        P("tile", None),
        P(None, None, "tile"),
        P("tile", None),
        P(None, None, None, "tile"),
        P(None, None, "tile"),
    )
    out_specs = P("tile", "blk", None, None)
    return jax.shard_map(
        on_device, mesh=mesh, in_specs=in_specs, out_specs=out_specs, check_vma=False
    )
```

```python
import functools

import jax
import jax.numpy as jnp
from jax import lax
from jax.experimental import pallas as pl
from jax.experimental.pallas import tpu as pltpu
from jax.sharding import PartitionSpec as P

HEADS = 20
HEAD_DIM = 112
D = 2240
TAPS = 3
EPS = 1e-6
LANES = 128
SLABS = 18
SUB = 14
PIECES = 256
BF = jnp.bfloat16
F32 = jnp.float32
MIB = 1 << 20
PIECES_MIB = 24


def slab_of(c):
    first = (LANES * c) // HEAD_DIM
    bound = HEAD_DIM * (first + 1) - LANES * c
    start = (HEAD_DIM * first) // LANES * LANES
    pair = 2 if first + 1 < HEADS else 1
    stop = min(-(-(HEAD_DIM * (first + pair)) // LANES) * LANES, D)
    return first, pair, bound, start, stop, HEAD_DIM * first - start


def kv_kernel(k_ref, v_ref, out_ref, last_ref):
    tokens = k_ref.shape[0]
    key_pos = jnp.maximum(k_ref[...], 0)
    last_ref[...] = jnp.ones((tokens, LANES), BF)
    last_ref[:, : D - LANES * (SLABS - 1)] = v_ref[:, LANES * (SLABS - 1) :]
    lane = lax.broadcasted_iota(jnp.int32, (HEAD_DIM, LANES), 1)
    over_tokens = (((0,), (0,)), ((), ()))
    for c in range(SLABS):
        first, pair, bound, start, stop, offset = slab_of(c)
        values = last_ref[...] if c == SLABS - 1 else v_ref[:, LANES * c : LANES * (c + 1)]
        product = lax.dot_general(
            key_pos[:, start:stop], values, over_tokens, preferred_element_type=F32
        )
        tile = product[offset : offset + HEAD_DIM]
        if pair == 2:
            tile = jnp.where(lane < bound, tile, product[offset + HEAD_DIM : offset + 2 * HEAD_DIM])
        if c == SLABS - 1:
            sums = lax.dot_general(
                key_pos, jnp.ones((tokens, LANES), BF), over_tokens, preferred_element_type=F32
            )
            tile = jnp.where(lane < bound, tile, 0.0)
            for h in range(HEADS):
                tile = jnp.where(
                    lane == bound + h, sums[HEAD_DIM * h : HEAD_DIM * (h + 1)], tile
                )
        out_ref[SUB * c : SUB * (c + 1)] = tile.reshape(SUB, 8, LANES).astype(BF)
    rest = PIECES - SUB * SLABS
    out_ref[SUB * SLABS :] = jnp.zeros((rest, 8, LANES), BF)


def prefix_kernel(in_ref, out_ref):
    per_block = 16

    def block(b, total):
        here = in_ref[pl.ds(b * per_block, per_block)].astype(F32)
        total = total + jnp.sum(here, axis=0)
        out_ref[pl.ds(b * per_block, per_block)] = jnp.broadcast_to(
            total.astype(BF)[None], (per_block, 8, LANES)
        )
        return total

    lax.fori_loop(0, PIECES // per_block, block, jnp.zeros((8, LANES), F32))


def attend_kernel(q_ref, state_ref, att_ref):
    query_pos = jnp.maximum(q_ref[...], 0)
    lane = lax.broadcasted_iota(jnp.int32, (HEAD_DIM, LANES), 1)
    tile_of = lambda c: state_ref[SUB * c : SUB * (c + 1)].astype(F32).reshape(HEAD_DIM, LANES)
    sums = tile_of(SLABS - 1)
    z_lane = D - LANES * (SLABS - 1)
    for c in range(SLABS):
        first, pair, bound, start, stop, offset = slab_of(c)
        tile = tile_of(c)
        weights = []
        for which in range(2):
            rows = []
            if offset > 0:
                rows.append(jnp.zeros((offset, LANES), F32))
            for k in range(pair):
                if which == 0:
                    part = tile
                else:
                    h = z_lane + first + k
                    part = jnp.broadcast_to(sums[:, h : h + 1], (HEAD_DIM, LANES))
                inside = (lane < bound) if k == 0 else (lane >= bound)
                rows.append(jnp.where(inside, part, 0.0))
            left = stop - start - offset - pair * HEAD_DIM
            if left > 0:
                rows.append(jnp.zeros((left, LANES), F32))
            weights.append(jnp.concatenate(rows, axis=0))
        weight = jnp.concatenate(weights, axis=1).astype(BF)
        both = jnp.dot(query_pos[:, start:stop], weight, preferred_element_type=F32)
        attended = (both[:, :LANES] / (both[:, LANES:] + EPS)).astype(BF)
        width = min(LANES, D - LANES * c)
        att_ref[:, LANES * c : LANES * c + width] = attended[:, :width]


def hidden_kernel(att_ref, stream_ref, w_hbm, needed_ref, early_ref, late_ref, w_ref, sems):
    tokens = att_ref.shape[0]
    step = 384
    spans = [(n, min(n + step, D)) for n in range(0, D, step)]
    copies = []
    for i, (n, stop) in enumerate(spans):
        span = pl.ds(n, stop - n)
        copies.append(pltpu.make_async_copy(w_hbm.at[:, span], w_ref.at[:, span], sems.at[i]))
    for copy in copies:
        copy.start()
    for copy, (n, stop) in zip(copies, spans):
        cols = slice(n, stop)
        copy.wait()
        out = jnp.dot(att_ref[...], w_ref[:, cols], preferred_element_type=F32)
        out = (out + stream_ref[:, cols].astype(F32)).astype(BF)
        for r in range(tokens // 32):
            rows = slice(16 * r, 16 * r + 16)
            early_ref[rows, cols] = out[32 * r : 32 * r + 16]
            late_ref[rows, cols] = out[32 * r + 16 : 32 * r + 32]


def depthwise(hid, w_ref, taps_ref, out_ref, act_ref):
    tokens, cols = hid.shape[0], 16
    width = w_ref.shape[1]
    product = jnp.dot(hid, w_ref[...], preferred_element_type=F32)
    act = (product * jax.nn.sigmoid(product)).astype(BF).astype(F32)
    act_ref[:cols] = jnp.zeros((cols, width), F32)
    act_ref[cols + tokens :] = jnp.zeros((cols, width), F32)
    act_ref[cols : cols + tokens] = act
    taps = taps_ref[...]
    chunk = 32
    col = lax.broadcasted_iota(jnp.int32, (chunk, width), 0) % cols
    for r in range(0, tokens, chunk):
        near = [act_ref[r + cols * a : r + cols * a + chunk] for a in range(3)]
        left, mid, right = (
            near[0] * taps[b : b + 1] + near[1] * taps[3 + b : 4 + b] + near[2] * taps[6 + b : 7 + b]
            for b in range(3)
        )
        left = jnp.where(col == 0, 0.0, pltpu.roll(left, 1, 0))
        right = jnp.where(col == cols - 1, 0.0, pltpu.roll(right, chunk - 1, 0))
        out_ref[r : r + chunk] = (left + mid + right).astype(BF)


def pieces_kernel(place_ref, *refs):
    peers = 8
    pieces = refs[:peers]
    w_ref, taps_ref, _, out_ref, token_ref, act_ref, hid_ref = refs[peers:]
    token_ref[...] = jnp.zeros(token_ref.shape, F32)
    rows = pieces[0].shape[0]

    @pl.when(pl.program_id(0) == 0)
    def _():
        for p, piece in enumerate(pieces):
            source = 2 * ((place_ref[0] + 4 - p // 2) % 4) + (place_ref[1] + p % 2) % 2
            hid_ref[pl.ds(pl.multiple_of(source * rows, rows), rows)] = piece[...]

    depthwise(hid_ref[...], w_ref, taps_ref, out_ref, act_ref)


def point_kernel(
    place_ref, now_ref, one_ref, two_ref, taps_ref, w_ref, needed_ref, mine_ref, other_ref
):
    half = w_ref.shape[1]
    taps = taps_ref[...]
    mix = now_ref[...].astype(F32) * taps[0:1]
    mix = mix + one_ref[...].astype(F32) * taps[1:2]
    mix = mix + two_ref[...].astype(F32) * taps[2:3]
    gate = mix[:, half:]
    gated = (mix[:, :half] * (gate * jax.nn.sigmoid(gate))).astype(BF)
    over_channels = (((1,), (1,)), ((), ()))
    out = lax.dot_general(gated, w_ref[...], over_channels, preferred_element_type=F32).astype(BF)
    y, core = place_ref[0], place_ref[1]
    i = pl.program_id(0)
    rows = out.shape[0] // 4
    for k in range(4):
        target = 4 * i + k
        slot = (target // 2 - y + 4) % 4

        @pl.when(core == k % 2)
        def _():
            mine_ref[slot] = out[rows * k : rows * (k + 1)]

        @pl.when(core != k % 2)
        def _():
            other_ref[slot] = out[rows * k : rows * (k + 1)]


def sum_kernel(mine_ref, other_ref, hidden_ref, kept_ref, *sends):
    total = lambda k: mine_ref[k].astype(F32) + other_ref[k].astype(F32)
    kept_ref[...] = hidden_ref[...].astype(F32) + total(0)
    for k, send in enumerate(sends):
        send[...] = total(k + 1).astype(BF)


def follow_kernel(count, *refs):
    for rows_ref, out_ref in zip(refs[:count], refs[-count:]):
        out_ref[...] = rows_ref[...]


def final_kernel(early_ref, late_ref, *refs):
    pieces, out_ref = refs[:6], refs[6]
    for f, kept in enumerate((early_ref, late_ref)):
        total = kept[...]
        for piece in pieces[3 * f : 3 * f + 3]:
            total = total + piece[...].astype(F32)
        out = total.astype(BF)
        for r in range(out_ref.shape[0]):
            out_ref[r, f] = out[16 * r : 16 * r + 16]


def params(mib):
    return pltpu.CompilerParams(vmem_limit_bytes=mib * MIB)


VMEM = pl.BlockSpec(memory_space=pltpu.VMEM)


def on_device(
    stream_in, queries, key_rows, value_rows, w_output, w_inner, w_down, spatial_taps, temporal_taps
):
    row_count, frames, col_count, width = queries.shape
    tokens = row_count * frames * col_count
    flat = lambda a: a.reshape(tokens, width)
    chan = w_inner.shape[2]
    peers = lax.axis_size("tile")
    place = lax.axis_index("tile")
    where_am_i = jnp.stack([place // 2, place % 2]).astype(jnp.int32)

    w_out_whole = lax.all_gather(w_output, "tile", axis=0, tiled=True)
    w_flat = w_inner.reshape(width, 2 * chan)
    taps_s = spatial_taps.reshape(9, 2 * chan)
    taps_t = temporal_taps.reshape(TAPS, 2 * chan)

    pieces = jax.ShapeDtypeStruct((PIECES, 8, LANES), BF)
    parts = pl.pallas_call(
        kv_kernel,
        out_shape=pieces,
        in_specs=[VMEM] * 2,
        out_specs=VMEM,
        scratch_shapes=[pltpu.VMEM((tokens, LANES), BF)],
        compiler_params=params(40),
    )(flat(key_rows), flat(value_rows))
    everyone = ("blk", "tile")
    parts = lax.all_to_all(parts, everyone, 0, 0, tiled=True)
    sums = pl.pallas_call(
        prefix_kernel, out_shape=pieces, in_specs=[VMEM], out_specs=VMEM, compiler_params=params(40)
    )(parts)
    state = lax.all_to_all(sums, everyone, 0, 0, tiled=True)

    anywhere = pl.BlockSpec(memory_space=pl.ANY)
    frame_rows = row_count * col_count
    attended = pl.pallas_call(
        attend_kernel,
        out_shape=jax.ShapeDtypeStruct((tokens, width), BF),
        in_specs=[VMEM, VMEM],
        out_specs=VMEM,
        compiler_params=params(40),
    )(flat(queries), state)
    one_frame = jax.ShapeDtypeStruct((frame_rows, width), BF)
    early, late = pl.pallas_call(
        hidden_kernel,
        out_shape=[one_frame] * 2,
        in_specs=[VMEM, VMEM, anywhere, anywhere],
        out_specs=[VMEM, VMEM],
        scratch_shapes=[pltpu.VMEM((width, width), BF), pltpu.SemaphoreType.DMA((6,))],
        compiler_params=params(52),
    )(attended, flat(stream_in), w_out_whole, w_flat)

    whole_rows = peers * frame_rows
    block = 256

    spatial_out = jax.ShapeDtypeStruct((whole_rows, 2 * chan), BF)
    weight_specs = [
        pl.BlockSpec((width, block), lambda i: (0, i)),
        pl.BlockSpec((9, block), lambda i: (0, i)),
    ]

    def pieces_call(pieces, needed):
        return pl.pallas_call(
            pieces_kernel,
            out_shape=[spatial_out, jax.ShapeDtypeStruct((8, LANES), F32)],
            grid=(2 * chan // block,),
            in_specs=[pl.BlockSpec(memory_space=pltpu.SMEM)]
            + [pl.BlockSpec((frame_rows, width), lambda i: (0, 0))] * peers
            + weight_specs
            + [anywhere],
            out_specs=[
                pl.BlockSpec((whole_rows, block), lambda i: (0, i)),
                pl.BlockSpec((8, LANES), lambda i: (0, 0)),
            ],
            scratch_shapes=[
                pltpu.VMEM((whole_rows + 2 * col_count, block), F32),
                pltpu.VMEM((whole_rows, width), BF),
            ],
            compiler_params=params(PIECES_MIB),
        )(where_am_i, *pieces, w_flat, taps_s, needed)

    row_block = 256
    point_call = pl.pallas_call(
        point_kernel,
        out_shape=[jax.ShapeDtypeStruct((4, frame_rows, width), BF)] * 2,
        grid=(whole_rows // row_block,),
        in_specs=[pl.BlockSpec(memory_space=pltpu.SMEM)]
        + [pl.BlockSpec((row_block, 2 * chan), lambda i: (i, 0))] * 3
        + [
            pl.BlockSpec((TAPS, 2 * chan), lambda i: (0, 0)),
            pl.BlockSpec((width, chan), lambda i: (0, 0)),
            anywhere,
        ],
        out_specs=[pl.BlockSpec((4, frame_rows, width), lambda i: (0, 0, 0))] * 2,
        compiler_params=params(40),
    )

    w_point = w_down.T
    blocks = lax.axis_size("blk")
    next_frames = [(i, i + 1) for i in range(blocks - 1)]
    other_core = [(i, i ^ 1) for i in range(peers)]
    ahead = [[(i, (i + 2 * k) % peers) for i in range(peers)] for k in range(4)]

    def along_of(rows):
        return [rows] + [lax.ppermute(rows, "tile", ahead[k]) for k in (1, 2, 3)]

    def after(rows, needed):
        return pl.pallas_call(
            functools.partial(follow_kernel, len(rows)),
            out_shape=[one_frame] * len(rows),
            in_specs=[VMEM] * len(rows) + [anywhere] * len(needed),
            out_specs=[VMEM] * len(rows),
            compiler_params=params(20),
        )(*rows, *needed)

    def spatial_of(along, needed):
        pieces = []
        for part in along:
            pieces += [part, lax.ppermute(part, "tile", other_core)]
        return pieces_call(pieces, needed)

    late_along = along_of(late)
    before_early = lax.ppermute(early, "blk", next_frames)
    early_along = along_of(*after([early], late_along[1:]))
    late_sp, late_token = spatial_of(late_along, taps_t)
    before_late_sp = lax.ppermute(late_sp, "blk", next_frames)
    before_early_along = along_of(*after([before_early], early_along[1:] + [late_token]))
    early_sp, early_token = spatial_of(early_along, late_token)
    before_early_along[1:] = after(before_early_along[1:], [early_token])
    before_early_sp, last_token = spatial_of(before_early_along, early_token)

    def core_shares(now, one, two, needed):
        mine, other = point_call(where_am_i, now, one, two, taps_t, w_point, needed)
        return mine, lax.ppermute(other, "tile", other_core)

    def sums(mine, from_core, rows):
        kept, *sends = pl.pallas_call(
            sum_kernel,
            out_shape=[jax.ShapeDtypeStruct((frame_rows, width), F32)] + [one_frame] * 3,
            in_specs=[VMEM] * 3,
            out_specs=[VMEM] * 4,
            compiler_params=params(20),
        )(mine, from_core, rows)
        return kept, [lax.ppermute(part, "tile", ahead[k + 1]) for k, part in enumerate(sends)]

    late_shares = core_shares(late_sp, early_sp, before_late_sp, last_token)
    late_kept, late_back = sums(*late_shares, late)
    early_shares = core_shares(early_sp, before_late_sp, before_early_sp, late_shares[0])
    early_kept, early_back = sums(*early_shares, early)
    return pl.pallas_call(
        final_kernel,
        out_shape=jax.ShapeDtypeStruct(stream_in.shape, BF),
        in_specs=[VMEM] * 8,
        out_specs=VMEM,
        compiler_params=params(20),
    )(early_kept, late_kept, *early_back, *late_back)


def solution(mesh):
    in_specs = (
        P("tile", "blk", None, None),
        P("tile", "blk", None, None),
        P("tile", "blk", None, None),
        P("tile", "blk", None, None),
        P("tile", None),
        P(None, None, "tile"),
        P("tile", None),
        P(None, None, None, "tile"),
        P(None, None, "tile"),
    )
    out_specs = P("tile", "blk", None, None)
    return jax.shard_map(
        on_device, mesh=mesh, in_specs=in_specs, out_specs=out_specs, check_vma=False
    )
```

```python
import functools

import jax
import jax.numpy as jnp
from jax import lax
from jax.experimental import pallas as pl
from jax.experimental.pallas import tpu as pltpu
from jax.sharding import PartitionSpec as P

HEADS = 20
HEAD_DIM = 112
D = 2240
TAPS = 3
EPS = 1e-6
LANES = 128
SLABS = 18
SUB = 14
PIECES = 256
BF = jnp.bfloat16
F32 = jnp.float32
MIB = 1 << 20


def slab_of(c):
    first = (LANES * c) // HEAD_DIM
    bound = HEAD_DIM * (first + 1) - LANES * c
    start = (HEAD_DIM * first) // LANES * LANES
    pair = 2 if first + 1 < HEADS else 1
    stop = min(-(-(HEAD_DIM * (first + pair)) // LANES) * LANES, D)
    return first, pair, bound, start, stop, HEAD_DIM * first - start


def kv_kernel(k_ref, v_ref, out_ref, last_ref):
    tokens = k_ref.shape[0]
    key_pos = jnp.maximum(k_ref[...], 0)
    last_ref[...] = jnp.ones((tokens, LANES), BF)
    last_ref[:, : D - LANES * (SLABS - 1)] = v_ref[:, LANES * (SLABS - 1) :]
    lane = lax.broadcasted_iota(jnp.int32, (HEAD_DIM, LANES), 1)
    over_tokens = (((0,), (0,)), ((), ()))
    for c in range(SLABS):
        first, pair, bound, start, stop, offset = slab_of(c)
        values = last_ref[...] if c == SLABS - 1 else v_ref[:, LANES * c : LANES * (c + 1)]
        product = lax.dot_general(
            key_pos[:, start:stop], values, over_tokens, preferred_element_type=F32
        )
        tile = product[offset : offset + HEAD_DIM]
        if pair == 2:
            tile = jnp.where(lane < bound, tile, product[offset + HEAD_DIM : offset + 2 * HEAD_DIM])
        if c == SLABS - 1:
            sums = lax.dot_general(
                key_pos, jnp.ones((tokens, LANES), BF), over_tokens, preferred_element_type=F32
            )
            tile = jnp.where(lane < bound, tile, 0.0)
            for h in range(HEADS):
                tile = jnp.where(
                    lane == bound + h, sums[HEAD_DIM * h : HEAD_DIM * (h + 1)], tile
                )
        out_ref[SUB * c : SUB * (c + 1)] = tile.reshape(SUB, 8, LANES).astype(BF)
    rest = PIECES - SUB * SLABS
    out_ref[SUB * SLABS :] = jnp.zeros((rest, 8, LANES), BF)


def prefix_kernel(in_ref, out_ref):
    per_block = 16

    def block(b, total):
        here = in_ref[pl.ds(b * per_block, per_block)].astype(F32)
        total = total + jnp.sum(here, axis=0)
        out_ref[pl.ds(b * per_block, per_block)] = jnp.broadcast_to(
            total.astype(BF)[None], (per_block, 8, LANES)
        )
        return total

    lax.fori_loop(0, PIECES // per_block, block, jnp.zeros((8, LANES), F32))


def attend_kernel(q_ref, state_ref, att_ref):
    query_pos = jnp.maximum(q_ref[...], 0)
    lane = lax.broadcasted_iota(jnp.int32, (HEAD_DIM, LANES), 1)
    tile_of = lambda c: state_ref[SUB * c : SUB * (c + 1)].astype(F32).reshape(HEAD_DIM, LANES)
    sums = tile_of(SLABS - 1)
    z_lane = D - LANES * (SLABS - 1)
    for c in range(SLABS):
        first, pair, bound, start, stop, offset = slab_of(c)
        tile = tile_of(c)
        weights = []
        for which in range(2):
            rows = []
            if offset > 0:
                rows.append(jnp.zeros((offset, LANES), F32))
            for k in range(pair):
                if which == 0:
                    part = tile
                else:
                    h = z_lane + first + k
                    part = jnp.broadcast_to(sums[:, h : h + 1], (HEAD_DIM, LANES))
                inside = (lane < bound) if k == 0 else (lane >= bound)
                rows.append(jnp.where(inside, part, 0.0))
            left = stop - start - offset - pair * HEAD_DIM
            if left > 0:
                rows.append(jnp.zeros((left, LANES), F32))
            weights.append(jnp.concatenate(rows, axis=0))
        weight = jnp.concatenate(weights, axis=1).astype(BF)
        both = jnp.dot(query_pos[:, start:stop], weight, preferred_element_type=F32)
        attended = (both[:, :LANES] / (both[:, LANES:] + EPS)).astype(BF)
        width = min(LANES, D - LANES * c)
        att_ref[:, LANES * c : LANES * c + width] = attended[:, :width]


def hidden_kernel(att_ref, stream_ref, w_hbm, needed_ref, early_ref, late_ref, w_ref, sems):
    tokens = att_ref.shape[0]
    step = 384
    spans = [(n, min(n + step, D)) for n in range(0, D, step)]
    copies = []
    for i, (n, stop) in enumerate(spans):
        span = pl.ds(n, stop - n)
        copies.append(pltpu.make_async_copy(w_hbm.at[:, span], w_ref.at[:, span], sems.at[i]))
    for copy in copies:
        copy.start()
    for copy, (n, stop) in zip(copies, spans):
        cols = slice(n, stop)
        copy.wait()
        out = jnp.dot(att_ref[...], w_ref[:, cols], preferred_element_type=F32)
        out = (out + stream_ref[:, cols].astype(F32)).astype(BF)
        for r in range(tokens // 32):
            rows = slice(16 * r, 16 * r + 16)
            early_ref[rows, cols] = out[32 * r : 32 * r + 16]
            late_ref[rows, cols] = out[32 * r + 16 : 32 * r + 32]


def depthwise(hid, w_ref, taps_ref, out_ref, act_ref):
    tokens, cols = hid.shape[0], 16
    width = w_ref.shape[1]
    product = jnp.dot(hid, w_ref[...], preferred_element_type=F32)
    act = (product * jax.nn.sigmoid(product)).astype(BF).astype(F32)
    act_ref[:cols] = jnp.zeros((cols, width), F32)
    act_ref[cols + tokens :] = jnp.zeros((cols, width), F32)
    act_ref[cols : cols + tokens] = act
    taps = taps_ref[...]
    chunk = 32
    col = lax.broadcasted_iota(jnp.int32, (chunk, width), 0) % cols
    for r in range(0, tokens, chunk):
        near = [act_ref[r + cols * a : r + cols * a + chunk] for a in range(3)]
        left, mid, right = (
            near[0] * taps[b : b + 1] + near[1] * taps[3 + b : 4 + b] + near[2] * taps[6 + b : 7 + b]
            for b in range(3)
        )
        left = jnp.where(col == 0, 0.0, pltpu.roll(left, 1, 0))
        right = jnp.where(col == cols - 1, 0.0, pltpu.roll(right, chunk - 1, 0))
        out_ref[r : r + chunk] = (left + mid + right).astype(BF)


def pieces_kernel(place_ref, *refs):
    peers = 8
    pieces, (w_ref, taps_ref, _, out_ref, act_ref, hid_ref) = refs[:peers], refs[peers:]
    rows = pieces[0].shape[0]

    @pl.when(pl.program_id(0) == 0)
    def _():
        for p, piece in enumerate(pieces):
            source = 2 * ((place_ref[0] + 4 - p // 2) % 4) + (place_ref[1] + p % 2) % 2
            hid_ref[pl.ds(pl.multiple_of(source * rows, rows), rows)] = piece[...]

    depthwise(hid_ref[...], w_ref, taps_ref, out_ref, act_ref)


def both_kernel(place_ref, *refs):
    peers, frames = 8, 2
    pieces = refs[:peers]
    w_ref, taps_ref, _, one_ref, two_ref, act_ref, hid_ref = refs[peers:]
    rows = pieces[0].shape[1]

    @pl.when(pl.program_id(0) == 0)
    def _():
        for p, piece in enumerate(pieces):
            source = 2 * ((place_ref[0] + 4 - p // 2) % 4) + (place_ref[1] + p % 2) % 2
            target = pl.ds(pl.multiple_of(source * rows, rows), rows)
            for f in range(frames):
                hid_ref[f, target] = piece[f]

    for f, out_ref in enumerate((one_ref, two_ref)):
        depthwise(hid_ref[f], w_ref, taps_ref, out_ref, act_ref.at[f])


def point_kernel(
    place_ref, now_ref, one_ref, two_ref, taps_ref, w_ref, needed_ref, mine_ref, other_ref
):
    half = w_ref.shape[1]
    taps = taps_ref[...]
    mix = now_ref[...].astype(F32) * taps[0:1]
    mix = mix + one_ref[...].astype(F32) * taps[1:2]
    mix = mix + two_ref[...].astype(F32) * taps[2:3]
    gate = mix[:, half:]
    gated = (mix[:, :half] * (gate * jax.nn.sigmoid(gate))).astype(BF)
    over_channels = (((1,), (1,)), ((), ()))
    out = lax.dot_general(gated, w_ref[...], over_channels, preferred_element_type=F32).astype(BF)
    y, core = place_ref[0], place_ref[1]
    i = pl.program_id(0)
    rows = out.shape[0] // 4
    for k in range(4):
        target = 4 * i + k
        slot = (target // 2 - y + 4) % 4

        @pl.when(core == k % 2)
        def _():
            mine_ref[slot] = out[rows * k : rows * (k + 1)]

        @pl.when(core != k % 2)
        def _():
            other_ref[slot] = out[rows * k : rows * (k + 1)]


def sum_kernel(mine_ref, other_ref, hidden_ref, kept_ref, *sends):
    total = lambda k: mine_ref[k].astype(F32) + other_ref[k].astype(F32)
    kept_ref[...] = hidden_ref[...].astype(F32) + total(0)
    for k, send in enumerate(sends):
        send[...] = total(k + 1).astype(BF)


def stack_kernel(*refs):
    one_ref, two_ref, out_ref = refs[-3:]
    out_ref[0] = one_ref[...]
    out_ref[1] = two_ref[...]


def final_kernel(early_ref, late_ref, *refs):
    pieces, out_ref = refs[:6], refs[6]
    for f, kept in enumerate((early_ref, late_ref)):
        total = kept[...]
        for piece in pieces[3 * f : 3 * f + 3]:
            total = total + piece[...].astype(F32)
        out = total.astype(BF)
        for r in range(out_ref.shape[0]):
            out_ref[r, f] = out[16 * r : 16 * r + 16]


def params(mib):
    return pltpu.CompilerParams(vmem_limit_bytes=mib * MIB)


VMEM = pl.BlockSpec(memory_space=pltpu.VMEM)


def on_device(
    stream_in, queries, key_rows, value_rows, w_output, w_inner, w_down, spatial_taps, temporal_taps
):
    row_count, frames, col_count, width = queries.shape
    tokens = row_count * frames * col_count
    flat = lambda a: a.reshape(tokens, width)
    chan = w_inner.shape[2]
    peers = lax.axis_size("tile")
    place = lax.axis_index("tile")
    where_am_i = jnp.stack([place // 2, place % 2]).astype(jnp.int32)

    w_out_whole = lax.all_gather(w_output, "tile", axis=0, tiled=True)
    w_flat = w_inner.reshape(width, 2 * chan)
    taps_s = spatial_taps.reshape(9, 2 * chan)
    taps_t = temporal_taps.reshape(TAPS, 2 * chan)

    pieces = jax.ShapeDtypeStruct((PIECES, 8, LANES), BF)
    parts = pl.pallas_call(
        kv_kernel,
        out_shape=pieces,
        in_specs=[VMEM] * 2,
        out_specs=VMEM,
        scratch_shapes=[pltpu.VMEM((tokens, LANES), BF)],
        compiler_params=params(40),
    )(flat(key_rows), flat(value_rows))
    everyone = ("blk", "tile")
    parts = lax.all_to_all(parts, everyone, 0, 0, tiled=True)
    sums = pl.pallas_call(
        prefix_kernel, out_shape=pieces, in_specs=[VMEM], out_specs=VMEM, compiler_params=params(40)
    )(parts)
    state = lax.all_to_all(sums, everyone, 0, 0, tiled=True)

    anywhere = pl.BlockSpec(memory_space=pl.ANY)
    frame_rows = row_count * col_count
    attended = pl.pallas_call(
        attend_kernel,
        out_shape=jax.ShapeDtypeStruct((tokens, width), BF),
        in_specs=[VMEM, VMEM],
        out_specs=VMEM,
        compiler_params=params(40),
    )(flat(queries), state)
    one_frame = jax.ShapeDtypeStruct((frame_rows, width), BF)
    early, late = pl.pallas_call(
        hidden_kernel,
        out_shape=[one_frame] * 2,
        in_specs=[VMEM, VMEM, anywhere, anywhere],
        out_specs=[VMEM, VMEM],
        scratch_shapes=[pltpu.VMEM((width, width), BF), pltpu.SemaphoreType.DMA((6,))],
        compiler_params=params(52),
    )(attended, flat(stream_in), w_out_whole, w_flat)

    whole_rows = peers * frame_rows
    block = 256

    spatial_out = jax.ShapeDtypeStruct((whole_rows, 2 * chan), BF)
    weight_specs = [
        pl.BlockSpec((width, block), lambda i: (0, i)),
        pl.BlockSpec((9, block), lambda i: (0, i)),
    ]

    def pieces_call(kernel, frames, pieces, needed):
        outs = 1 if frames is None else frames
        lead = () if frames is None else (frames,)
        return pl.pallas_call(
            kernel,
            out_shape=[spatial_out] * outs,
            grid=(2 * chan // block,),
            in_specs=[pl.BlockSpec(memory_space=pltpu.SMEM)]
            + [pl.BlockSpec(part.shape, lambda i, n=part.ndim: (0,) * n) for part in pieces]
            + weight_specs
            + [anywhere],
            out_specs=[pl.BlockSpec((whole_rows, block), lambda i: (0, i))] * outs,
            scratch_shapes=[
                pltpu.VMEM(lead + (whole_rows + 2 * col_count, block), F32),
                pltpu.VMEM(lead + (whole_rows, width), BF),
            ],
            compiler_params=params(24 if frames is None else 32),
        )(where_am_i, *pieces, w_flat, taps_s, needed)

    row_block = 256
    point_call = pl.pallas_call(
        point_kernel,
        out_shape=[jax.ShapeDtypeStruct((4, frame_rows, width), BF)] * 2,
        grid=(whole_rows // row_block,),
        in_specs=[pl.BlockSpec(memory_space=pltpu.SMEM)]
        + [pl.BlockSpec((row_block, 2 * chan), lambda i: (i, 0))] * 3
        + [
            pl.BlockSpec((TAPS, 2 * chan), lambda i: (0, 0)),
            pl.BlockSpec((width, chan), lambda i: (0, 0)),
            anywhere,
        ],
        out_specs=[pl.BlockSpec((4, frame_rows, width), lambda i: (0, 0, 0))] * 2,
        compiler_params=params(40),
    )

    w_point = w_down.T
    blocks = lax.axis_size("blk")
    next_frames = [(i, i + 1) for i in range(blocks - 1)]
    other_core = [(i, i ^ 1) for i in range(peers)]
    ahead = [[(i, (i + 2 * k) % peers) for i in range(peers)] for k in range(4)]

    def along_of(rows):
        return [rows] + [lax.ppermute(rows, "tile", ahead[k]) for k in (1, 2, 3)]

    late_along = along_of(late)
    before_early = lax.ppermute(early, "blk", next_frames)
    others = pl.pallas_call(
        stack_kernel,
        out_shape=jax.ShapeDtypeStruct((2, frame_rows, width), BF),
        in_specs=[anywhere] * 3 + [VMEM] * 2,
        out_specs=VMEM,
        compiler_params=params(20),
    )(*late_along[1:], early, before_early)
    others_along = along_of(others)
    pieces = []
    for part in late_along:
        pieces += [part, lax.ppermute(part, "tile", other_core)]
    (late_sp,) = pieces_call(pieces_kernel, None, pieces, taps_t)
    before_late_sp = lax.ppermute(late_sp, "blk", next_frames)
    both = []
    for part in others_along:
        both += [part, lax.ppermute(part, "tile", other_core)]
    early_sp, before_early_sp = pieces_call(both_kernel, 2, both, late_sp)

    def core_shares(now, one, two, needed):
        mine, other = point_call(where_am_i, now, one, two, taps_t, w_point, needed)
        return mine, lax.ppermute(other, "tile", other_core)

    def sums(mine, from_core, rows):
        kept, *sends = pl.pallas_call(
            sum_kernel,
            out_shape=[jax.ShapeDtypeStruct((frame_rows, width), F32)] + [one_frame] * 3,
            in_specs=[VMEM] * 3,
            out_specs=[VMEM] * 4,
            compiler_params=params(20),
        )(mine, from_core, rows)
        return kept, [lax.ppermute(part, "tile", ahead[k + 1]) for k, part in enumerate(sends)]

    late_shares = core_shares(late_sp, early_sp, before_late_sp, before_early_sp)
    late_kept, late_back = sums(*late_shares, late)
    early_shares = core_shares(early_sp, before_late_sp, before_early_sp, late_shares[0])
    early_kept, early_back = sums(*early_shares, early)
    return pl.pallas_call(
        final_kernel,
        out_shape=jax.ShapeDtypeStruct(stream_in.shape, BF),
        in_specs=[VMEM] * 8,
        out_specs=VMEM,
        compiler_params=params(20),
    )(early_kept, late_kept, *early_back, *late_back)


def solution(mesh):
    in_specs = (
        P("tile", "blk", None, None),
        P("tile", "blk", None, None),
        P("tile", "blk", None, None),
        P("tile", "blk", None, None),
        P("tile", None),
        P(None, None, "tile"),
        P("tile", None),
        P(None, None, None, "tile"),
        P(None, None, "tile"),
    )
    out_specs = P("tile", "blk", None, None)
    return jax.shard_map(
        on_device, mesh=mesh, in_specs=in_specs, out_specs=out_specs, check_vma=False
    )
```

```python
import functools

import jax
import jax.numpy as jnp
from jax import lax
from jax.experimental import pallas as pl
from jax.experimental.pallas import tpu as pltpu
from jax.sharding import PartitionSpec as P

HEADS = 20
HEAD_DIM = 112
D = 2240
TAPS = 3
EPS = 1e-6
LANES = 128
SLABS = 18
SUB = 14
PIECES = 256
HALF = 128
TILE = ("y", "core")
BF = jnp.bfloat16
F32 = jnp.float32
MIB = 1 << 20


def slab_of(c):
    first = (LANES * c) // HEAD_DIM
    bound = HEAD_DIM * (first + 1) - LANES * c
    start = (HEAD_DIM * first) // LANES * LANES
    pair = 2 if first + 1 < HEADS else 1
    stop = min(-(-(HEAD_DIM * (first + pair)) // LANES) * LANES, D)
    return first, pair, bound, start, stop, HEAD_DIM * first - start


def kv_kernel(place_ref, k_ref, v_ref, mine_ref, other_ref, last_ref, out_ref):
    tokens = k_ref.shape[0]
    key_pos = jnp.maximum(k_ref[...], 0)
    last_ref[...] = jnp.ones((tokens, LANES), BF)
    last_ref[:, : D - LANES * (SLABS - 1)] = v_ref[:, LANES * (SLABS - 1) :]
    lane = lax.broadcasted_iota(jnp.int32, (HEAD_DIM, LANES), 1)
    over_tokens = (((0,), (0,)), ((), ()))
    for c in range(SLABS):
        first, pair, bound, start, stop, offset = slab_of(c)
        values = last_ref[...] if c == SLABS - 1 else v_ref[:, LANES * c : LANES * (c + 1)]
        product = lax.dot_general(
            key_pos[:, start:stop], values, over_tokens, preferred_element_type=F32
        )
        tile = product[offset : offset + HEAD_DIM]
        if pair == 2:
            tile = jnp.where(lane < bound, tile, product[offset + HEAD_DIM : offset + 2 * HEAD_DIM])
        if c == SLABS - 1:
            sums = lax.dot_general(
                key_pos, jnp.ones((tokens, LANES), BF), over_tokens, preferred_element_type=F32
            )
            tile = jnp.where(lane < bound, tile, 0.0)
            for h in range(HEADS):
                tile = jnp.where(
                    lane == bound + h, sums[HEAD_DIM * h : HEAD_DIM * (h + 1)], tile
                )
        out_ref[SUB * c : SUB * (c + 1)] = tile.reshape(SUB, 8, LANES).astype(BF)
    rest = PIECES - SUB * SLABS
    out_ref[SUB * SLABS :] = jnp.zeros((rest, 8, LANES), BF)
    core = place_ref[1]
    mine_ref[...] = out_ref[pl.ds(HALF * core, HALF)]
    other_ref[...] = out_ref[pl.ds(HALF * (1 - core), HALF)]


def add_kernel(one_ref, two_ref, out_ref):
    out_ref[...] = (one_ref[...].astype(F32) + two_ref[...].astype(F32)).astype(BF)


def prefix_kernel(in_ref, out_ref):
    per_block = 8

    def block(b, total):
        here = in_ref[pl.ds(b * per_block, per_block)].astype(F32)
        total = total + jnp.sum(here, axis=0)
        out_ref[pl.ds(b * per_block, per_block)] = jnp.broadcast_to(
            total.astype(BF)[None], (per_block, 8, LANES)
        )
        return total

    lax.fori_loop(0, HALF // per_block, block, jnp.zeros((8, LANES), F32))


def attend_kernel(place_ref, q_ref, mine_ref, other_ref, att_ref, state_ref):
    core = place_ref[1]
    state_ref[pl.ds(HALF * core, HALF)] = mine_ref[...]
    state_ref[pl.ds(HALF * (1 - core), HALF)] = other_ref[...]
    query_pos = jnp.maximum(q_ref[...], 0)
    lane = lax.broadcasted_iota(jnp.int32, (HEAD_DIM, LANES), 1)
    tile_of = lambda c: state_ref[SUB * c : SUB * (c + 1)].astype(F32).reshape(HEAD_DIM, LANES)
    sums = tile_of(SLABS - 1)
    z_lane = D - LANES * (SLABS - 1)
    for c in range(SLABS):
        first, pair, bound, start, stop, offset = slab_of(c)
        tile = tile_of(c)
        weights = []
        for which in range(2):
            rows = []
            if offset > 0:
                rows.append(jnp.zeros((offset, LANES), F32))
            for k in range(pair):
                if which == 0:
                    part = tile
                else:
                    h = z_lane + first + k
                    part = jnp.broadcast_to(sums[:, h : h + 1], (HEAD_DIM, LANES))
                inside = (lane < bound) if k == 0 else (lane >= bound)
                rows.append(jnp.where(inside, part, 0.0))
            left = stop - start - offset - pair * HEAD_DIM
            if left > 0:
                rows.append(jnp.zeros((left, LANES), F32))
            weights.append(jnp.concatenate(rows, axis=0))
        weight = jnp.concatenate(weights, axis=1).astype(BF)
        both = jnp.dot(query_pos[:, start:stop], weight, preferred_element_type=F32)
        attended = (both[:, :LANES] / (both[:, LANES:] + EPS)).astype(BF)
        width = min(LANES, D - LANES * c)
        att_ref[:, LANES * c : LANES * c + width] = attended[:, :width]


def hidden_kernel(att_ref, stream_ref, w_hbm, needed_ref, early_ref, late_ref, w_ref, sems):
    tokens = att_ref.shape[0]
    step = 384
    spans = [(n, min(n + step, D)) for n in range(0, D, step)]
    copies = []
    for i, (n, stop) in enumerate(spans):
        span = pl.ds(n, stop - n)
        copies.append(pltpu.make_async_copy(w_hbm.at[:, span], w_ref.at[:, span], sems.at[i]))
    for copy in copies:
        copy.start()
    for copy, (n, stop) in zip(copies, spans):
        cols = slice(n, stop)
        copy.wait()
        out = jnp.dot(att_ref[...], w_ref[:, cols], preferred_element_type=F32)
        out = (out + stream_ref[:, cols].astype(F32)).astype(BF)
        for r in range(tokens // 32):
            rows = slice(16 * r, 16 * r + 16)
            early_ref[rows, cols] = out[32 * r : 32 * r + 16]
            late_ref[rows, cols] = out[32 * r + 16 : 32 * r + 32]


def depthwise(hid, w_ref, taps_ref, out_ref, act_ref):
    tokens, cols = hid.shape[0], 16
    width = w_ref.shape[1]
    product = jnp.dot(hid, w_ref[...], preferred_element_type=F32)
    act = (product * jax.nn.sigmoid(product)).astype(BF).astype(F32)
    act_ref[:cols] = jnp.zeros((cols, width), F32)
    act_ref[cols + tokens :] = jnp.zeros((cols, width), F32)
    act_ref[cols : cols + tokens] = act
    taps = taps_ref[...]
    chunk = 32
    col = lax.broadcasted_iota(jnp.int32, (chunk, width), 0) % cols
    for r in range(0, tokens, chunk):
        near = [act_ref[r + cols * a : r + cols * a + chunk] for a in range(3)]
        left, mid, right = (
            near[0] * taps[b : b + 1] + near[1] * taps[3 + b : 4 + b] + near[2] * taps[6 + b : 7 + b]
            for b in range(3)
        )
        left = jnp.where(col == 0, 0.0, pltpu.roll(left, 1, 0))
        right = jnp.where(col == cols - 1, 0.0, pltpu.roll(right, chunk - 1, 0))
        out_ref[r : r + chunk] = (left + mid + right).astype(BF)


def pieces_kernel(place_ref, *refs):
    peers = 8
    pieces, (w_ref, taps_ref, _, out_ref, act_ref, hid_ref) = refs[:peers], refs[peers:]
    rows = pieces[0].shape[0]

    @pl.when(pl.program_id(0) == 0)
    def _():
        for p, piece in enumerate(pieces):
            source = 2 * ((place_ref[0] + 4 - p // 2) % 4) + (place_ref[1] + p % 2) % 2
            hid_ref[pl.ds(pl.multiple_of(source * rows, rows), rows)] = piece[...]

    depthwise(hid_ref[...], w_ref, taps_ref, out_ref, act_ref)


def both_kernel(place_ref, *refs):
    peers, frames = 8, 2
    pieces = refs[:peers]
    w_ref, taps_ref, _, one_ref, two_ref, act_ref, hid_ref = refs[peers:]
    rows = pieces[0].shape[1]

    @pl.when(pl.program_id(0) == 0)
    def _():
        for p, piece in enumerate(pieces):
            source = 2 * ((place_ref[0] + 4 - p // 2) % 4) + (place_ref[1] + p % 2) % 2
            target = pl.ds(pl.multiple_of(source * rows, rows), rows)
            for f in range(frames):
                hid_ref[f, target] = piece[f]

    for f, out_ref in enumerate((one_ref, two_ref)):
        depthwise(hid_ref[f], w_ref, taps_ref, out_ref, act_ref.at[f])


def point_kernel(
    place_ref, now_ref, one_ref, two_ref, taps_ref, w_ref, needed_ref, mine_ref, other_ref
):
    half = w_ref.shape[1]
    taps = taps_ref[...]
    mix = now_ref[...].astype(F32) * taps[0:1]
    mix = mix + one_ref[...].astype(F32) * taps[1:2]
    mix = mix + two_ref[...].astype(F32) * taps[2:3]
    gate = mix[:, half:]
    gated = (mix[:, :half] * (gate * jax.nn.sigmoid(gate))).astype(BF)
    over_channels = (((1,), (1,)), ((), ()))
    out = lax.dot_general(gated, w_ref[...], over_channels, preferred_element_type=F32).astype(BF)
    y, core = place_ref[0], place_ref[1]
    i = pl.program_id(0)
    rows = out.shape[0] // 4
    for k in range(4):
        target = 4 * i + k
        slot = (target // 2 - y + 4) % 4

        @pl.when(core == k % 2)
        def _():
            mine_ref[slot] = out[rows * k : rows * (k + 1)]

        @pl.when(core != k % 2)
        def _():
            other_ref[slot] = out[rows * k : rows * (k + 1)]


def sum_kernel(mine_ref, other_ref, hidden_ref, kept_ref, *sends):
    total = lambda k: mine_ref[k].astype(F32) + other_ref[k].astype(F32)
    kept_ref[...] = hidden_ref[...].astype(F32) + total(0)
    for k, send in enumerate(sends):
        send[...] = total(k + 1).astype(BF)


def stack_kernel(*refs):
    one_ref, two_ref, out_ref = refs[-3:]
    out_ref[0] = one_ref[...]
    out_ref[1] = two_ref[...]


def final_kernel(early_ref, late_ref, *refs):
    pieces, out_ref = refs[:6], refs[6]
    for f, kept in enumerate((early_ref, late_ref)):
        total = kept[...]
        for piece in pieces[3 * f : 3 * f + 3]:
            total = total + piece[...].astype(F32)
        out = total.astype(BF)
        for r in range(out_ref.shape[0]):
            out_ref[r, f] = out[16 * r : 16 * r + 16]


def params(mib):
    return pltpu.CompilerParams(vmem_limit_bytes=mib * MIB)


VMEM = pl.BlockSpec(memory_space=pltpu.VMEM)


def on_device(
    stream_in, queries, key_rows, value_rows, w_output, w_inner, w_down, spatial_taps, temporal_taps
):
    row_count, frames, col_count, width = queries.shape
    tokens = row_count * frames * col_count
    flat = lambda a: a.reshape(tokens, width)
    chan = w_inner.shape[2]
    peers = lax.axis_size(TILE)
    place = lax.axis_index(TILE)
    where_am_i = jnp.stack([place // 2, place % 2]).astype(jnp.int32)

    w_out_whole = lax.all_gather(w_output, TILE, axis=0, tiled=True)
    w_flat = w_inner.reshape(width, 2 * chan)
    taps_s = spatial_taps.reshape(9, 2 * chan)
    taps_t = temporal_taps.reshape(TAPS, 2 * chan)

    half = jax.ShapeDtypeStruct((HALF, 8, LANES), BF)
    scalars = pl.BlockSpec(memory_space=pltpu.SMEM)
    other_core = [(i, i ^ 1) for i in range(peers)]
    mine, other = pl.pallas_call(
        kv_kernel,
        out_shape=[half] * 2,
        in_specs=[scalars, VMEM, VMEM],
        out_specs=[VMEM] * 2,
        scratch_shapes=[pltpu.VMEM((tokens, LANES), BF), pltpu.VMEM((PIECES, 8, LANES), BF)],
        compiler_params=params(40),
    )(where_am_i, flat(key_rows), flat(value_rows))
    parts = pl.pallas_call(
        add_kernel, out_shape=half, in_specs=[VMEM] * 2, out_specs=VMEM, compiler_params=params(20)
    )(mine, lax.ppermute(other, TILE, other_core))
    same_core = ("blk", "y")
    parts = lax.all_to_all(parts, same_core, 0, 0, tiled=True)
    sums = pl.pallas_call(
        prefix_kernel, out_shape=half, in_specs=[VMEM], out_specs=VMEM, compiler_params=params(40)
    )(parts)
    state = lax.all_to_all(sums, same_core, 0, 0, tiled=True)

    anywhere = pl.BlockSpec(memory_space=pl.ANY)
    frame_rows = row_count * col_count
    attended = pl.pallas_call(
        attend_kernel,
        out_shape=jax.ShapeDtypeStruct((tokens, width), BF),
        in_specs=[scalars, VMEM, VMEM, VMEM],
        out_specs=VMEM,
        scratch_shapes=[pltpu.VMEM((PIECES, 8, LANES), BF)],
        compiler_params=params(40),
    )(where_am_i, flat(queries), state, lax.ppermute(state, TILE, other_core))
    one_frame = jax.ShapeDtypeStruct((frame_rows, width), BF)
    early, late = pl.pallas_call(
        hidden_kernel,
        out_shape=[one_frame] * 2,
        in_specs=[VMEM, VMEM, anywhere, anywhere],
        out_specs=[VMEM, VMEM],
        scratch_shapes=[pltpu.VMEM((width, width), BF), pltpu.SemaphoreType.DMA((6,))],
        compiler_params=params(52),
    )(attended, flat(stream_in), w_out_whole, w_flat)

    whole_rows = peers * frame_rows
    block = 256

    spatial_out = jax.ShapeDtypeStruct((whole_rows, 2 * chan), BF)
    weight_specs = [
        pl.BlockSpec((width, block), lambda i: (0, i)),
        pl.BlockSpec((9, block), lambda i: (0, i)),
    ]

    def pieces_call(kernel, frames, pieces, needed):
        outs = 1 if frames is None else frames
        lead = () if frames is None else (frames,)
        return pl.pallas_call(
            kernel,
            out_shape=[spatial_out] * outs,
            grid=(2 * chan // block,),
            in_specs=[pl.BlockSpec(memory_space=pltpu.SMEM)]
            + [pl.BlockSpec(part.shape, lambda i, n=part.ndim: (0,) * n) for part in pieces]
            + weight_specs
            + [anywhere],
            out_specs=[pl.BlockSpec((whole_rows, block), lambda i: (0, i))] * outs,
            scratch_shapes=[
                pltpu.VMEM(lead + (whole_rows + 2 * col_count, block), F32),
                pltpu.VMEM(lead + (whole_rows, width), BF),
            ],
            compiler_params=params(24 if frames is None else 32),
        )(where_am_i, *pieces, w_flat, taps_s, needed)

    row_block = 256
    point_call = pl.pallas_call(
        point_kernel,
        out_shape=[jax.ShapeDtypeStruct((4, frame_rows, width), BF)] * 2,
        grid=(whole_rows // row_block,),
        in_specs=[pl.BlockSpec(memory_space=pltpu.SMEM)]
        + [pl.BlockSpec((row_block, 2 * chan), lambda i: (i, 0))] * 3
        + [
            pl.BlockSpec((TAPS, 2 * chan), lambda i: (0, 0)),
            pl.BlockSpec((width, chan), lambda i: (0, 0)),
            anywhere,
        ],
        out_specs=[pl.BlockSpec((4, frame_rows, width), lambda i: (0, 0, 0))] * 2,
        compiler_params=params(40),
    )

    w_point = w_down.T
    blocks = lax.axis_size("blk")
    next_frames = [(i, i + 1) for i in range(blocks - 1)]
    other_core = [(i, i ^ 1) for i in range(peers)]
    ahead = [[(i, (i + 2 * k) % peers) for i in range(peers)] for k in range(4)]

    def along_of(rows):
        return [rows] + [lax.ppermute(rows, TILE, ahead[k]) for k in (1, 2, 3)]

    late_along = along_of(late)
    before_early = lax.ppermute(early, "blk", next_frames)
    others = pl.pallas_call(
        stack_kernel,
        out_shape=jax.ShapeDtypeStruct((2, frame_rows, width), BF),
        in_specs=[anywhere] * 3 + [VMEM] * 2,
        out_specs=VMEM,
        compiler_params=params(20),
    )(*late_along[1:], early, before_early)
    others_along = along_of(others)
    pieces = []
    for part in late_along:
        pieces += [part, lax.ppermute(part, TILE, other_core)]
    (late_sp,) = pieces_call(pieces_kernel, None, pieces, taps_t)
    before_late_sp = lax.ppermute(late_sp, "blk", next_frames)
    both = []
    for part in others_along:
        both += [part, lax.ppermute(part, TILE, other_core)]
    early_sp, before_early_sp = pieces_call(both_kernel, 2, both, late_sp)

    def core_shares(now, one, two, needed):
        mine, other = point_call(where_am_i, now, one, two, taps_t, w_point, needed)
        return mine, lax.ppermute(other, TILE, other_core)

    def sums(mine, from_core, rows):
        kept, *sends = pl.pallas_call(
            sum_kernel,
            out_shape=[jax.ShapeDtypeStruct((frame_rows, width), F32)] + [one_frame] * 3,
            in_specs=[VMEM] * 3,
            out_specs=[VMEM] * 4,
            compiler_params=params(20),
        )(mine, from_core, rows)
        return kept, [lax.ppermute(part, TILE, ahead[k + 1]) for k, part in enumerate(sends)]

    late_shares = core_shares(late_sp, early_sp, before_late_sp, before_early_sp)
    late_kept, late_back = sums(*late_shares, late)
    early_shares = core_shares(early_sp, before_late_sp, before_early_sp, late_shares[0])
    early_kept, early_back = sums(*early_shares, early)
    return pl.pallas_call(
        final_kernel,
        out_shape=jax.ShapeDtypeStruct(stream_in.shape, BF),
        in_specs=[VMEM] * 8,
        out_specs=VMEM,
        compiler_params=params(20),
    )(early_kept, late_kept, *early_back, *late_back)


def solution(mesh):
    in_specs = (
        P(TILE, "blk", None, None),
        P(TILE, "blk", None, None),
        P(TILE, "blk", None, None),
        P(TILE, "blk", None, None),
        P(TILE, None),
        P(None, None, TILE),
        P(TILE, None),
        P(None, None, None, TILE),
        P(None, None, TILE),
    )
    out_specs = P(TILE, "blk", None, None)
    sizes = mesh.devices.shape
    mesh = jax.sharding.Mesh(mesh.devices.reshape(sizes[0], sizes[1] // 2, 2), ("blk", "y", "core"))
    return jax.shard_map(
        on_device, mesh=mesh, in_specs=in_specs, out_specs=out_specs, check_vma=False
    )
```

```python
import functools

import jax
import jax.numpy as jnp
from jax import lax
from jax.experimental import pallas as pl
from jax.experimental.pallas import tpu as pltpu
from jax.sharding import PartitionSpec as P

HEADS = 20
HEAD_DIM = 112
D = 2240
TAPS = 3
EPS = 1e-6
LANES = 128
SLABS = 18
SUB = 14
PIECES = 256
HALF = 128
TILE = ("y", "core")
BF = jnp.bfloat16
F32 = jnp.float32
MIB = 1 << 20


def slab_of(c):
    first = (LANES * c) // HEAD_DIM
    bound = HEAD_DIM * (first + 1) - LANES * c
    start = (HEAD_DIM * first) // LANES * LANES
    pair = 2 if first + 1 < HEADS else 1
    stop = min(-(-(HEAD_DIM * (first + pair)) // LANES) * LANES, D)
    return first, pair, bound, start, stop, HEAD_DIM * first - start


def kv_kernel(place_ref, k_ref, v_ref, mine_ref, other_ref, last_ref, out_ref):
    tokens = k_ref.shape[0]
    key_pos = jnp.maximum(k_ref[...], 0)
    last_ref[...] = jnp.ones((tokens, LANES), BF)
    last_ref[:, : D - LANES * (SLABS - 1)] = v_ref[:, LANES * (SLABS - 1) :]
    lane = lax.broadcasted_iota(jnp.int32, (HEAD_DIM, LANES), 1)
    over_tokens = (((0,), (0,)), ((), ()))
    for c in range(SLABS):
        first, pair, bound, start, stop, offset = slab_of(c)
        values = last_ref[...] if c == SLABS - 1 else v_ref[:, LANES * c : LANES * (c + 1)]
        product = lax.dot_general(
            key_pos[:, start:stop], values, over_tokens, preferred_element_type=F32
        )
        tile = product[offset : offset + HEAD_DIM]
        if pair == 2:
            tile = jnp.where(lane < bound, tile, product[offset + HEAD_DIM : offset + 2 * HEAD_DIM])
        if c == SLABS - 1:
            sums = lax.dot_general(
                key_pos, jnp.ones((tokens, LANES), BF), over_tokens, preferred_element_type=F32
            )
            tile = jnp.where(lane < bound, tile, 0.0)
            for h in range(HEADS):
                tile = jnp.where(
                    lane == bound + h, sums[HEAD_DIM * h : HEAD_DIM * (h + 1)], tile
                )
        out_ref[SUB * c : SUB * (c + 1)] = tile.reshape(SUB, 8, LANES).astype(BF)
    rest = PIECES - SUB * SLABS
    out_ref[SUB * SLABS :] = jnp.zeros((rest, 8, LANES), BF)
    core = place_ref[1]
    mine_ref[...] = out_ref[pl.ds(HALF * core, HALF)]
    other_ref[...] = out_ref[pl.ds(HALF * (1 - core), HALF)]


def add_kernel(one_ref, two_ref, out_ref):
    out_ref[...] = (one_ref[...].astype(F32) + two_ref[...].astype(F32)).astype(BF)


def prefix_kernel(in_ref, out_ref):
    per_block = 8

    def block(b, total):
        here = in_ref[pl.ds(b * per_block, per_block)].astype(F32)
        total = total + jnp.sum(here, axis=0)
        out_ref[pl.ds(b * per_block, per_block)] = jnp.broadcast_to(
            total.astype(BF)[None], (per_block, 8, LANES)
        )
        return total

    lax.fori_loop(0, HALF // per_block, block, jnp.zeros((8, LANES), F32))


def attend_kernel(place_ref, q_ref, mine_ref, other_ref, att_ref, state_ref):
    core = place_ref[1]
    state_ref[pl.ds(HALF * core, HALF)] = mine_ref[...]
    state_ref[pl.ds(HALF * (1 - core), HALF)] = other_ref[...]
    query_pos = jnp.maximum(q_ref[...], 0)
    lane = lax.broadcasted_iota(jnp.int32, (HEAD_DIM, LANES), 1)
    tile_of = lambda c: state_ref[SUB * c : SUB * (c + 1)].astype(F32).reshape(HEAD_DIM, LANES)
    sums = tile_of(SLABS - 1)
    z_lane = D - LANES * (SLABS - 1)
    for c in range(SLABS):
        first, pair, bound, start, stop, offset = slab_of(c)
        tile = tile_of(c)
        weights = []
        for which in range(2):
            rows = []
            if offset > 0:
                rows.append(jnp.zeros((offset, LANES), F32))
            for k in range(pair):
                if which == 0:
                    part = tile
                else:
                    h = z_lane + first + k
                    part = jnp.broadcast_to(sums[:, h : h + 1], (HEAD_DIM, LANES))
                inside = (lane < bound) if k == 0 else (lane >= bound)
                rows.append(jnp.where(inside, part, 0.0))
            left = stop - start - offset - pair * HEAD_DIM
            if left > 0:
                rows.append(jnp.zeros((left, LANES), F32))
            weights.append(jnp.concatenate(rows, axis=0))
        weight = jnp.concatenate(weights, axis=1).astype(BF)
        both = jnp.dot(query_pos[:, start:stop], weight, preferred_element_type=F32)
        attended = (both[:, :LANES] / (both[:, LANES:] + EPS)).astype(BF)
        width = min(LANES, D - LANES * c)
        att_ref[:, LANES * c : LANES * c + width] = attended[:, :width]


def hidden_kernel(att_ref, stream_ref, w_hbm, needed_ref, early_ref, late_ref, w_ref, sems):
    tokens = att_ref.shape[0]
    step = 512
    spans = [(n, min(n + step, D)) for n in range(0, D, step)]
    copies = []
    for i, (n, stop) in enumerate(spans):
        span = pl.ds(n, stop - n)
        copies.append(pltpu.make_async_copy(w_hbm.at[span], w_ref.at[span], sems.at[i]))
    for copy in copies:
        copy.start()
    total = stream_ref[...].astype(F32)
    for copy, (n, stop) in zip(copies, spans):
        copy.wait()
        total = total + jnp.dot(att_ref[:, n:stop], w_ref[n:stop], preferred_element_type=F32)
    out = total.astype(BF)
    for r in range(tokens // 32):
        rows = slice(16 * r, 16 * r + 16)
        early_ref[rows] = out[32 * r : 32 * r + 16]
        late_ref[rows] = out[32 * r + 16 : 32 * r + 32]


def depthwise(hid, w_ref, taps_ref, out_ref, act_ref):
    tokens, cols = hid.shape[0], 16
    width = w_ref.shape[1]
    product = jnp.dot(hid, w_ref[...], preferred_element_type=F32)
    act = (product * jax.nn.sigmoid(product)).astype(BF).astype(F32)
    act_ref[:cols] = jnp.zeros((cols, width), F32)
    act_ref[cols + tokens :] = jnp.zeros((cols, width), F32)
    act_ref[cols : cols + tokens] = act
    taps = taps_ref[...]
    chunk = 16
    col = lax.broadcasted_iota(jnp.int32, (chunk, width), 0) % cols
    for r in range(0, tokens, chunk):
        near = [act_ref[r + cols * a : r + cols * a + chunk] for a in range(3)]
        left, mid, right = (
            near[0] * taps[b : b + 1] + near[1] * taps[3 + b : 4 + b] + near[2] * taps[6 + b : 7 + b]
            for b in range(3)
        )
        left = jnp.where(col == 0, 0.0, pltpu.roll(left, 1, 0))
        right = jnp.where(col == cols - 1, 0.0, pltpu.roll(right, chunk - 1, 0))
        out_ref[r : r + chunk] = (left + mid + right).astype(BF)


def pieces_kernel(place_ref, *refs):
    peers = 8
    pieces, (w_ref, taps_ref, _, out_ref, act_ref, hid_ref) = refs[:peers], refs[peers:]
    rows = pieces[0].shape[0]

    @pl.when(pl.program_id(0) == 0)
    def _():
        for p, piece in enumerate(pieces):
            source = 2 * ((place_ref[0] + 4 - p // 2) % 4) + (place_ref[1] + p % 2) % 2
            hid_ref[pl.ds(pl.multiple_of(source * rows, rows), rows)] = piece[...]

    depthwise(hid_ref[...], w_ref, taps_ref, out_ref, act_ref)


def both_kernel(place_ref, *refs):
    peers, frames = 8, 2
    pieces = refs[:peers]
    w_ref, taps_ref, _, one_ref, two_ref, act_ref, hid_ref = refs[peers:]
    rows = pieces[0].shape[1]

    @pl.when(pl.program_id(0) == 0)
    def _():
        for p, piece in enumerate(pieces):
            source = 2 * ((place_ref[0] + 4 - p // 2) % 4) + (place_ref[1] + p % 2) % 2
            target = pl.ds(pl.multiple_of(source * rows, rows), rows)
            for f in range(frames):
                hid_ref[f, target] = piece[f]

    for f, out_ref in enumerate((one_ref, two_ref)):
        depthwise(hid_ref[f], w_ref, taps_ref, out_ref, act_ref.at[f])


def point_kernel(
    place_ref, now_ref, one_ref, two_ref, taps_ref, w_ref, needed_ref, mine_ref, other_ref
):
    half = w_ref.shape[1]
    taps = taps_ref[...]
    mix = now_ref[...].astype(F32) * taps[0:1]
    mix = mix + one_ref[...].astype(F32) * taps[1:2]
    mix = mix + two_ref[...].astype(F32) * taps[2:3]
    gate = mix[:, half:]
    gated = (mix[:, :half] * (gate * jax.nn.sigmoid(gate))).astype(BF)
    over_channels = (((1,), (1,)), ((), ()))
    out = lax.dot_general(gated, w_ref[...], over_channels, preferred_element_type=F32).astype(BF)
    y, core = place_ref[0], place_ref[1]
    i = pl.program_id(0)
    rows = out.shape[0] // 4
    for k in range(4):
        target = 4 * i + k
        slot = (target // 2 - y + 4) % 4

        @pl.when(core == k % 2)
        def _():
            mine_ref[slot] = out[rows * k : rows * (k + 1)]

        @pl.when(core != k % 2)
        def _():
            other_ref[slot] = out[rows * k : rows * (k + 1)]


def sum_kernel(mine_ref, other_ref, hidden_ref, kept_ref, *sends):
    total = lambda k: mine_ref[k].astype(F32) + other_ref[k].astype(F32)
    kept_ref[...] = hidden_ref[...].astype(F32) + total(0)
    for k, send in enumerate(sends):
        send[...] = total(k + 1).astype(BF)


def stack_kernel(*refs):
    one_ref, two_ref, out_ref = refs[-3:]
    out_ref[0] = one_ref[...]
    out_ref[1] = two_ref[...]


def final_kernel(early_ref, late_ref, *refs):
    pieces, out_ref = refs[:6], refs[6]
    for f, kept in enumerate((early_ref, late_ref)):
        total = kept[...]
        for piece in pieces[3 * f : 3 * f + 3]:
            total = total + piece[...].astype(F32)
        out = total.astype(BF)
        for r in range(out_ref.shape[0]):
            out_ref[r, f] = out[16 * r : 16 * r + 16]


def params(mib):
    return pltpu.CompilerParams(vmem_limit_bytes=mib * MIB)


VMEM = pl.BlockSpec(memory_space=pltpu.VMEM)


def on_device(
    stream_in, queries, key_rows, value_rows, w_output, w_inner, w_down, spatial_taps, temporal_taps
):
    row_count, frames, col_count, width = queries.shape
    tokens = row_count * frames * col_count
    flat = lambda a: a.reshape(tokens, width)
    chan = w_inner.shape[2]
    peers = lax.axis_size(TILE)
    place = lax.axis_index(TILE)
    where_am_i = jnp.stack([place // 2, place % 2]).astype(jnp.int32)

    w_out_whole = lax.all_gather(w_output, TILE, axis=0, tiled=True)
    w_flat = w_inner.reshape(width, 2 * chan)
    taps_s = spatial_taps.reshape(9, 2 * chan)
    taps_t = temporal_taps.reshape(TAPS, 2 * chan)

    half = jax.ShapeDtypeStruct((HALF, 8, LANES), BF)
    scalars = pl.BlockSpec(memory_space=pltpu.SMEM)
    other_core = [(i, i ^ 1) for i in range(peers)]
    mine, other = pl.pallas_call(
        kv_kernel,
        out_shape=[half] * 2,
        in_specs=[scalars, VMEM, VMEM],
        out_specs=[VMEM] * 2,
        scratch_shapes=[pltpu.VMEM((tokens, LANES), BF), pltpu.VMEM((PIECES, 8, LANES), BF)],
        compiler_params=params(40),
    )(where_am_i, flat(key_rows), flat(value_rows))
    parts = pl.pallas_call(
        add_kernel, out_shape=half, in_specs=[VMEM] * 2, out_specs=VMEM, compiler_params=params(20)
    )(mine, lax.ppermute(other, TILE, other_core))
    same_core = ("blk", "y")
    parts = lax.all_to_all(parts, same_core, 0, 0, tiled=True)
    sums = pl.pallas_call(
        prefix_kernel, out_shape=half, in_specs=[VMEM], out_specs=VMEM, compiler_params=params(40)
    )(parts)
    state = lax.all_to_all(sums, same_core, 0, 0, tiled=True)

    anywhere = pl.BlockSpec(memory_space=pl.ANY)
    frame_rows = row_count * col_count
    attended = pl.pallas_call(
        attend_kernel,
        out_shape=jax.ShapeDtypeStruct((tokens, width), BF),
        in_specs=[scalars, VMEM, VMEM, VMEM],
        out_specs=VMEM,
        scratch_shapes=[pltpu.VMEM((PIECES, 8, LANES), BF)],
        compiler_params=params(40),
    )(where_am_i, flat(queries), state, lax.ppermute(state, TILE, other_core))
    one_frame = jax.ShapeDtypeStruct((frame_rows, width), BF)
    early, late = pl.pallas_call(
        hidden_kernel,
        out_shape=[one_frame] * 2,
        in_specs=[VMEM, VMEM, anywhere, anywhere],
        out_specs=[VMEM, VMEM],
        scratch_shapes=[pltpu.VMEM((width, width), BF), pltpu.SemaphoreType.DMA((5,))],
        compiler_params=params(52),
    )(attended, flat(stream_in), w_out_whole, w_flat)

    whole_rows = peers * frame_rows
    block = 512

    spatial_out = jax.ShapeDtypeStruct((whole_rows, 2 * chan), BF)
    weight_specs = [
        pl.BlockSpec((width, block), lambda i: (0, i)),
        pl.BlockSpec((9, block), lambda i: (0, i)),
    ]

    def pieces_call(kernel, frames, pieces, needed):
        outs = 1 if frames is None else frames
        lead = () if frames is None else (frames,)
        return pl.pallas_call(
            kernel,
            out_shape=[spatial_out] * outs,
            grid=(2 * chan // block,),
            in_specs=[pl.BlockSpec(memory_space=pltpu.SMEM)]
            + [pl.BlockSpec(part.shape, lambda i, n=part.ndim: (0,) * n) for part in pieces]
            + weight_specs
            + [anywhere],
            out_specs=[pl.BlockSpec((whole_rows, block), lambda i: (0, i))] * outs,
            scratch_shapes=[
                pltpu.VMEM(lead + (whole_rows + 2 * col_count, block), F32),
                pltpu.VMEM(lead + (whole_rows, width), BF),
            ],
            compiler_params=params(30 if frames is None else 40),
        )(where_am_i, *pieces, w_flat, taps_s, needed)

    row_block = 256
    point_call = pl.pallas_call(
        point_kernel,
        out_shape=[jax.ShapeDtypeStruct((4, frame_rows, width), BF)] * 2,
        grid=(whole_rows // row_block,),
        in_specs=[pl.BlockSpec(memory_space=pltpu.SMEM)]
        + [pl.BlockSpec((row_block, 2 * chan), lambda i: (i, 0))] * 3
        + [
            pl.BlockSpec((TAPS, 2 * chan), lambda i: (0, 0)),
            pl.BlockSpec((width, chan), lambda i: (0, 0)),
            anywhere,
        ],
        out_specs=[pl.BlockSpec((4, frame_rows, width), lambda i: (0, 0, 0))] * 2,
        compiler_params=params(40),
    )

    w_point = w_down.T
    blocks = lax.axis_size("blk")
    next_frames = [(i, i + 1) for i in range(blocks - 1)]
    other_core = [(i, i ^ 1) for i in range(peers)]
    ahead = [[(i, (i + 2 * k) % peers) for i in range(peers)] for k in range(4)]

    def along_of(rows):
        return [rows] + [lax.ppermute(rows, TILE, ahead[k]) for k in (1, 2, 3)]

    late_along = along_of(late)
    before_early = lax.ppermute(early, "blk", next_frames)
    others = pl.pallas_call(
        stack_kernel,
        out_shape=jax.ShapeDtypeStruct((2, frame_rows, width), BF),
        in_specs=[anywhere] * 3 + [VMEM] * 2,
        out_specs=VMEM,
        compiler_params=params(20),
    )(*late_along[1:], early, before_early)
    others_along = along_of(others)
    pieces = []
    for part in late_along:
        pieces += [part, lax.ppermute(part, TILE, other_core)]
    (late_sp,) = pieces_call(pieces_kernel, None, pieces, taps_t)
    before_late_sp = lax.ppermute(late_sp, "blk", next_frames)
    both = []
    for part in others_along:
        both += [part, lax.ppermute(part, TILE, other_core)]
    early_sp, before_early_sp = pieces_call(both_kernel, 2, both, late_sp)

    def core_shares(now, one, two, needed):
        mine, other = point_call(where_am_i, now, one, two, taps_t, w_point, needed)
        return mine, lax.ppermute(other, TILE, other_core)

    def sums(mine, from_core, rows):
        kept, *sends = pl.pallas_call(
            sum_kernel,
            out_shape=[jax.ShapeDtypeStruct((frame_rows, width), F32)] + [one_frame] * 3,
            in_specs=[VMEM] * 3,
            out_specs=[VMEM] * 4,
            compiler_params=params(20),
        )(mine, from_core, rows)
        return kept, [lax.ppermute(part, TILE, ahead[k + 1]) for k, part in enumerate(sends)]

    late_shares = core_shares(late_sp, early_sp, before_late_sp, before_early_sp)
    late_kept, late_back = sums(*late_shares, late)
    early_shares = core_shares(early_sp, before_late_sp, before_early_sp, late_shares[0])
    early_kept, early_back = sums(*early_shares, early)
    return pl.pallas_call(
        final_kernel,
        out_shape=jax.ShapeDtypeStruct(stream_in.shape, BF),
        in_specs=[VMEM] * 8,
        out_specs=VMEM,
        compiler_params=params(20),
    )(early_kept, late_kept, *early_back, *late_back)


def solution(mesh):
    in_specs = (
        P(TILE, "blk", None, None),
        P(TILE, "blk", None, None),
        P(TILE, "blk", None, None),
        P(TILE, "blk", None, None),
        P(TILE, None),
        P(None, None, TILE),
        P(TILE, None),
        P(None, None, None, TILE),
        P(None, None, TILE),
    )
    out_specs = P(TILE, "blk", None, None)
    sizes = mesh.devices.shape
    mesh = jax.sharding.Mesh(mesh.devices.reshape(sizes[0], sizes[1] // 2, 2), ("blk", "y", "core"))
    return jax.shard_map(
        on_device, mesh=mesh, in_specs=in_specs, out_specs=out_specs, check_vma=False
    )
```

```python
import functools

import jax
import jax.numpy as jnp
from jax import lax
from jax.experimental import pallas as pl
from jax.experimental.pallas import tpu as pltpu
from jax.sharding import PartitionSpec as P

HEADS = 20
HEAD_DIM = 112
D = 2240
TAPS = 3
EPS = 1e-6
LANES = 128
SLABS = 18
SUB = 14
PIECES = 256
HALF = 128
TILE = ("y", "core")
BF = jnp.bfloat16
F32 = jnp.float32
MIB = 1 << 20


def slab_of(c):
    first = (LANES * c) // HEAD_DIM
    bound = HEAD_DIM * (first + 1) - LANES * c
    start = (HEAD_DIM * first) // LANES * LANES
    pair = 2 if first + 1 < HEADS else 1
    stop = min(-(-(HEAD_DIM * (first + pair)) // LANES) * LANES, D)
    return first, pair, bound, start, stop, HEAD_DIM * first - start


def kv_kernel(place_ref, k_ref, v_ref, mine_ref, other_ref, last_ref, out_ref):
    tokens = k_ref.shape[0]
    key_pos = jnp.maximum(k_ref[...], 0)
    last_ref[...] = jnp.ones((tokens, LANES), BF)
    last_ref[:, : D - LANES * (SLABS - 1)] = v_ref[:, LANES * (SLABS - 1) :]
    lane = lax.broadcasted_iota(jnp.int32, (HEAD_DIM, LANES), 1)
    over_tokens = (((0,), (0,)), ((), ()))
    for c in range(SLABS):
        first, pair, bound, start, stop, offset = slab_of(c)
        values = last_ref[...] if c == SLABS - 1 else v_ref[:, LANES * c : LANES * (c + 1)]
        product = lax.dot_general(
            key_pos[:, start:stop], values, over_tokens, preferred_element_type=F32
        )
        tile = product[offset : offset + HEAD_DIM]
        if pair == 2:
            tile = jnp.where(lane < bound, tile, product[offset + HEAD_DIM : offset + 2 * HEAD_DIM])
        if c == SLABS - 1:
            sums = lax.dot_general(
                key_pos, jnp.ones((tokens, LANES), BF), over_tokens, preferred_element_type=F32
            )
            tile = jnp.where(lane < bound, tile, 0.0)
            for h in range(HEADS):
                tile = jnp.where(
                    lane == bound + h, sums[HEAD_DIM * h : HEAD_DIM * (h + 1)], tile
                )
        out_ref[SUB * c : SUB * (c + 1)] = tile.reshape(SUB, 8, LANES).astype(BF)
    rest = PIECES - SUB * SLABS
    out_ref[SUB * SLABS :] = jnp.zeros((rest, 8, LANES), BF)
    core = place_ref[1]
    mine_ref[...] = out_ref[pl.ds(HALF * core, HALF)]
    other_ref[...] = out_ref[pl.ds(HALF * (1 - core), HALF)]


def add_kernel(one_ref, two_ref, out_ref):
    out_ref[...] = (one_ref[...].astype(F32) + two_ref[...].astype(F32)).astype(BF)


def prefix_kernel(in_ref, out_ref):
    per_block = 8

    def block(b, total):
        here = in_ref[pl.ds(b * per_block, per_block)].astype(F32)
        total = total + jnp.sum(here, axis=0)
        out_ref[pl.ds(b * per_block, per_block)] = jnp.broadcast_to(
            total.astype(BF)[None], (per_block, 8, LANES)
        )
        return total

    lax.fori_loop(0, HALF // per_block, block, jnp.zeros((8, LANES), F32))


def attend_kernel(place_ref, q_ref, mine_ref, other_ref, att_ref, state_ref):
    core = place_ref[1]
    state_ref[pl.ds(HALF * core, HALF)] = mine_ref[...]
    state_ref[pl.ds(HALF * (1 - core), HALF)] = other_ref[...]
    query_pos = jnp.maximum(q_ref[...], 0)
    lane = lax.broadcasted_iota(jnp.int32, (HEAD_DIM, LANES), 1)
    tile_of = lambda c: state_ref[SUB * c : SUB * (c + 1)].astype(F32).reshape(HEAD_DIM, LANES)
    sums = tile_of(SLABS - 1)
    z_lane = D - LANES * (SLABS - 1)
    for c in range(SLABS):
        first, pair, bound, start, stop, offset = slab_of(c)
        tile = tile_of(c)
        weights = []
        for which in range(2):
            rows = []
            if offset > 0:
                rows.append(jnp.zeros((offset, LANES), F32))
            for k in range(pair):
                if which == 0:
                    part = tile
                else:
                    h = z_lane + first + k
                    part = jnp.broadcast_to(sums[:, h : h + 1], (HEAD_DIM, LANES))
                inside = (lane < bound) if k == 0 else (lane >= bound)
                rows.append(jnp.where(inside, part, 0.0))
            left = stop - start - offset - pair * HEAD_DIM
            if left > 0:
                rows.append(jnp.zeros((left, LANES), F32))
            weights.append(jnp.concatenate(rows, axis=0))
        weight = jnp.concatenate(weights, axis=1).astype(BF)
        both = jnp.dot(query_pos[:, start:stop], weight, preferred_element_type=F32)
        attended = (both[:, :LANES] / (both[:, LANES:] + EPS)).astype(BF)
        width = min(LANES, D - LANES * c)
        att_ref[:, LANES * c : LANES * c + width] = attended[:, :width]


def hidden_kernel(att_ref, stream_ref, w_hbm, needed_ref, early_ref, late_ref, w_ref, sems):
    tokens = att_ref.shape[0]
    step = 512
    spans = [(n, min(n + step, D)) for n in range(0, D, step)]
    copies = []
    for i, (n, stop) in enumerate(spans):
        span = pl.ds(n, stop - n)
        copies.append(pltpu.make_async_copy(w_hbm.at[span], w_ref.at[span], sems.at[i]))
    for copy in copies:
        copy.start()
    total = stream_ref[...].astype(F32)
    for copy, (n, stop) in zip(copies, spans):
        copy.wait()
        total = total + jnp.dot(att_ref[:, n:stop], w_ref[n:stop], preferred_element_type=F32)
    out = total.astype(BF)
    for r in range(tokens // 32):
        rows = slice(16 * r, 16 * r + 16)
        early_ref[rows] = out[32 * r : 32 * r + 16]
        late_ref[rows] = out[32 * r + 16 : 32 * r + 32]


def depthwise(hid, w_ref, taps_ref, out_ref, act_ref):
    tokens, cols = hid.shape[0], 16
    width = w_ref.shape[1]
    product = jnp.dot(hid, w_ref[...], preferred_element_type=F32)
    act = (product * jax.nn.sigmoid(product)).astype(BF).astype(F32)
    act_ref[:cols] = jnp.zeros((cols, width), F32)
    act_ref[cols + tokens :] = jnp.zeros((cols, width), F32)
    act_ref[cols : cols + tokens] = act
    taps = taps_ref[...]
    chunk = 16
    col = lax.broadcasted_iota(jnp.int32, (chunk, width), 0) % cols
    for r in range(0, tokens, chunk):
        near = [act_ref[r + cols * a : r + cols * a + chunk] for a in range(3)]
        left, mid, right = (
            near[0] * taps[b : b + 1] + near[1] * taps[3 + b : 4 + b] + near[2] * taps[6 + b : 7 + b]
            for b in range(3)
        )
        left = jnp.where(col == 0, 0.0, pltpu.roll(left, 1, 0))
        right = jnp.where(col == cols - 1, 0.0, pltpu.roll(right, chunk - 1, 0))
        out_ref[r : r + chunk] = (left + mid + right).astype(BF)


def pieces_kernel(place_ref, *refs):
    peers = 8
    pieces, (w_ref, taps_ref, _, out_ref, act_ref, hid_ref) = refs[:peers], refs[peers:]
    rows = pieces[0].shape[0]

    @pl.when(pl.program_id(0) == 0)
    def _():
        for p, piece in enumerate(pieces):
            source = 2 * ((place_ref[0] + 4 - p // 2) % 4) + (place_ref[1] + p % 2) % 2
            hid_ref[pl.ds(pl.multiple_of(source * rows, rows), rows)] = piece[...]

    depthwise(hid_ref[...], w_ref, taps_ref, out_ref, act_ref)


def both_kernel(place_ref, *refs):
    peers, frames = 8, 2
    pieces = refs[:peers]
    w_ref, taps_ref, _, one_ref, two_ref, act_ref, hid_ref = refs[peers:]
    rows = pieces[0].shape[1]

    @pl.when(pl.program_id(0) == 0)
    def _():
        for p, piece in enumerate(pieces):
            source = 2 * ((place_ref[0] + 4 - p // 2) % 4) + (place_ref[1] + p % 2) % 2
            target = pl.ds(pl.multiple_of(source * rows, rows), rows)
            for f in range(frames):
                hid_ref[f, target] = piece[f]

    for f, out_ref in enumerate((one_ref, two_ref)):
        depthwise(hid_ref[f], w_ref, taps_ref, out_ref, act_ref.at[f])


def point_kernel(
    place_ref, now_ref, one_ref, two_ref, taps_ref, w_ref, needed_ref, mine_ref, other_ref
):
    half = w_ref.shape[1]
    taps = taps_ref[...]
    mix = now_ref[...].astype(F32) * taps[0:1]
    mix = mix + one_ref[...].astype(F32) * taps[1:2]
    mix = mix + two_ref[...].astype(F32) * taps[2:3]
    gate = mix[:, half:]
    gated = (mix[:, :half] * (gate * jax.nn.sigmoid(gate))).astype(BF)
    over_channels = (((1,), (1,)), ((), ()))
    out = lax.dot_general(gated, w_ref[...], over_channels, preferred_element_type=F32).astype(BF)
    y, core = place_ref[0], place_ref[1]
    i = pl.program_id(0)
    rows = mine_ref.shape[1]
    count = out.shape[0] // rows
    for k in range(count):
        target = count * i + k
        slot = (target // 2 - y + 4) % 4

        @pl.when(core == k % 2)
        def _():
            mine_ref[slot] = out[rows * k : rows * (k + 1)]

        @pl.when(core != k % 2)
        def _():
            other_ref[slot] = out[rows * k : rows * (k + 1)]


def sum_kernel(mine_ref, other_ref, hidden_ref, kept_ref, *sends):
    total = lambda k: mine_ref[k].astype(F32) + other_ref[k].astype(F32)
    kept_ref[...] = hidden_ref[...].astype(F32) + total(0)
    for k, send in enumerate(sends):
        send[...] = total(k + 1).astype(BF)


def stack_kernel(*refs):
    one_ref, two_ref, out_ref = refs[-3:]
    out_ref[0] = one_ref[...]
    out_ref[1] = two_ref[...]


def final_kernel(early_ref, late_ref, *refs):
    pieces, out_ref = refs[:6], refs[6]
    for f, kept in enumerate((early_ref, late_ref)):
        total = kept[...]
        for piece in pieces[3 * f : 3 * f + 3]:
            total = total + piece[...].astype(F32)
        out = total.astype(BF)
        for r in range(out_ref.shape[0]):
            out_ref[r, f] = out[16 * r : 16 * r + 16]


def params(mib):
    return pltpu.CompilerParams(vmem_limit_bytes=mib * MIB)


VMEM = pl.BlockSpec(memory_space=pltpu.VMEM)


def on_device(
    stream_in, queries, key_rows, value_rows, w_output, w_inner, w_down, spatial_taps, temporal_taps
):
    row_count, frames, col_count, width = queries.shape
    tokens = row_count * frames * col_count
    flat = lambda a: a.reshape(tokens, width)
    chan = w_inner.shape[2]
    peers = lax.axis_size(TILE)
    place = lax.axis_index(TILE)
    where_am_i = jnp.stack([place // 2, place % 2]).astype(jnp.int32)

    w_out_whole = lax.all_gather(w_output, TILE, axis=0, tiled=True)
    w_flat = w_inner.reshape(width, 2 * chan)
    taps_s = spatial_taps.reshape(9, 2 * chan)
    taps_t = temporal_taps.reshape(TAPS, 2 * chan)

    half = jax.ShapeDtypeStruct((HALF, 8, LANES), BF)
    scalars = pl.BlockSpec(memory_space=pltpu.SMEM)
    other_core = [(i, i ^ 1) for i in range(peers)]
    mine, other = pl.pallas_call(
        kv_kernel,
        out_shape=[half] * 2,
        in_specs=[scalars, VMEM, VMEM],
        out_specs=[VMEM] * 2,
        scratch_shapes=[pltpu.VMEM((tokens, LANES), BF), pltpu.VMEM((PIECES, 8, LANES), BF)],
        compiler_params=params(40),
    )(where_am_i, flat(key_rows), flat(value_rows))
    parts = pl.pallas_call(
        add_kernel, out_shape=half, in_specs=[VMEM] * 2, out_specs=VMEM, compiler_params=params(20)
    )(mine, lax.ppermute(other, TILE, other_core))
    same_core = ("blk", "y")
    parts = lax.all_to_all(parts, same_core, 0, 0, tiled=True)
    sums = pl.pallas_call(
        prefix_kernel, out_shape=half, in_specs=[VMEM], out_specs=VMEM, compiler_params=params(40)
    )(parts)
    state = lax.all_to_all(sums, same_core, 0, 0, tiled=True)

    anywhere = pl.BlockSpec(memory_space=pl.ANY)
    frame_rows = row_count * col_count
    attended = pl.pallas_call(
        attend_kernel,
        out_shape=jax.ShapeDtypeStruct((tokens, width), BF),
        in_specs=[scalars, VMEM, VMEM, VMEM],
        out_specs=VMEM,
        scratch_shapes=[pltpu.VMEM((PIECES, 8, LANES), BF)],
        compiler_params=params(40),
    )(where_am_i, flat(queries), state, lax.ppermute(state, TILE, other_core))
    one_frame = jax.ShapeDtypeStruct((frame_rows, width), BF)
    early, late = pl.pallas_call(
        hidden_kernel,
        out_shape=[one_frame] * 2,
        in_specs=[VMEM, VMEM, anywhere, anywhere],
        out_specs=[VMEM, VMEM],
        scratch_shapes=[pltpu.VMEM((width, width), BF), pltpu.SemaphoreType.DMA((5,))],
        compiler_params=params(52),
    )(attended, flat(stream_in), w_out_whole, w_flat)

    whole_rows = peers * frame_rows
    block = 512

    spatial_out = jax.ShapeDtypeStruct((whole_rows, 2 * chan), BF)
    weight_specs = [
        pl.BlockSpec((width, block), lambda i: (0, i)),
        pl.BlockSpec((9, block), lambda i: (0, i)),
    ]

    def pieces_call(kernel, frames, pieces, needed):
        outs = 1 if frames is None else frames
        lead = () if frames is None else (frames,)
        return pl.pallas_call(
            kernel,
            out_shape=[spatial_out] * outs,
            grid=(2 * chan // block,),
            in_specs=[pl.BlockSpec(memory_space=pltpu.SMEM)]
            + [pl.BlockSpec(part.shape, lambda i, n=part.ndim: (0,) * n) for part in pieces]
            + weight_specs
            + [anywhere],
            out_specs=[pl.BlockSpec((whole_rows, block), lambda i: (0, i))] * outs,
            scratch_shapes=[
                pltpu.VMEM(lead + (whole_rows + 2 * col_count, block), F32),
                pltpu.VMEM(lead + (whole_rows, width), BF),
            ],
            compiler_params=params(30 if frames is None else 40),
        )(where_am_i, *pieces, w_flat, taps_s, needed)

    row_block = 512
    point_call = pl.pallas_call(
        point_kernel,
        out_shape=[jax.ShapeDtypeStruct((4, frame_rows, width), BF)] * 2,
        grid=(whole_rows // row_block,),
        in_specs=[pl.BlockSpec(memory_space=pltpu.SMEM)]
        + [pl.BlockSpec((row_block, 2 * chan), lambda i: (i, 0))] * 3
        + [
            pl.BlockSpec((TAPS, 2 * chan), lambda i: (0, 0)),
            pl.BlockSpec((width, chan), lambda i: (0, 0)),
            anywhere,
        ],
        out_specs=[pl.BlockSpec((4, frame_rows, width), lambda i: (0, 0, 0))] * 2,
        compiler_params=params(40),
    )

    w_point = w_down.T
    blocks = lax.axis_size("blk")
    next_frames = [(i, i + 1) for i in range(blocks - 1)]
    other_core = [(i, i ^ 1) for i in range(peers)]
    ahead = [[(i, (i + 2 * k) % peers) for i in range(peers)] for k in range(4)]

    def along_of(rows):
        return [rows] + [lax.ppermute(rows, TILE, ahead[k]) for k in (1, 2, 3)]

    late_along = along_of(late)
    before_early = lax.ppermute(early, "blk", next_frames)
    others = pl.pallas_call(
        stack_kernel,
        out_shape=jax.ShapeDtypeStruct((2, frame_rows, width), BF),
        in_specs=[anywhere] * 3 + [VMEM] * 2,
        out_specs=VMEM,
        compiler_params=params(20),
    )(*late_along[1:], early, before_early)
    others_along = along_of(others)
    pieces = []
    for part in late_along:
        pieces += [part, lax.ppermute(part, TILE, other_core)]
    (late_sp,) = pieces_call(pieces_kernel, None, pieces, taps_t)
    before_late_sp = lax.ppermute(late_sp, "blk", next_frames)
    both = []
    for part in others_along:
        both += [part, lax.ppermute(part, TILE, other_core)]
    early_sp, before_early_sp = pieces_call(both_kernel, 2, both, late_sp)

    def core_shares(now, one, two, needed):
        mine, other = point_call(where_am_i, now, one, two, taps_t, w_point, needed)
        return mine, lax.ppermute(other, TILE, other_core)

    def sums(mine, from_core, rows):
        kept, *sends = pl.pallas_call(
            sum_kernel,
            out_shape=[jax.ShapeDtypeStruct((frame_rows, width), F32)] + [one_frame] * 3,
            in_specs=[VMEM] * 3,
            out_specs=[VMEM] * 4,
            compiler_params=params(20),
        )(mine, from_core, rows)
        return kept, [lax.ppermute(part, TILE, ahead[k + 1]) for k, part in enumerate(sends)]

    late_shares = core_shares(late_sp, early_sp, before_late_sp, before_early_sp)
    late_kept, late_back = sums(*late_shares, late)
    early_shares = core_shares(early_sp, before_late_sp, before_early_sp, late_shares[0])
    early_kept, early_back = sums(*early_shares, early)
    return pl.pallas_call(
        final_kernel,
        out_shape=jax.ShapeDtypeStruct(stream_in.shape, BF),
        in_specs=[VMEM] * 8,
        out_specs=VMEM,
        compiler_params=params(20),
    )(early_kept, late_kept, *early_back, *late_back)


def solution(mesh):
    in_specs = (
        P(TILE, "blk", None, None),
        P(TILE, "blk", None, None),
        P(TILE, "blk", None, None),
        P(TILE, "blk", None, None),
        P(TILE, None),
        P(None, None, TILE),
        P(TILE, None),
        P(None, None, None, TILE),
        P(None, None, TILE),
    )
    out_specs = P(TILE, "blk", None, None)
    sizes = mesh.devices.shape
    mesh = jax.sharding.Mesh(mesh.devices.reshape(sizes[0], sizes[1] // 2, 2), ("blk", "y", "core"))
    return jax.shard_map(
        on_device, mesh=mesh, in_specs=in_specs, out_specs=out_specs, check_vma=False
    )
```
